128 devices in a mesh: inline: 16 (over z, x), crosslin: 8 (over y, core).
Axes of the slice: x: 4, y: 4, z: 4, core: 2. Of those that a mesh axis runs over, the one named last changes fastest.
Arguments:
- amplitudes: bfloat16 [16, 4096, 8192], P(None, 'inline', 'crosslin'), may hold values from -6 to 6
- pick_mask: int32 [4096, 8192], P('inline', 'crosslin'), may hold values 0 or 1
- pick_depth: int32 [4096, 8192], P('inline', 'crosslin'), may hold values from 0 to 15
- iterate: float32 [4096, 8192], P('inline', 'crosslin'), may hold values from -60 to 60
Outputs:
- new_iterate: float32 [4096, 8192], P('inline', 'crosslin')
- new_residual: float32 [4096, 8192], P('inline', 'crosslin')
- new_direction: float32 [4096, 8192], P('inline', 'crosslin')
The draws below stay inside these ranges and needn't reach their ends.
All inputs are finite; a program needn't handle non-finite values. No bound on the sum of `pick_mask` on one device may be relied on, other than what follows from the above.
Results may differ from the reference program's by a relative error of at most 0.0022.
Values may be sent and summed in bfloat16 or wider, within the bound.
No kernel may reach another device: no remote copies, remote signals or barrier semaphores. Data moves between devices by JAX's collectives and lax.ppermute only.
A program may use at most 128 MiB of HBM per device.

```python
import jax
import jax.numpy as jnp
from jax import lax

K = 16
DEC = 8
NI = 4096
NJ = 8192
CI = 32


def draw_iterate(key, part):
    row_frac = jnp.arange(NI, dtype=jnp.float32) / NI
    col_frac = jnp.arange(NJ, dtype=jnp.float32) / NJ
    noise = jnp.clip(jax.random.normal(key, (NI, NJ), jnp.float32), -6.0, 6.0)
    scale = jnp.power(10.0, row_frac[:, None] + col_frac[None, :] - 1.0)
    return noise * scale


def plant(drawn, rng, smallest, top_value):
    index_at = [jax.random.randint(jax.random.fold_in(rng, axis), (), 0, length) for axis, length in enumerate(drawn.shape)]
    longest = drawn.shape.index(max(drawn.shape))
    next_to = index_at[:longest] + [(index_at[longest] + 1) % drawn.shape[longest]] + index_at[longest + 1:]
    return drawn.at[tuple(index_at)].set(smallest).at[tuple(next_to)].set(top_value)


def levels(own_key, dims, cuts, low, largest):
    factor_of = 1.0
    for axis_at, parts in cuts:
        heights = jax.random.uniform(jax.random.fold_in(jax.random.fold_in(own_key, 6), axis_at), (parts,), jnp.float32, low / len(cuts), largest / len(cuts))
        factor_of = factor_of * jnp.repeat(jnp.exp(heights), dims[axis_at] // parts).reshape((-1,) + (1,) * (len(dims) - 1 - axis_at))
    return factor_of


def centred(rng, shape, spread, bound, cuts=(), kind=jnp.bfloat16):
    loudness = levels(rng, shape, cuts, -0.22, 0.18) if cuts else 1.0
    entries = jax.random.normal(rng, shape, jnp.float32) * spread * loudness
    return jnp.minimum(jnp.maximum(entries, -bound), bound).astype(kind)


def setup_inputs(seed: int = 0) -> dict:
    splits = jax.random.split(jax.random.key(seed), 5)
    amplitudes = centred(splits[0], (K, NI, NJ), 1.0, 6.0, ((1, 16), (2, 8)))
    pick_mask = plant((jax.random.randint(splits[1], (NI, NJ), 0, 8) < 1).astype(jnp.int32), jax.random.fold_in(splits[1], 1), 0, 1)
    pick_depth = plant(jax.random.randint(splits[2], (NI, NJ), 0, K), jax.random.fold_in(splits[2], 1), 0, K - 1).astype(jnp.int32)
    iterate = draw_iterate(jax.random.fold_in(splits[4], 71), 0)
    return {"amplitudes": amplitudes, "pick_mask": pick_mask, "pick_depth": pick_depth, "iterate": iterate}


pick_weight = 1.0
tensor_eps = 1.0
coupling = 4.0
highest = lax.Precision.HIGHEST

def cosine_rows(row_ids, col_ids, length):
    phase_index = jnp.remainder(row_ids[:, None] * (2 * col_ids[None, :] + 1), 4 * length)
    phase_angle = phase_index.astype(jnp.float32) * (jnp.pi / (2.0 * length))
    normalizer = jnp.where(row_ids == 0, jnp.sqrt(1.0 / length), jnp.sqrt(2.0 / length)).astype(jnp.float32)
    return normalizer[:, None] * jnp.cos(phase_angle)

def coarse_eigen(row_ids, col_ids, total_rows, total_cols):
    angle_rows = row_ids.astype(jnp.float32) * (jnp.pi / total_rows)
    angle_cols = col_ids.astype(jnp.float32) * (jnp.pi / total_cols)
    return coupling * ((2.0 - 2.0 * jnp.cos(angle_rows))[:, None] + (2.0 - 2.0 * jnp.cos(angle_cols))[None, :]) + coupling / (CI * CI)

def tensor_fields(amplitudes):
    sample_count, row_count, col_count = amplitudes.shape
    tensor_ii = jnp.zeros((row_count, col_count), jnp.float32)
    tensor_ic = jnp.zeros((row_count, col_count), jnp.float32)
    tensor_cc = jnp.zeros((row_count, col_count), jnp.float32)
    for sample in range(sample_count):
        padded = jnp.pad(amplitudes[sample].astype(jnp.float32), 1)
        grad_inline = (padded[2:, 1:-1] - padded[:-2, 1:-1]) * 0.5
        grad_cross = (padded[1:-1, 2:] - padded[1:-1, :-2]) * 0.5
        tensor_ii = tensor_ii + grad_inline * grad_inline
        tensor_ic = tensor_ic + grad_inline * grad_cross
        tensor_cc = tensor_cc + grad_cross * grad_cross
    trace_sum = tensor_ii + tensor_cc + 2.0 * tensor_eps
    return ((tensor_cc + tensor_eps) / trace_sum, -tensor_ic / trace_sum, (tensor_ii + tensor_eps) / trace_sum)

def valid_masks(row_count, col_count):
    valid_down = (jnp.arange(row_count, dtype=jnp.int32) < row_count - 1).astype(jnp.float32)[:, None]
    valid_right = (jnp.arange(col_count, dtype=jnp.int32) < col_count - 1).astype(jnp.float32)[None, :]
    return (valid_down, valid_right)

def operate(field, tensors, weight):
    tensor_xx, tensor_xy, tensor_yy = tensors
    valid_down, valid_right = valid_masks(field.shape[0], field.shape[1])
    below = jnp.concatenate([field[1:], jnp.zeros_like(field[:1])], 0)
    beside = jnp.concatenate([field[:, 1:], jnp.zeros_like(field[:, :1])], 1)
    diff_down = (below - field) * valid_down
    diff_right = (beside - field) * valid_right
    flux_down = (tensor_xx * diff_down + tensor_xy * diff_right) * valid_down
    flux_right = (tensor_xy * diff_down + tensor_yy * diff_right) * valid_right
    flux_above = jnp.concatenate([jnp.zeros_like(flux_down[:1]), flux_down[:-1]], 0)
    flux_left = jnp.concatenate([jnp.zeros_like(flux_right[:, :1]), flux_right[:, :-1]], 1)
    return flux_above - flux_down + flux_left - flux_right + weight * field

def main_diagonal(tensors, weight):
    tensor_xx, tensor_xy, tensor_yy = tensors
    valid_down, valid_right = valid_masks(weight.shape[0], weight.shape[1])
    own_terms = valid_down * tensor_xx + 2.0 * valid_down * valid_right * tensor_xy + valid_right * tensor_yy
    upper = valid_down * tensor_xx
    lefter = valid_right * tensor_yy
    upper = jnp.concatenate([jnp.zeros_like(upper[:1]), upper[:-1]], 0)
    lefter = jnp.concatenate([jnp.zeros_like(lefter[:, :1]), lefter[:, :-1]], 1)
    return own_terms + upper + lefter + weight

def precondition(residual, diag_values):
    row_count, col_count = residual.shape
    coarse_rows = row_count // DEC
    coarse_cols = col_count // DEC
    blocks = residual.reshape(coarse_rows, DEC, coarse_cols, DEC).sum(axis=(1, 3))
    row_ids = jnp.arange(coarse_rows, dtype=jnp.int32)
    col_ids = jnp.arange(coarse_cols, dtype=jnp.int32)
    table_rows = cosine_rows(row_ids, row_ids, coarse_rows)
    table_cols = cosine_rows(col_ids, col_ids, coarse_cols)
    spectrum = jnp.dot(jnp.dot(table_rows, blocks, precision=highest), table_cols.T, precision=highest)
    spectrum = spectrum / coarse_eigen(row_ids, col_ids, coarse_rows, coarse_cols)
    coarse_back = jnp.dot(table_rows.T, jnp.dot(spectrum, table_cols, precision=highest), precision=highest)
    spread_back = jnp.broadcast_to(coarse_back[:, None, :, None], (coarse_rows, DEC, coarse_cols, DEC)).reshape(row_count, col_count)
    return residual / diag_values + spread_back

def reference(amplitudes, pick_mask, pick_depth, iterate):
    tensors = tensor_fields(amplitudes)
    weight = pick_weight * pick_mask.astype(jnp.float32)
    source = weight * (pick_depth.astype(jnp.float32) - 0.5 * (K - 1))
    diag_values = main_diagonal(tensors, weight)
    residual = source - operate(iterate, tensors, weight)
    precond = precondition(residual, diag_values)
    image_field = operate(precond, tensors, weight)
    inner_old = jnp.sum(residual * precond)
    curvature = jnp.sum(precond * image_field)
    step_length = inner_old / curvature
    new_iterate = iterate + step_length * precond
    new_residual = residual - step_length * image_field
    new_precond = precondition(new_residual, diag_values)
    step_ratio = jnp.sum(new_residual * new_precond) / inner_old
    new_direction = new_precond + step_ratio * precond
    return (new_iterate, new_residual, new_direction)
```

```python
import functools

import jax
import jax.numpy as jnp
import ml_dtypes
import numpy as np
from jax import lax
from jax.experimental import pallas as pl
from jax.experimental.pallas import tpu as pltpu
from jax.sharding import PartitionSpec as P

K = 16
DEC = 8
CI = 32
COUPLING = 4.0
F32 = jnp.float32
BF16 = jnp.bfloat16
NPB = ml_dtypes.bfloat16
VMEM = pltpu.VMEM

RD = 256
CD = 1024
ER = RD + 32
EC = CD + 256
CR = RD // DEC
CC = CD // DEC
MSG = 64
LIMIT = 56 * 1024 * 1024


def dot(a, b):
    return jnp.dot(a, b, preferred_element_type=F32)


def parts2(x):
    hi = x.astype(BF16)
    return hi, (x - hi.astype(F32)).astype(BF16)


def parts3(x):
    hi = x.astype(BF16)
    rest = x - hi.astype(F32)
    mid = rest.astype(BF16)
    return hi, mid, (rest - mid.astype(F32)).astype(BF16)


def np2(x):
    hi = x.astype(np.float32).astype(NPB)
    return hi, (x - hi.astype(np.float64)).astype(np.float32).astype(NPB)


def line_tables():
    sel = np.zeros((2, 21, 128, 128), np.float32)
    for s in range(K):
        for k in range(3):
            sel[0, s, k, 3 * s + k] = 1
            sel[1, s, 125 + k, 3 * s + k] = 1
    for part in range(3):
        for l in range(2):
            sel[0, 16 + part, l, 48 + 3 * l + part] = 1
            sel[1, 16 + part, 126 + l, 48 + 3 * l + part] = 1
    for o in range(2):
        sel[0, 19 + o, 0, 54 + o] = 1
        sel[1, 19 + o, 127, 54 + o] = 1
    place = np.zeros((2, 128, 19 * 128), np.float32)
    for side in range(2):
        for s in range(K):
            place[side, :, s * 128 : s * 128 + 128] = sel[side, s].T
        place[side, :, 2048:2176] = sel[side, 16:19].sum(0).T
        place[side, :, 2176:2304] = sel[side, 19].T
        place[side, :, 2304:2432] = sel[side, 20].T
    rows = np.zeros((2, MSG, 256), np.float32)
    put = np.zeros((2, 304, MSG), np.float32)
    for s in range(K):
        for k in range(3):
            rows[0, 3 * s + k, 16 * s + k] = 1
            rows[1, 3 * s + k, 16 * s + 13 + k] = 1
    for side in range(2):
        put[side, :256] = rows[side].T
        for l in range(2):
            for part in range(3):
                put[side, 256 + (14 + l if side else l), 48 + 3 * l + part] = 1
        put[side, 272 + (15 if side else 0), 54] = 1
        put[side, 288 + (15 if side else 0), 55] = 1
    mix = np.zeros((2, 3, MSG, 128), np.float32)
    for k in range(3):
        for s in range(K):
            mix[:, k, 3 * s + k, 3 * s : 3 * s + 3] = 1
    for l in range(2):
        for part in range(3):
            for other in range(2):
                mix[0, l, 48 + 3 * l + part, 48 + 3 * other + part] = 1
                mix[1, l + 1, 48 + 3 * l + part, 48 + 3 * other + part] = 1
    for o in (54, 55):
        mix[0, 0, o, o] = 1
        mix[1, 2, o, o] = 1
    lanes = sel.sum(1).transpose(0, 2, 1)
    return tuple(t.astype(NPB) for t in (sel, place, rows, put, mix, lanes))


def coarse_tables(n_in, n_cr):
    n = CC * n_cr
    freq = np.arange(n, dtype=np.float64)
    norm = np.where(freq == 0, np.sqrt(1.0 / n), np.sqrt(2.0 / n))

    def cosines(cols):
        phase = (freq[:, None] * (2 * cols[None, :] + 1)) % (4 * n)
        return norm[:, None] * np.cos(np.pi * phase / (2 * n))

    forward = cosines(np.arange(n, dtype=np.float64)).T
    back = np.zeros((n_cr, n, 2 * CC))
    for j in range(n_cr):
        cols = np.zeros(2 * CC)
        cols[:CC] = j * CC + np.arange(CC)
        cols[CC] = j * CC - 1
        cols[CC + 1] = j * CC + CC
        back[j] = cosines(cols)
        back[j, :, CC + 2 :] = 0
    half = (2.0 - 2.0 * np.cos(np.pi * freq / n) + 1.0 / (CI * CI)) / 2.0
    kappa = np.log1p(half + np.sqrt(half * (half + 2.0)))
    scale = 1.0 / (COUPLING * 2.0 * np.sinh(kappa))
    steps = np.stack([np.exp(-kappa * d) for d in (1, 2, 4, 8, 16)] + [scale] + [scale * 0] * 2)
    at = np.arange(40)[:, None]
    grow = scale * np.exp(-kappa * at) * (at < 34)
    fall = scale * np.exp(-kappa * (33.0 - at)) * (at < 34)
    whole = CR * n_in
    blocks = np.stack(
        [
            np.exp(-kappa * CR),
            np.exp(-kappa * whole),
            1.0 / (1.0 - np.exp(-kappa * 2 * whole)),
            scale * np.exp(-kappa),
        ]
    ).reshape(4, n_cr, 128)
    spread = np.zeros((2 * CC, EC))
    for lane in range(EC):
        col = (lane - 128) // DEC
        if -1 <= col <= CC:
            spread[{-1: CC, CC: CC + 1}.get(col, col), lane] = 1
    group = np.zeros((CD, CC))
    group[np.arange(CD), np.arange(CD) // DEC] = 1
    f = np.float32
    return dict(
        forward=np2(forward), back=np2(back), steps=steps.astype(f), grow=grow.astype(f),
        fall=fall.astype(f), blocks=blocks.astype(f), spread=spread.astype(NPB), group=group.astype(NPB),
    )


def pack_columns_kernel(a0, a1, v0, v1, m0, m1, d0, d1, sel, out0, out1):
    for side, (a, v, m, d, out) in enumerate(((a0, v0, m0, d0, out0), (a1, v1, m1, d1, out1))):
        weight = m[...].astype(F32)
        source = weight * (d[...].astype(F32) - 0.5 * (K - 1))
        total = jnp.zeros((RD, 128), F32)
        for s in range(K):
            total += dot(a[s], sel[side, s])
        for i, part in enumerate(parts3(v[...]) + (weight.astype(BF16), source.astype(BF16))):
            total += dot(part, sel[side, 16 + i])
        out[...] = total.astype(BF16)


def pack_columns(amplitudes, iterate, mask, depth, sel):
    last = CD // 128 - 1
    cube = [pl.BlockSpec((K, RD, 128), lambda i, c=c: (0, 0, c)) for c in (0, last)]
    flat = [pl.BlockSpec((RD, 128), lambda i, c=c: (0, c)) for c in (0, last)]
    whole = pl.BlockSpec(sel.shape, lambda i: (0, 0, 0, 0))
    out = jax.ShapeDtypeStruct((RD, 128), BF16)
    return pl.pallas_call(
        pack_columns_kernel, grid=(1,), in_specs=cube + flat * 3 + [whole],
        out_specs=[pl.BlockSpec((RD, 128), lambda i: (0, 0))] * 2, out_shape=[out, out],
        compiler_params=pltpu.CompilerParams(vmem_limit_bytes=32 * 1024 * 1024),
        cost_estimate=pl.CostEstimate(flops=10**8, bytes_accessed=3 * 10**6, transcendentals=0),
        name="pack_columns",
    )(amplitudes, amplitudes, iterate, iterate, mask, mask, depth, depth, sel)


def pack_rows_kernel(a0, a1, v0, v1, m0, m1, d0, d1, left, right, rows, mix, lanes, out0, out1):
    at = lax.broadcasted_iota(jnp.int32, (MSG, CD), 0)
    for side, (a, v, m, d, out) in enumerate(((a0, v0, m0, d0, out0), (a1, v1, m1, d1, out1))):
        middle = dot(rows[side], a[...].reshape(K * 16, CD))
        split = [p.astype(F32) for p in parts3(v[...])]
        for l in range(2):
            row = 6 + l if side else l
            for part in range(3):
                middle = jnp.where(at == 48 + 3 * l + part, split[part][row : row + 1], middle)
        row = 7 if side else 0
        weight = m[row : row + 1].astype(F32)
        source = weight * (d[row : row + 1].astype(F32) - 0.5 * (K - 1))
        middle = jnp.where(at == 54, weight, jnp.where(at == 55, source, middle))
        out[:, 128 : 128 + CD] = middle.astype(BF16)
        for tile, halo, which in ((0, left, 1), (128 + CD, right, 0)):
            total = jnp.zeros((MSG, 128), F32)
            edge = halo[RD - 16 : RD].astype(F32)[13:16] if side else halo[0:16].astype(F32)[0:3]
            for k in range(3):
                term = mix[side, k].astype(F32) * edge[k : k + 1]
                total += dot(term.astype(BF16), lanes[which])
            out[:, tile : tile + 128] = total.astype(BF16)


def pack_rows(amplitudes, iterate, mask, depth, left, right, rows, mix, lanes):
    cube = [pl.BlockSpec((K, 16, CD), lambda i, c=c: (0, c, 0)) for c in (0, RD // 16 - 1)]
    flat = [pl.BlockSpec((8, CD), lambda i, c=c: (c, 0)) for c in (0, RD // 8 - 1)]
    full = [pl.BlockSpec(t.shape, lambda i, n=t.ndim: (0,) * n) for t in (left, right, rows, mix, lanes)]
    out = jax.ShapeDtypeStruct((MSG, EC), BF16)
    return pl.pallas_call(
        pack_rows_kernel, grid=(1,), in_specs=cube + flat * 3 + full,
        out_specs=[pl.BlockSpec((MSG, EC), lambda i: (0, 0))] * 2, out_shape=[out, out],
        compiler_params=pltpu.CompilerParams(vmem_limit_bytes=32 * 1024 * 1024),
        cost_estimate=pl.CostEstimate(flops=10**8, bytes_accessed=2 * 10**6, transcendentals=0),
        name="pack_rows",
    )(amplitudes, amplitudes, iterate, iterate, mask, mask, depth, depth, left, right, rows, mix, lanes)


def block_sums(rows, group):
    return sum(dot(part, group) for part in parts3(rows))


def tensor_kernel(
    n_in, n_cr, pos, amp, v_in, mask, depth, up, down, left, right, put, place, group,
    ta_o, tb_o, tc_o, z_o, r_o, rd_o, blocks_o, sums_o,
    ext, v_ext, w_ext, s_ext, fd, fr, rowsum, sems,
):
    inner = (slice(16, 16 + RD), slice(128, 128 + CD))
    copies = [
        pltpu.make_async_copy(amp, ext.at[:, 16 : 16 + RD, 128 : 128 + CD], sems.at[0]),
        pltpu.make_async_copy(v_in, v_ext.at[16 : 16 + RD, 128 : 128 + CD], sems.at[1]),
    ]
    for c in copies:
        c.start()
    weight = mask[...].astype(F32)
    w_ext[inner] = weight
    s_ext[inner] = weight * (depth[...].astype(F32) - 0.5 * (K - 1))
    for side, halo, lane in ((1, left, 0), (0, right, 128 + CD)):
        tile = dot(halo[...], place[side])
        for s in range(K):
            ext[s, 16 : 16 + RD, lane : lane + 128] = tile[:, s * 128 : s * 128 + 128].astype(BF16)
        v_ext[16 : 16 + RD, lane : lane + 128] = tile[:, 2048:2176]
        w_ext[16 : 16 + RD, lane : lane + 128] = tile[:, 2176:2304]
        s_ext[16 : 16 + RD, lane : lane + 128] = tile[:, 2304:2432]
    for side, halo, row in ((1, up, 0), (0, down, 16 + RD)):
        lines = dot(put[side], halo[...])
        for s in range(K):
            ext[s, row : row + 16, :] = lines[16 * s : 16 * s + 16].astype(BF16)
        v_ext[row : row + 16, :] = lines[256:272]
        w_ext[row : row + 16, :] = lines[272:288]
        s_ext[row : row + 16, :] = lines[288:304]
    for c in copies:
        c.wait()
    first_row = pos[0] * RD - 16
    col = pos[1] * CD - 128 + lax.broadcasted_iota(jnp.int32, (8, EC), 1)
    valid_right = ((col >= 0) & (col < n_cr * CD - 1)).astype(F32)
    row_iota = lax.broadcasted_iota(jnp.int32, (8, EC), 0)

    def left_of(x):
        return pltpu.roll(x, 1, 1)

    def right_of(x):
        return pltpu.roll(x, EC - 1, 1)

    def tensors(t, carry):
        for half in range(2):
            at = pl.multiple_of(16 * t + 8 + 8 * half, 8)
            sii = jnp.zeros((8, EC), F32)
            sic = jnp.zeros((8, EC), F32)
            scc = jnp.zeros((8, EC), F32)
            for s in range(K):
                x = ext[s, pl.ds(pl.multiple_of(16 * t, 16), 32), :].astype(F32)
                lo = 8 + 8 * half
                middle = x[lo : lo + 8]
                gi = x[lo + 1 : lo + 9] - x[lo - 1 : lo + 7]
                gc = right_of(middle) - left_of(middle)
                sii += gi * gi
                sic += gi * gc
                scc += gc * gc
            sii, sic, scc = 0.25 * sii, 0.25 * sic, 0.25 * scc
            inv = 1.0 / (sii + scc + 2.0)
            row = first_row + at + row_iota
            valid_down = ((row >= 0) & (row < n_in * RD - 1)).astype(F32)
            ta = valid_down * ((scc + 1.0) * inv)
            tb = (valid_down * valid_right) * (-sic * inv)
            tc = valid_right * ((sii + 1.0) * inv)
            value = v_ext[pl.ds(at, 16), :]
            here = value[0:8]
            dd = value[1:9] - here
            dr = right_of(here) - here
            ta_o[pl.ds(at, 8), :] = ta
            tb_o[pl.ds(at, 8), :] = tb
            tc_o[pl.ds(at, 8), :] = tc
            fd[pl.ds(at, 8), :] = ta * dd + tb * dr
            fr[pl.ds(at, 8), :] = tb * dd + tc * dr
        return carry

    lax.fori_loop(0, ER // 16 - 1, tensors, 0)

    def residuals(at):
        before = pl.ds(pl.multiple_of(at - 8, 8), 16)
        here = pl.ds(at, 8)
        fdw, taw = fd[before, :], ta_o[before, :]
        tc, right_flux, weight = tc_o[here, :], fr[here, :], w_ext[here, :]
        image = fdw[7:15] - fdw[8:16] + left_of(right_flux) - right_flux + weight * v_ext[here, :]
        r = s_ext[here, :] - image
        diag = taw[8:16] + 2.0 * tb_o[here, :] + tc + taw[7:15] + left_of(tc) + weight
        inv = jnp.where(diag != 0.0, 1.0 / diag, 0.0)
        z = r * inv
        z_o[here, :] = z
        return r, inv, z

    def own(e, total):
        at = pl.multiple_of(16 + 8 * e, 8)
        r, inv, z = residuals(at)
        r, inv, z = r[:, 128 : 128 + CD], inv[:, 128 : 128 + CD], z[:, 128 : 128 + CD]
        to = pl.ds(pl.multiple_of(8 * e, 8), 8)
        r_o[to, :] = r
        rd_o[to, :] = inv
        rowsum[pl.ds(e, 1), :] = jnp.sum(r, axis=0, keepdims=True)
        return total + r * z

    residuals(8)
    residuals(16 + RD)
    total = lax.fori_loop(0, CR, own, jnp.zeros((8, CD), F32))
    sums_o[...] = sum(total[:, k * 128 : k * 128 + 128] for k in range(CD // 128))
    sums = block_sums(rowsum[...], group[...])
    for j in range(n_cr):
        blocks_o[j] = sums


def tensor_stage(n_in, n_cr, pos, amp, v, mask, depth, up, down, left, right, put, place, group):
    vmem = pl.BlockSpec(memory_space=VMEM)
    anyw = pl.BlockSpec(memory_space=pl.ANY)
    ext = jax.ShapeDtypeStruct((ER, EC), F32)
    flat = jax.ShapeDtypeStruct((RD, CD), F32)
    return pl.pallas_call(
        functools.partial(tensor_kernel, n_in, n_cr),
        in_specs=[pl.BlockSpec(memory_space=pltpu.SMEM), anyw, anyw] + [vmem] * 9,
        out_specs=[vmem] * 8,
        out_shape=[
            ext, ext, ext, ext, flat, flat,
            jax.ShapeDtypeStruct((n_cr, CR, CC), F32),
            jax.ShapeDtypeStruct((8, 128), F32),
        ],
        scratch_shapes=[
            VMEM((K, ER, EC), BF16), VMEM((ER, EC), F32), VMEM((ER, EC), F32), VMEM((ER, EC), F32),
            VMEM((ER, EC), F32), VMEM((ER, EC), F32), VMEM((CR, CD), F32), pltpu.SemaphoreType.DMA((2,)),
        ],
        compiler_params=pltpu.CompilerParams(vmem_limit_bytes=LIMIT),
        cost_estimate=pl.CostEstimate(flops=10**8, bytes_accessed=2 * 10**7, transcendentals=0),
        name="tensor_stage",
    )(pos, amp, v, mask, depth, up, down, left, right, put, place, group)


def moments_kernel(n_in, n_cr, extra, blocks, fwd_hi, fwd_lo, steps, pay_o, own_o):
    x = jnp.concatenate([blocks[j, :CR] for j in range(n_cr)], axis=1)
    hi, lo = parts2(x)
    both = dot(jnp.concatenate([hi, lo], axis=0), fwd_hi[...])
    x = both[:CR] + both[CR:] + dot(hi, fwd_lo[...])
    width = x.shape[1]
    forth, back = x, x
    for i in range(5):
        d = 1 << i
        zero = jnp.zeros((d, width), F32)
        decay = steps[i : i + 1]
        forth = forth + decay * jnp.concatenate([zero, forth[:-d]], axis=0)
        back = back + decay * jnp.concatenate([back[d:], zero], axis=0)
    decay, scale = steps[0:1], steps[5:6]
    zero = jnp.zeros((1, width), F32)
    inside = forth + decay * jnp.concatenate([back[1:], zero], axis=0)
    inside = scale * inside
    own_o[...] = jnp.concatenate(
        [scale * decay * back[0:1], inside, scale * decay * forth[CR - 1 :], jnp.zeros((6, width), F32)],
        axis=0,
    )
    f = jnp.concatenate([forth[CR - 1 :, 128 * k : 128 * k + 128] for k in range(n_cr)], axis=0)
    b = jnp.concatenate([back[0:1, 128 * k : 128 * k + 128] for k in range(n_cr)], axis=0)
    for i in range(n_in):
        pay_o[i, 0:n_cr] = f
        pay_o[i, n_cr : 2 * n_cr] = b
    if extra:
        sums = sum(blocks[j, CR : CR + 8] for j in range(n_cr))
        energy = jnp.sum(x * inside, axis=0, keepdims=True)
        energy = sum(energy[:, 128 * k : 128 * k + 128] for k in range(n_cr))
        at = lax.broadcasted_iota(jnp.int32, (8, 128), 0)
        sums = jnp.where(at == 3, energy, sums)
        for i in range(n_in):
            pay_o[i, 2 * n_cr : 2 * n_cr + 8] = sums


def moments_stage(n_in, n_cr, extra, blocks, fwd_hi, fwd_lo, steps):
    vmem = pl.BlockSpec(memory_space=VMEM)
    return pl.pallas_call(
        functools.partial(moments_kernel, n_in, n_cr, extra),
        in_specs=[vmem] * 4, out_specs=[vmem] * 2,
        out_shape=[
            jax.ShapeDtypeStruct((n_in, 2 * n_cr + 8 * extra, 128), F32),
            jax.ShapeDtypeStruct((40, CC * n_cr), F32),
        ],
        compiler_params=pltpu.CompilerParams(vmem_limit_bytes=32 * 1024 * 1024),
        cost_estimate=pl.CostEstimate(flops=2 * 10**8, bytes_accessed=5 * 10**6, transcendentals=0),
        name="moments_stage",
    )(blocks, fwd_hi, fwd_lo, steps)


def coarse_values(n_in, n_cr, mine, moments, own, grow, fall, blocks, back_hi, back_lo, spread):
    r32, whole, series, link = (blocks[i] for i in range(4))
    f = [moments[i, 0:n_cr] for i in range(n_in)]
    b = [moments[i, n_cr : 2 * n_cr] for i in range(n_in)]
    hf, hb = f[0], b[n_in - 1]
    for i in range(1, n_in):
        hf = r32 * hf + f[i]
        hb = r32 * hb + b[n_in - 1 - i]
    above = (hb + whole * hf) * series
    below = (hf + whole * hb) * series
    mine_above, mine_below = jnp.zeros_like(above), jnp.zeros_like(below)
    energy = jnp.zeros_like(above)
    for i in range(n_in):
        k = n_in - 1 - i
        mine_above = jnp.where(mine == i, above, mine_above)
        mine_below = jnp.where(mine == k, below, mine_below)
        energy += above * b[i] + below * f[k]
        above = r32 * above + f[i]
        below = r32 * below + b[k]
    energy = energy * link
    a_row = jnp.concatenate([mine_above[k : k + 1] for k in range(n_cr)], axis=1)
    b_row = jnp.concatenate([mine_below[k : k + 1] for k in range(n_cr)], axis=1)
    u = own[...] + a_row * grow[...] + b_row * fall[...]
    hi, lo = parts2(u)
    both = dot(jnp.concatenate([hi, lo], axis=0), back_hi[0])
    values = both[:40] + both[40:] + dot(hi, back_lo[0])
    three = dot(jnp.concatenate(parts3(values), axis=0), spread[...])
    return values, three[:40] + three[40:80] + three[80:], energy


def image_kernel(
    n_in, n_cr, pos, moments, own, grow, fall, blocks, back_hi, back_lo, spread, group,
    ta, tb, tc, z, r, rd, mask, first_blocks, first_sums,
    p_o, q_o, blocks_o, p_ext, fd, fr, rowsum, cs,
):
    values, spread_rows, _ = coarse_values(
        n_in, n_cr, pos[0], moments, own, grow, fall, blocks, back_hi, back_lo, spread
    )
    cs[...] = spread_rows

    def fields(e, carry):
        at = pl.ds(pl.multiple_of(8 + 8 * e, 8), 8)
        p_ext[at, :] = z[at, :] + cs[pl.ds(e, 1), :]
        return carry

    lax.fori_loop(0, CR + 2, fields, 0)

    def fluxes(e, carry):
        at = pl.multiple_of(8 + 8 * e, 8)
        value = p_ext[pl.ds(at, 16), :]
        here = value[0:8]
        dd = value[1:9] - here
        dr = pltpu.roll(here, EC - 1, 1) - here
        at = pl.ds(at, 8)
        b = tb[at, :]
        fd[at, :] = ta[at, :] * dd + b * dr
        fr[at, :] = b * dd + tc[at, :] * dr
        return carry

    lax.fori_loop(0, CR + 1, fluxes, 0)

    def images(e, totals):
        at = pl.multiple_of(16 + 8 * e, 8)
        fdw = fd[pl.ds(pl.multiple_of(at - 8, 8), 16), :]
        side = fr[pl.ds(at, 8), :]
        flux = fdw[7:15] - fdw[8:16] + pltpu.roll(side, 1, 1) - side
        to = pl.ds(pl.multiple_of(8 * e, 8), 8)
        p = p_ext[pl.ds(at, 8), :][:, 128 : 128 + CD]
        q = flux[:, 128 : 128 + CD] + mask[to, :].astype(F32) * p
        p_o[to, :] = p
        q_o[to, :] = q
        rowsum[pl.ds(e, 1), :] = jnp.sum(q, axis=0, keepdims=True)
        return totals[0] + p * q, totals[1] + q * q * rd[to, :]

    zero = jnp.zeros((8, CD), F32)
    pq, qq = lax.fori_loop(0, CR, images, (zero, zero))

    def lanes(x):
        x = jnp.sum(x, axis=0, keepdims=True)
        return sum(x[:, k * 128 : k * 128 + 128] for k in range(CD // 128))

    rp = jnp.sum(first_sums[...], axis=0, keepdims=True)
    rp += jnp.sum(first_blocks[0] * values[1 : CR + 1, :CC], axis=0, keepdims=True)
    tail = jnp.concatenate([rp, lanes(pq), lanes(qq), jnp.zeros((5, 128), F32)], axis=0)
    sums = block_sums(rowsum[...], group[...])
    for j in range(n_cr):
        blocks_o[j, 0:CR] = sums
        blocks_o[j, CR : CR + 8] = tail


def final_kernel(
    n_in, n_cr, pos, moments, own, grow, fall, blocks, back_hi, back_lo, spread,
    p_in, q_in, r_in, rd, v_in, v_o, r_o, d_o, cs,
):
    _, spread_rows, energy = coarse_values(
        n_in, n_cr, pos[0], moments, own, grow, fall, blocks, back_hi, back_lo, spread
    )
    cs[...] = spread_rows
    sums = sum(moments[i, 2 * n_cr : 2 * n_cr + 8] for i in range(n_in))
    old = jnp.sum(sums[0:1], axis=1, keepdims=True)
    curvature = jnp.sum(sums[1:2], axis=1, keepdims=True)
    energy = jnp.sum(jnp.sum(energy, axis=0, keepdims=True), axis=1, keepdims=True)
    image = jnp.sum(sums[2:3] + sums[3:4], axis=1, keepdims=True) + energy
    step = old / curvature
    ratio = (step * step * image - old) / old
    more = 1.0 + ratio

    def body(e, carry):
        at = pl.ds(pl.multiple_of(8 * e, 8), 8)
        p, q = p_in[at, :], q_in[at, :]
        coarse = cs[pl.ds(e + 1, 1), 128 : 128 + CD]
        v_o[at, :] = v_in[at, :] + step * p
        r_o[at, :] = r_in[at, :] - step * q
        d_o[at, :] = more * p - step * (q * rd[at, :] + coarse)
        return carry

    lax.fori_loop(0, CR, body, 0)


def coarse_call(kernel, n_in, n_cr, name, out_shape, scratch, pos, moments, own, tables, rest, group=None):
    n = CC * n_cr

    def whole(t):
        return pl.BlockSpec(t.shape, lambda i, pos, n=t.ndim: (0,) * n)

    pick = pl.BlockSpec((1, n, 2 * CC), lambda i, pos: (pos[1], 0, 0))
    first = [moments, own, tables["grow"], tables["fall"], tables["blocks"]]
    last = [tables["spread"]] + ([group] if group is not None else []) + list(rest)
    return pl.pallas_call(
        functools.partial(kernel, n_in, n_cr),
        grid_spec=pltpu.PrefetchScalarGridSpec(
            num_scalar_prefetch=1, grid=(1,),
            in_specs=[whole(t) for t in first] + [pick, pick] + [whole(t) for t in last],
            out_specs=[whole(t) for t in out_shape], scratch_shapes=scratch,
        ),
        out_shape=out_shape,
        compiler_params=pltpu.CompilerParams(vmem_limit_bytes=LIMIT),
        cost_estimate=pl.CostEstimate(flops=10**8, bytes_accessed=10**7, transcendentals=0),
        name=name,
    )(pos, *first, *tables["back"], *last)


def neighbours(value_low, value_high, axis, count):
    ahead = [(i, i + 1) for i in range(count - 1)]
    behind = [(j, i) for i, j in ahead]
    return lax.ppermute(value_high, axis, ahead), lax.ppermute(value_low, axis, behind)


def per_device(n_in, n_cr, amplitudes, mask, depth, iterate):
    sel, place, rows, put, mix, lanes = (jnp.asarray(t) for t in line_tables())
    tables = coarse_tables(n_in, n_cr)
    pos = jnp.stack([lax.axis_index("inline"), lax.axis_index("crosslin")]).astype(jnp.int32)
    col_first, col_last = pack_columns(amplitudes, iterate, mask, depth, sel)
    left, right = neighbours(col_first, col_last, "crosslin", n_cr)
    row_first, row_last = pack_rows(amplitudes, iterate, mask, depth, left, right, rows, mix, lanes)
    up, down = neighbours(row_first, row_last, "inline", n_in)
    group = jnp.asarray(tables["group"])
    ta, tb, tc, z, r, rd, blocks, sums = tensor_stage(
        n_in, n_cr, pos, amplitudes, iterate, mask, depth, up, down, left, right, put, place, group
    )

    def moments_of(payload, extra):
        gathered = lax.all_to_all(payload, "crosslin", 0, 0, tiled=True)
        pay, own = moments_stage(n_in, n_cr, extra, gathered, *tables["forward"], tables["steps"])
        return lax.all_to_all(pay, "inline", 0, 0, tiled=True), own

    flat = jax.ShapeDtypeStruct((RD, CD), F32)
    ext = VMEM((ER, EC), F32)
    cs = VMEM((40, EC), F32)
    moments, own = moments_of(blocks, False)
    p, q, payload = coarse_call(
        image_kernel, n_in, n_cr, "image_stage",
        [flat, flat, jax.ShapeDtypeStruct((n_cr, CR + 8, CC), F32)],
        [ext, ext, ext, VMEM((CR, CD), F32), cs],
        pos, moments, own, tables, [ta, tb, tc, z, r, rd, mask, blocks, sums], group,
    )
    moments, own = moments_of(payload, True)
    return tuple(
        coarse_call(
            final_kernel, n_in, n_cr, "final_stage", [flat, flat, flat], [cs],
            pos, moments, own, tables, [p, q, r, rd, iterate],
        )
    )


def solution(mesh):
    n_in, n_cr = mesh.shape["inline"], mesh.shape["crosslin"]
    flat = P("inline", "crosslin")
    return jax.shard_map(
        functools.partial(per_device, n_in, n_cr), mesh=mesh,
        in_specs=(P(None, "inline", "crosslin"), flat, flat, flat),
        out_specs=(flat, flat, flat), check_vma=False,
    )
```

```python
import functools

import jax
import jax.numpy as jnp
import ml_dtypes
import numpy as np
from jax import lax
from jax.experimental import pallas as pl
from jax.experimental.pallas import tpu as pltpu
from jax.sharding import PartitionSpec as P

K = 16
DEC = 8
CI = 32
COUPLING = 4.0
F32 = jnp.float32
BF16 = jnp.bfloat16
NPB = ml_dtypes.bfloat16
VMEM = pltpu.VMEM

RD = 256
CD = 1024
ER = RD + 32
EC = CD + 128
CR = RD // DEC
CC = CD // DEC
MSG = 64


def dot(a, b):
    return jnp.dot(a, b, preferred_element_type=F32)


def parts2(x):
    hi = x.astype(BF16)
    return hi, (x - hi.astype(F32)).astype(BF16)


def parts3(x):
    hi = x.astype(BF16)
    rest = x - hi.astype(F32)
    mid = rest.astype(BF16)
    return hi, mid, (rest - mid.astype(F32)).astype(BF16)


def np2(x):
    hi = x.astype(np.float32).astype(NPB)
    return hi, (x - hi.astype(np.float64)).astype(np.float32).astype(NPB)


def line_tables():
    rows = np.zeros((2, MSG, 256), np.float32)
    put = np.zeros((2, 304, MSG), np.float32)
    for s in range(K):
        for k in range(3):
            rows[0, 3 * s + k, 16 * s + k] = 1
            rows[1, 3 * s + k, 16 * s + 13 + k] = 1
    for side in range(2):
        put[side, :256] = rows[side].T
        for l in range(2):
            for part in range(3):
                put[side, 256 + (14 + l if side else l), 48 + 3 * l + part] = 1
        put[side, 272 + (15 if side else 0), 54] = 1
        put[side, 288 + (15 if side else 0), 55] = 1
    mix = np.zeros((2, 3, MSG, 128), np.float32)
    for k in range(3):
        for s in range(K):
            mix[:, k, 3 * s + k, 3 * s : 3 * s + 3] = 1
    for l in range(2):
        for part in range(3):
            for other in range(2):
                mix[0, l, 48 + 3 * l + part, 48 + 3 * other + part] = 1
                mix[1, l + 1, 48 + 3 * l + part, 48 + 3 * other + part] = 1
    for o in (54, 55):
        mix[0, 0, o, o] = 1
        mix[1, 2, o, o] = 1
    lanes = np.zeros((2, 128, 128), np.float32)
    for s in range(K):
        for k in range(3):
            lanes[0, 3 * s + k, k] = 1
            lanes[1, 3 * s + k, 125 + k] = 1
    for l in range(2):
        for part in range(3):
            lanes[0, 48 + 3 * l + part, l] = 1
            lanes[1, 48 + 3 * l + part, 126 + l] = 1
    for o in (54, 55):
        lanes[0, o, 0] = 1
        lanes[1, o, 127] = 1
    return tuple(t.astype(NPB) for t in (rows, put, mix, lanes))


def coarse_tables(n_in, n_cr):
    n = CC * n_cr
    freq = np.arange(n, dtype=np.float64)
    norm = np.where(freq == 0, np.sqrt(1.0 / n), np.sqrt(2.0 / n))

    def cosines(cols):
        phase = (freq[:, None] * (2 * cols[None, :] + 1)) % (4 * n)
        return norm[:, None] * np.cos(np.pi * phase / (2 * n))

    lead = np.arange(n + CC, dtype=np.float64) - 16
    forward = cosines(lead).T * (lead[:, None] >= -1) * (lead[:, None] <= n)
    half = (2.0 - 2.0 * np.cos(np.pi * freq / n) + 1.0 / (CI * CI)) / 2.0
    kappa = np.log1p(half + np.sqrt(half * (half + 2.0)))
    scale = 1.0 / (COUPLING * 2.0 * np.sinh(kappa))
    steps = np.stack([np.exp(-kappa * d) for d in (1, 2, 4, 8, 16)] + [scale] + [scale * 0] * 2)
    at = np.arange(40)[:, None]
    grow = scale * np.exp(-kappa * at) * (at < 34)
    fall = scale * np.exp(-kappa * (33.0 - at)) * (at < 34)
    whole = CR * n_in
    blocks = np.stack(
        [
            np.exp(-kappa * CR),
            np.exp(-kappa * whole),
            1.0 / (1.0 - np.exp(-kappa * 2 * whole)),
            scale * np.exp(-kappa),
        ]
    ).reshape(4, n_cr, 128)
    spread = np.zeros((2 * CC, EC))
    for lane in range(EC):
        col = ((lane if lane >= 64 else lane + EC) - 128) // DEC
        if -1 <= col <= CC:
            spread[16 + col, lane] = 1
    group = np.zeros((CD, CC))
    group[np.arange(CD), np.arange(CD) // DEC] = 1
    f = np.float32
    return dict(
        forward=np2(forward), steps=steps.astype(f), grow=grow.astype(f),
        fall=fall.astype(f), blocks=blocks.astype(f), spread=spread.astype(NPB), group=group.astype(NPB),
    )


def moved(x, lane, to):
    turn = (to - lane) % x.shape[1]
    return pltpu.roll(x, turn, 1) if turn else x


def pack_columns_kernel(amp, v_in, m_in, d_in, out0, out1, a, v, m, d, sems):
    copies = []
    for side, at in enumerate((0, CD - 128)):
        span = pl.ds(at, 128)
        copies.append(pltpu.make_async_copy(amp.at[:, :, span], a.at[side], sems.at[side, 0]))
        copies.append(pltpu.make_async_copy(v_in.at[:, span], v.at[side], sems.at[side, 1]))
        copies.append(pltpu.make_async_copy(m_in.at[:, span], m.at[side], sems.at[side, 2]))
        copies.append(pltpu.make_async_copy(d_in.at[:, span], d.at[side], sems.at[side, 3]))
    for c in copies:
        c.start()
    lane = lax.broadcasted_iota(jnp.int32, (RD, 128), 1)
    for c in copies:
        c.wait()
    for side, out in enumerate((out0, out1)):
        low = 125 if side else 0
        weight = m[side].astype(F32)
        source = weight * (d[side].astype(F32) - 0.5 * (K - 1))
        end = 127 if side else 0
        total = jnp.where(lane == 54, moved(weight, end, 54), moved(source, end, 55))
        for part, value in enumerate(parts3(v[side])):
            value = value.astype(F32)
            for l in range(2):
                to = 48 + 3 * l + part
                total = jnp.where(lane == to, moved(value, (126 if side else 0) + l, to), total)
        for s in range(K):
            total = jnp.where((lane >= 3 * s) & (lane < 3 * s + 3), moved(a[side, s].astype(F32), low, 3 * s), total)
        out[...] = jnp.where(lane < 56, total, 0.0).astype(BF16)


def pack_columns(amplitudes, iterate, mask, depth):
    hbm = pl.BlockSpec(memory_space=pltpu.HBM)
    out = jax.ShapeDtypeStruct((RD, 128), BF16)
    return pl.pallas_call(
        pack_columns_kernel, in_specs=[hbm] * 4,
        out_specs=[pl.BlockSpec(memory_space=VMEM)] * 2, out_shape=[out, out],
        scratch_shapes=[
            VMEM((2, K, RD, 128), BF16), VMEM((2, RD, 128), F32), VMEM((2, RD, 128), jnp.int32),
            VMEM((2, RD, 128), jnp.int32), pltpu.SemaphoreType.DMA((2, 4)),
        ],
        compiler_params=pltpu.CompilerParams(vmem_limit_bytes=60 * 1024 * 1024),
        cost_estimate=pl.CostEstimate(flops=10**7, bytes_accessed=3 * 10**6, transcendentals=0),
        name="pack_columns",
    )(amplitudes, iterate, mask, depth)


def pack_rows_kernel(
    amp, v_in, m_in, d_in, left, right, rows, mix, lanes, out0, out1, a, v, m, d, sems
):
    copies = []
    for side in range(2):
        copies.append(pltpu.make_async_copy(amp.at[:, pl.ds(side * (RD - 16), 16)], a.at[side], sems.at[side, 0]))
        for i, (source, to) in enumerate(((v_in, v), (m_in, m), (d_in, d))):
            copies.append(
                pltpu.make_async_copy(source.at[pl.ds(side * (RD - 8), 8)], to.at[side], sems.at[side, 1 + i])
            )
    for c in copies:
        c.start()
    for c in copies:
        c.wait()
    at = lax.broadcasted_iota(jnp.int32, (MSG, CD), 0)
    for side, out in enumerate((out0, out1)):
        middle = dot(rows[side], a[side].reshape(K * 16, CD))
        split = [p.astype(F32) for p in parts3(v[side])]
        for l in range(2):
            row = 6 + l if side else l
            for part in range(3):
                middle = jnp.where(at == 48 + 3 * l + part, split[part][row : row + 1], middle)
        row = 7 if side else 0
        weight = m[side, row : row + 1].astype(F32)
        source = weight * (d[side, row : row + 1].astype(F32) - 0.5 * (K - 1))
        middle = jnp.where(at == 54, weight, jnp.where(at == 55, source, middle))
        out[:, 128:] = middle.astype(BF16)
        total = jnp.zeros((MSG, 128), F32)
        for halo, which in ((left, 1), (right, 0)):
            edge = halo[RD - 16 : RD].astype(F32)[13:16] if side else halo[0:16].astype(F32)[0:3]
            for k in range(3):
                term = mix[side, k].astype(F32) * edge[k : k + 1]
                total += dot(term.astype(BF16), lanes[which])
        out[:, 0:128] = total.astype(BF16)


def pack_rows(amplitudes, iterate, mask, depth, left, right, rows, mix, lanes):
    hbm = pl.BlockSpec(memory_space=pltpu.HBM)
    vmem = pl.BlockSpec(memory_space=VMEM)
    out = jax.ShapeDtypeStruct((MSG, EC), BF16)
    return pl.pallas_call(
        pack_rows_kernel, in_specs=[hbm] * 4 + [vmem] * 5, out_specs=[vmem] * 2, out_shape=[out, out],
        scratch_shapes=[
            VMEM((2, K, 16, CD), BF16), VMEM((2, 8, CD), F32), VMEM((2, 8, CD), jnp.int32),
            VMEM((2, 8, CD), jnp.int32), pltpu.SemaphoreType.DMA((2, 4)),
        ],
        compiler_params=pltpu.CompilerParams(vmem_limit_bytes=58 * 1024 * 1024),
        cost_estimate=pl.CostEstimate(flops=10**7, bytes_accessed=2 * 10**6, transcendentals=0),
        name="pack_rows",
    )(amplitudes, iterate, mask, depth, left, right, rows, mix, lanes)


def gradient_sums(window, off, take):
    total = None
    for s in range(K):
        x = window(s).astype(F32)
        n = x.shape[1]
        middle = x[8:24]
        gc = (pltpu.roll(middle, n - 1, 1) - pltpu.roll(middle, 1, 1))[:, off : off + take]
        x = x[:, off : off + take]
        gi = pltpu.roll(x, 31, 0)[8:24] - pltpu.roll(x, 1, 0)[8:24]
        terms = (gi * gi, gi * gc, gc * gc)
        total = terms if total is None else tuple(t + u for t, u in zip(total, terms))
    return total


def inner_kernel(first, steps, amp, sii_o, sic_o, scc_o, edge_o, a, sems):
    rows = 16 * (steps + 1)
    half = 64
    bounds = [(r, min(half, rows - r)) for r in range(0, rows, half)]
    copies = [
        pltpu.make_async_copy(amp.at[:, pl.ds(16 * first + r, n)], a.at[:, pl.ds(r, n)], sems.at[i])
        for i, (r, n) in enumerate(bounds)
    ]
    for c in copies:
        c.start()
    lane = lax.broadcasted_iota(jnp.int32, (16, 128), 1)

    def step(t, carry):
        at = pl.multiple_of(16 * t, 16)
        for part in range(2):
            lanes = slice(0, 640) if part == 0 else slice(384, CD)
            off = 0 if part == 0 else 128
            sums = gradient_sums(lambda s: a[s, pl.ds(at, 32), lanes], off, 512)
            for o, value in zip((sii_o, sic_o, scc_o), sums):
                o[pl.ds(at, 16), 512 * part : 512 * part + 512] = value
        return carry

    def edges(t, carry):
        at = pl.ds(pl.multiple_of(16 * t, 16), 16)
        for s in range(K):
            low = moved(a[s, at, 0:128].astype(F32), 0, 35)
            high = moved(a[s, at, CD - 128 : CD].astype(F32), 125, 64)
            tile = jnp.where((lane >= 35) & (lane < 38), low, jnp.where((lane >= 64) & (lane < 67), high, 0.0))
            edge_o[s, at, :] = tile.astype(BF16)
        return carry

    done = 0
    for i, (r, n) in enumerate(bounds):
        copies[i].wait()
        until = min(steps, (r + n) // 16 - 1)
        lax.fori_loop(done, until, step, 0)
        done = until
    lax.fori_loop(0, steps + 1, edges, 0)


def inner_stage(first, steps, amplitudes):
    rows = 16 * (steps + 1)
    flat = jax.ShapeDtypeStruct((16 * steps, CD), F32)
    return pl.pallas_call(
        functools.partial(inner_kernel, first, steps),
        in_specs=[pl.BlockSpec(memory_space=pltpu.HBM)], out_specs=[pl.BlockSpec(memory_space=VMEM)] * 4,
        out_shape=[flat, flat, flat, jax.ShapeDtypeStruct((K, rows, 128), BF16)],
        scratch_shapes=[VMEM((K, rows, CD), BF16), pltpu.SemaphoreType.DMA((4,))],
        compiler_params=pltpu.CompilerParams(vmem_limit_bytes=57 * 1024 * 1024),
        cost_estimate=pl.CostEstimate(flops=10**8, bytes_accessed=6 * 10**6, transcendentals=0),
        name="inner_stage",
    )(amplitudes)


def block_sums(rows, group):
    return sum(dot(part, group) for part in parts3(rows))


def tensor_kernel(
    n_in, n_cr, cuts, pos, amp, v_in, mask, depth, up, down, left, right, put, group, *rest
):
    inner_refs, rest = rest[: 4 * len(cuts)], rest[4 * len(cuts) :]
    (ta_o, tb_o, tc_o, z_o, r_o, rd_o, blocks_o, sums_o,
     tops, rim, v_ext, w_ext, s_ext, fd, fr, rowsum, sems) = rest
    inner = (slice(16, 16 + RD), slice(128, EC))
    copies = [
        pltpu.make_async_copy(amp.at[:, 0:16], tops.at[0, :, 16:32, 128:EC], sems.at[0]),
        pltpu.make_async_copy(amp.at[:, RD - 16 : RD], tops.at[1, :, 0:16, 128:EC], sems.at[1]),
        pltpu.make_async_copy(v_in, v_ext.at[16 : 16 + RD, 128:EC], sems.at[2]),
    ]
    for c in copies:
        c.start()
    weight = mask[...].astype(F32)
    w_ext[inner] = weight
    s_ext[inner] = weight * (depth[...].astype(F32) - 0.5 * (K - 1))
    lane = lax.broadcasted_iota(jnp.int32, (RD, 128), 1)
    before, after = left[...].astype(F32), right[...].astype(F32)
    here = slice(16, 16 + RD)
    value = jnp.zeros((RD, 128), F32)
    for l in range(2):
        for halo, to in ((before, 126 + l), (after, l)):
            got = sum(moved(halo, 48 + 3 * l + part, to) for part in range(3))
            value = jnp.where(lane == to, got, value)
    v_ext[here, 0:128] = value
    for o, message in ((w_ext, 54), (s_ext, 55)):
        value = jnp.where(lane == 127, moved(before, message, 127), 0.0)
        o[here, 0:128] = jnp.where(lane == 0, moved(after, message, 0), value)
    for s in range(K):
        value = jnp.where(lane < 3, moved(after, 3 * s, 0), 0.0)
        value = jnp.where(lane >= 125, moved(before, 3 * s, 125), value).astype(BF16)
        tops[0, s, 16:32, 0:128] = value[0:16]
        tops[1, s, 0:16, 0:128] = value[RD - 16 : RD]
    for c, (first, steps) in enumerate(cuts):
        begin, rows = (0 if c == 0 else 16 * first + 16), 16 * (steps + 1)
        at = begin - 16 * first
        span, local = slice(begin, 16 * first + rows), slice(at, rows)
        turned, turned_after, tile = before[span], after[span], lane[span]
        for s in range(K):
            value = inner_refs[4 * c + 3][s, local, :].astype(F32)
            value = jnp.where((tile >= 32) & (tile < 35), moved(turned, 3 * s, 32), value)
            value = jnp.where((tile >= 67) & (tile < 70), moved(turned_after, 3 * s, 67), value)
            rim[s, span, :] = value.astype(BF16)
    for side, halo, row in ((1, up, 0), (0, down, 16 + RD)):
        lines = dot(put[side], halo[...])
        for s in range(K):
            tops[1 - side, s, 16 - 16 * side : 32 - 16 * side, :] = lines[16 * s : 16 * s + 16].astype(BF16)
        v_ext[row : row + 16, :] = lines[256:272]
        w_ext[row : row + 16, :] = lines[272:288]
        s_ext[row : row + 16, :] = lines[288:304]
    for c in copies:
        c.wait()
    at_lane = lax.broadcasted_iota(jnp.int32, (1, EC), 1)
    col = pos[1] * CD + jnp.where(at_lane < 64, at_lane + CD, at_lane - 128)
    valid_right = ((col >= 0) & (col < n_cr * CD - 1)).astype(F32)
    row_iota = lax.broadcasted_iota(jnp.int32, (16, 1), 0)
    tile_lane = lax.broadcasted_iota(jnp.int32, (16, 128), 1)

    def left_of(x):
        return pltpu.roll(x, 1, 1)

    def right_of(x):
        return pltpu.roll(x, EC - 1, 1)

    def finish(at, sums):
        sii, sic, scc = (0.25 * x for x in sums)
        inv = 1.0 / (sii + scc + 2.0)
        row = pos[0] * RD - 16 + at + row_iota
        valid_down = ((row >= 0) & (row < n_in * RD - 1)).astype(F32)
        ta = valid_down * ((scc + 1.0) * inv)
        tb = (valid_down * valid_right) * (-sic * inv)
        tc = valid_right * ((sii + 1.0) * inv)
        value = v_ext[pl.ds(at, 24), :]
        here = value[0:16]
        dd = value[1:17] - here
        dr = right_of(here) - here
        to = pl.ds(at, 16)
        ta_o[to, :] = ta
        tb_o[to, :] = tb
        tc_o[to, :] = tc
        fd[to, :] = ta * dd + tb * dr
        fr[to, :] = tb * dd + tc * dr

    for side in range(2):
        sums = gradient_sums(lambda s, side=side: tops[side, s], 0, EC)
        finish(8 + side * (RD), sums)

    for c, (first, steps) in enumerate(cuts):
        sii, sic, scc = inner_refs[4 * c : 4 * c + 3]

        def step(t, carry, sii=sii, sic=sic, scc=scc, first=first):
            local = pl.ds(pl.multiple_of(16 * (t - first), 16), 16)
            at = pl.multiple_of(16 * t, 16)
            edge = gradient_sums(lambda s: rim[s, pl.ds(at, 32), :], 0, 128)
            sums = []
            for ref, e in zip((sii, sic, scc), edge):
                low, high = pltpu.roll(e, 93, 1), pltpu.roll(e, 61, 1)
                x = ref[local, :]
                sums.append(
                    jnp.concatenate(
                        [
                            jnp.where(tile_lane < 64, high, low),
                            jnp.where(tile_lane == 0, low, x[:, 0:128]),
                            x[:, 128 : CD - 128],
                            jnp.where(tile_lane == 127, high, x[:, CD - 128 :]),
                        ],
                        axis=1,
                    )
                )
            finish(pl.multiple_of(24 + 16 * t, 8), sums)
            return carry

        lax.fori_loop(first, first + steps, step, 0)

    def residuals(at, n):
        before = pl.ds(pl.multiple_of(at - 8, 8), n + 8)
        here = pl.ds(at, n)
        fdw, taw = fd[before, :], ta_o[before, :]
        tc, right_flux, weight = tc_o[here, :], fr[here, :], w_ext[here, :]
        image = fdw[7 : n + 7] - fdw[8 : n + 8] + left_of(right_flux) - right_flux + weight * v_ext[here, :]
        r = s_ext[here, :] - image
        diag = taw[8 : n + 8] + 2.0 * tb_o[here, :] + tc + taw[7 : n + 7] + left_of(tc) + weight
        inv = jnp.where(diag != 0.0, 1.0 / diag, 0.0)
        z = r * inv
        z_o[here, :] = z
        return r, inv, z

    def own(e, total):
        at = pl.multiple_of(16 + 16 * e, 16)
        r, inv, z = (x[:, 128:] for x in residuals(at, 16))
        to = pl.ds(pl.multiple_of(16 * e, 16), 16)
        r_o[to, :] = r
        rd_o[to, :] = inv
        rowsum[pl.ds(2 * e, 1), :] = jnp.sum(r[0:8], axis=0, keepdims=True)
        rowsum[pl.ds(2 * e + 1, 1), :] = jnp.sum(r[8:16], axis=0, keepdims=True)
        rz = r * z
        rz = rz[0:8] + rz[8:16]
        return total + sum(rz[:, k * 128 : k * 128 + 128] for k in range(CD // 128))

    residuals(8, 8)
    residuals(16 + RD, 8)
    sums_o[...] = lax.fori_loop(0, RD // 16, own, jnp.zeros((8, 128), F32))
    sums = block_sums(rowsum[...], group[...])
    for j in range(n_cr):
        blocks_o[j] = sums


def tensor_stage(n_in, n_cr, cuts, pos, amp, v, mask, depth, up, down, left, right, put, group, sums):
    vmem = pl.BlockSpec(memory_space=VMEM)
    hbm = pl.BlockSpec(memory_space=pltpu.HBM)
    ext = jax.ShapeDtypeStruct((ER, EC), F32)
    flat = jax.ShapeDtypeStruct((RD, CD), F32)
    return pl.pallas_call(
        functools.partial(tensor_kernel, n_in, n_cr, cuts),
        in_specs=[pl.BlockSpec(memory_space=pltpu.SMEM), hbm, hbm] + [vmem] * (8 + len(sums)),
        out_specs=[vmem] * 8,
        out_shape=[
            ext, ext, ext, ext, flat, flat,
            jax.ShapeDtypeStruct((n_cr, CR, CC), F32),
            jax.ShapeDtypeStruct((8, 128), F32),
        ],
        scratch_shapes=[
            VMEM((2, K, 32, EC), BF16), VMEM((K, RD, 128), BF16), VMEM((ER, EC), F32), VMEM((ER, EC), F32),
            VMEM((ER, EC), F32), VMEM((ER, EC), F32), VMEM((ER, EC), F32), VMEM((CR, CD), F32),
            pltpu.SemaphoreType.DMA((3,)),
        ],
        compiler_params=pltpu.CompilerParams(vmem_limit_bytes=42 * 1024 * 1024),
        cost_estimate=pl.CostEstimate(flops=10**8, bytes_accessed=2 * 10**7, transcendentals=0),
        name="tensor_stage",
    )(pos, amp, v, mask, depth, up, down, left, right, put, group, *sums)


def moments_kernel(n_in, n_cr, extra, blocks, fwd_hi, fwd_lo, steps, pay_o, own_o):
    x = jnp.concatenate([blocks[j, :CR] for j in range(n_cr)], axis=1)
    hi, lo = parts2(x)
    span = slice(16, 16 + x.shape[1])
    both = dot(jnp.concatenate([hi, lo], axis=0), fwd_hi[span, :])
    x = both[:CR] + both[CR:] + dot(hi, fwd_lo[span, :])
    width = x.shape[1]
    forth, back = x, x
    for i in range(5):
        d = 1 << i
        zero = jnp.zeros((d, width), F32)
        decay = steps[i : i + 1]
        forth = forth + decay * jnp.concatenate([zero, forth[:-d]], axis=0)
        back = back + decay * jnp.concatenate([back[d:], zero], axis=0)
    decay, scale = steps[0:1], steps[5:6]
    zero = jnp.zeros((1, width), F32)
    inside = forth + decay * jnp.concatenate([back[1:], zero], axis=0)
    inside = scale * inside
    own_o[...] = jnp.concatenate(
        [scale * decay * back[0:1], inside, scale * decay * forth[CR - 1 :], jnp.zeros((6, width), F32)],
        axis=0,
    )
    f = jnp.concatenate([forth[CR - 1 :, 128 * k : 128 * k + 128] for k in range(n_cr)], axis=0)
    b = jnp.concatenate([back[0:1, 128 * k : 128 * k + 128] for k in range(n_cr)], axis=0)
    for i in range(n_in):
        pay_o[i, 0:n_cr] = f
        pay_o[i, n_cr : 2 * n_cr] = b
    if extra:
        sums = sum(blocks[j, CR : CR + 8] for j in range(n_cr))
        energy = jnp.sum(x * inside, axis=0, keepdims=True)
        energy = sum(energy[:, 128 * k : 128 * k + 128] for k in range(n_cr))
        at = lax.broadcasted_iota(jnp.int32, (8, 128), 0)
        sums = jnp.where(at == 3, energy, sums)
        for i in range(n_in):
            pay_o[i, 2 * n_cr : 2 * n_cr + 8] = sums


def moments_stage(n_in, n_cr, extra, blocks, fwd_hi, fwd_lo, steps):
    vmem = pl.BlockSpec(memory_space=VMEM)
    return pl.pallas_call(
        functools.partial(moments_kernel, n_in, n_cr, extra),
        in_specs=[vmem] * 4, out_specs=[vmem] * 2,
        out_shape=[
            jax.ShapeDtypeStruct((n_in, 2 * n_cr + 8 * extra, 128), F32),
            jax.ShapeDtypeStruct((40, CC * n_cr), F32),
        ],
        compiler_params=pltpu.CompilerParams(vmem_limit_bytes=32 * 1024 * 1024),
        cost_estimate=pl.CostEstimate(flops=2 * 10**8, bytes_accessed=5 * 10**6, transcendentals=0),
        name="moments_stage",
    )(blocks, fwd_hi, fwd_lo, steps)


def coarse_values(n_in, n_cr, pos, moments, own, grow, fall, blocks, fwd_hi, fwd_lo, spread):
    mine = pos[0]
    r32, whole, series, link = (blocks[i] for i in range(4))
    f = [moments[i, 0:n_cr] for i in range(n_in)]
    b = [moments[i, n_cr : 2 * n_cr] for i in range(n_in)]
    hf, hb = f[0], b[n_in - 1]
    for i in range(1, n_in):
        hf = r32 * hf + f[i]
        hb = r32 * hb + b[n_in - 1 - i]
    above = (hb + whole * hf) * series
    below = (hf + whole * hb) * series
    mine_above, mine_below = jnp.zeros_like(above), jnp.zeros_like(below)
    energy = jnp.zeros_like(above)
    for i in range(n_in):
        k = n_in - 1 - i
        mine_above = jnp.where(mine == i, above, mine_above)
        mine_below = jnp.where(mine == k, below, mine_below)
        energy += above * b[i] + below * f[k]
        above = r32 * above + f[i]
        below = r32 * below + b[k]
    energy = energy * link
    a_row = jnp.concatenate([mine_above[k : k + 1] for k in range(n_cr)], axis=1)
    b_row = jnp.concatenate([mine_below[k : k + 1] for k in range(n_cr)], axis=1)
    u = own[...] + a_row * grow[...] + b_row * fall[...]
    hi, lo = parts2(u)
    span = pl.ds(pl.multiple_of(pos[1] * CC, CC), 2 * CC)
    turned = (((1,), (1,)), ((), ()))
    both = lax.dot_general(jnp.concatenate([hi, lo], axis=0), fwd_hi[span, :], turned, preferred_element_type=F32)
    values = both[:40] + both[40:] + lax.dot_general(hi, fwd_lo[span, :], turned, preferred_element_type=F32)
    three = dot(jnp.concatenate(parts3(values), axis=0), spread[...])
    return values, three[:40] + three[40:80] + three[80:], energy


def image_kernel(
    n_in, n_cr, pos, moments, own, grow, fall, blocks, fwd_hi, fwd_lo, spread, group,
    ta, tb, tc, z, rd, mask, first_blocks, first_sums,
    p_o, q_o, blocks_o, rowsum, cs,
):
    values, spread_rows, _ = coarse_values(
        n_in, n_cr, pos, moments, own, grow, fall, blocks, fwd_hi, fwd_lo, spread
    )
    cs[...] = spread_rows

    def field(strip):
        at = pl.ds(pl.multiple_of(8 + 8 * strip, 8), 8)
        return z[at, :] + cs[pl.ds(strip, 1), :]

    def fluxes(at, n, value):
        here = value[0:n]
        dd = value[1 : n + 1] - here
        dr = pltpu.roll(here, EC - 1, 1) - here
        at = pl.ds(at, n)
        b = tb[at, :]
        return ta[at, :] * dd + b * dr, b * dd + tc[at, :] * dr

    def images(e, carry):
        pq, qq, strip, above = carry
        following = [field(2 * e + 2), field(2 * e + 3)]
        value = jnp.concatenate([strip] + following, axis=0)
        down, side = fluxes(pl.multiple_of(16 + 16 * e, 16), 16, value)
        flux = jnp.concatenate([above[7:8], down[0:15]], axis=0) - down + pltpu.roll(side, 1, 1) - side
        to = pl.ds(pl.multiple_of(16 * e, 16), 16)
        p = value[0:16, 128:]
        q = flux[:, 128:] + mask[to, :].astype(F32) * p
        p_o[to, :] = p
        q_o[to, :] = q
        rowsum[pl.ds(2 * e, 1), :] = jnp.sum(q[0:8], axis=0, keepdims=True)
        rowsum[pl.ds(2 * e + 1, 1), :] = jnp.sum(q[8:16], axis=0, keepdims=True)
        return pq + folded(p * q), qq + folded(q * q * rd[to, :]), following[1], down[8:16]

    def folded(x):
        x = x[0:8] + x[8:16]
        return sum(x[:, k * 128 : k * 128 + 128] for k in range(CD // 128))

    strip = field(1)
    above, _ = fluxes(8, 8, jnp.concatenate([field(0), strip], axis=0))
    zero = jnp.zeros((8, 128), F32)
    pq, qq, _, _ = lax.fori_loop(0, RD // 16, images, (zero, zero, strip, above))

    def lanes(x):
        return jnp.sum(x, axis=0, keepdims=True)

    rp = jnp.sum(first_sums[...], axis=0, keepdims=True)
    rp += jnp.sum(first_blocks[0] * pltpu.roll(values, 2 * CC - 16, 1)[1 : CR + 1, :CC], axis=0, keepdims=True)
    tail = jnp.concatenate([rp, lanes(pq), lanes(qq), jnp.zeros((5, 128), F32)], axis=0)
    sums = block_sums(rowsum[...], group[...])
    for j in range(n_cr):
        blocks_o[j, 0:CR] = sums
        blocks_o[j, CR : CR + 8] = tail


def final_kernel(
    n_in, n_cr, pos, moments, own, grow, fall, blocks, fwd_hi, fwd_lo, spread,
    p_in, q_in, r_in, rd, v_in, v_o, r_o, d_o, cs,
):
    _, spread_rows, energy = coarse_values(
        n_in, n_cr, pos, moments, own, grow, fall, blocks, fwd_hi, fwd_lo, spread
    )
    cs[...] = spread_rows
    sums = sum(moments[i, 2 * n_cr : 2 * n_cr + 8] for i in range(n_in))
    old = jnp.sum(sums[0:1], axis=1, keepdims=True)
    curvature = jnp.sum(sums[1:2], axis=1, keepdims=True)
    energy = jnp.sum(jnp.sum(energy, axis=0, keepdims=True), axis=1, keepdims=True)
    image = jnp.sum(sums[2:3] + sums[3:4], axis=1, keepdims=True) + energy
    step = old / curvature
    ratio = (step * step * image - old) / old
    more = 1.0 + ratio

    def body(e, carry):
        at = pl.ds(pl.multiple_of(16 * e, 16), 16)
        p, q = p_in[at, :], q_in[at, :]
        coarse = [jnp.broadcast_to(cs[pl.ds(2 * e + k, 1), 128:], (8, CD)) for k in (1, 2)]
        coarse = jnp.concatenate(coarse, axis=0)
        v_o[at, :] = v_in[at, :] + step * p
        r_o[at, :] = r_in[at, :] - step * q
        d_o[at, :] = more * p - step * (q * rd[at, :] + coarse)
        return carry

    lax.fori_loop(0, RD // 16, body, 0)


def coarse_call(kernel, n_in, n_cr, name, out_shape, scratch, pos, moments, own, tables, rest, group=None):
    vmem = pl.BlockSpec(memory_space=VMEM)
    args = [moments, own, tables["grow"], tables["fall"], tables["blocks"], *tables["forward"], tables["spread"]]
    args += ([group] if group is not None else []) + list(rest)
    return pl.pallas_call(
        functools.partial(kernel, n_in, n_cr),
        in_specs=[pl.BlockSpec(memory_space=pltpu.SMEM)] + [vmem] * len(args),
        out_specs=[vmem] * len(out_shape), out_shape=out_shape, scratch_shapes=scratch,
        compiler_params=pltpu.CompilerParams(vmem_limit_bytes=32 * 1024 * 1024),
        cost_estimate=pl.CostEstimate(flops=10**8, bytes_accessed=10**7, transcendentals=0),
        name=name,
    )(pos, *args)


def neighbours(value_low, value_high, axis, count):
    ahead = [(i, i + 1) for i in range(count - 1)]
    behind = [(j, i) for i, j in ahead]
    return lax.ppermute(value_high, axis, ahead), lax.ppermute(value_low, axis, behind)


def per_device(n_in, n_cr, amplitudes, mask, depth, iterate):
    rows, put, mix, lanes = (jnp.asarray(t) for t in line_tables())
    tables = coarse_tables(n_in, n_cr)
    pos = jnp.stack([lax.axis_index("inline"), lax.axis_index("crosslin")]).astype(jnp.int32)
    col_first, col_last = pack_columns(amplitudes, iterate, mask, depth)
    left, right = neighbours(col_first, col_last, "crosslin", n_cr)
    cuts = ((0, 7), (7, 8))
    inner = inner_stage(*cuts[0], amplitudes)
    (left, right), inner = lax.optimization_barrier(((left, right), inner))
    row_first, row_last = pack_rows(amplitudes, iterate, mask, depth, left, right, rows, mix, lanes)
    up, down = neighbours(row_first, row_last, "inline", n_in)
    inner = list(inner) + list(inner_stage(*cuts[1], amplitudes))
    group = jnp.asarray(tables["group"])
    ta, tb, tc, z, r, rd, blocks, sums = tensor_stage(
        n_in, n_cr, cuts, pos, amplitudes, iterate, mask, depth, up, down, left, right, put, group, inner
    )

    def moments_of(payload, extra):
        gathered = lax.all_to_all(payload, "crosslin", 0, 0, tiled=True)
        pay, own = moments_stage(n_in, n_cr, extra, gathered, *tables["forward"], tables["steps"])
        return lax.all_to_all(pay, "inline", 0, 0, tiled=True), own

    flat = jax.ShapeDtypeStruct((RD, CD), F32)
    cs = VMEM((40, EC), F32)
    moments, own = moments_of(blocks, False)
    p, q, payload = coarse_call(
        image_kernel, n_in, n_cr, "image_stage",
        [flat, flat, jax.ShapeDtypeStruct((n_cr, CR + 8, CC), F32)],
        [VMEM((CR, CD), F32), cs],
        pos, moments, own, tables, [ta, tb, tc, z, rd, mask, blocks, sums], group,
    )
    moments, own = moments_of(payload, True)
    return tuple(
        coarse_call(
            final_kernel, n_in, n_cr, "final_stage", [flat, flat, flat], [cs],
            pos, moments, own, tables, [p, q, r, rd, iterate],
        )
    )


def solution(mesh):
    n_in, n_cr = mesh.shape["inline"], mesh.shape["crosslin"]
    flat = P("inline", "crosslin")
    return jax.shard_map(
        functools.partial(per_device, n_in, n_cr), mesh=mesh,
        in_specs=(P(None, "inline", "crosslin"), flat, flat, flat),
        out_specs=(flat, flat, flat), check_vma=False,
    )
```

```python
import functools

import jax
import jax.numpy as jnp
import ml_dtypes
import numpy as np
from jax import lax
from jax.experimental import pallas as pl
from jax.experimental.pallas import tpu as pltpu
from jax.sharding import PartitionSpec as P

K = 16
DEC = 8
CI = 32
COUPLING = 4.0
F32 = jnp.float32
BF16 = jnp.bfloat16
NPB = ml_dtypes.bfloat16
VMEM = pltpu.VMEM

RD = 256
CD = 1024
ER = RD + 32
EC = CD + 128
CR = RD // DEC
CC = CD // DEC
MSG = 64


def dot(a, b):
    return jnp.dot(a, b, preferred_element_type=F32)


def parts2(x):
    hi = x.astype(BF16)
    return hi, (x - hi.astype(F32)).astype(BF16)


def parts3(x):
    hi = x.astype(BF16)
    rest = x - hi.astype(F32)
    mid = rest.astype(BF16)
    return hi, mid, (rest - mid.astype(F32)).astype(BF16)


def np2(x):
    hi = x.astype(np.float32).astype(NPB)
    return hi, (x - hi.astype(np.float64)).astype(np.float32).astype(NPB)


def line_tables():
    rows = np.zeros((2, MSG, 256), np.float32)
    put = np.zeros((2, 304, MSG), np.float32)
    for s in range(K):
        for k in range(3):
            rows[0, 3 * s + k, 16 * s + k] = 1
            rows[1, 3 * s + k, 16 * s + 13 + k] = 1
    for side in range(2):
        put[side, :256] = rows[side].T
        for l in range(2):
            for part in range(3):
                put[side, 256 + (14 + l if side else l), 48 + 3 * l + part] = 1
        put[side, 272 + (15 if side else 0), 54] = 1
        put[side, 288 + (15 if side else 0), 55] = 1
    mix = np.zeros((2, 3, MSG, 128), np.float32)
    for k in range(3):
        for s in range(K):
            mix[:, k, 3 * s + k, 3 * s : 3 * s + 3] = 1
    for l in range(2):
        for part in range(3):
            for other in range(2):
                mix[0, l, 48 + 3 * l + part, 48 + 3 * other + part] = 1
                mix[1, l + 1, 48 + 3 * l + part, 48 + 3 * other + part] = 1
    for o in (54, 55):
        mix[0, 0, o, o] = 1
        mix[1, 2, o, o] = 1
    lanes = np.zeros((2, 128, 128), np.float32)
    for s in range(K):
        for k in range(3):
            lanes[0, 3 * s + k, k] = 1
            lanes[1, 3 * s + k, 125 + k] = 1
    for l in range(2):
        for part in range(3):
            lanes[0, 48 + 3 * l + part, l] = 1
            lanes[1, 48 + 3 * l + part, 126 + l] = 1
    for o in (54, 55):
        lanes[0, o, 0] = 1
        lanes[1, o, 127] = 1
    return tuple(t.astype(NPB) for t in (rows, put, mix, lanes))


def coarse_tables(n_in, n_cr):
    n = CC * n_cr
    freq = np.arange(n, dtype=np.float64)
    norm = np.where(freq == 0, np.sqrt(1.0 / n), np.sqrt(2.0 / n))

    def cosines(cols):
        phase = (freq[:, None] * (2 * cols[None, :] + 1)) % (4 * n)
        return norm[:, None] * np.cos(np.pi * phase / (2 * n))

    lead = np.arange(n + CC, dtype=np.float64) - 16
    forward = cosines(lead).T * (lead[:, None] >= -1) * (lead[:, None] <= n)
    half = (2.0 - 2.0 * np.cos(np.pi * freq / n) + 1.0 / (CI * CI)) / 2.0
    kappa = np.log1p(half + np.sqrt(half * (half + 2.0)))
    scale = 1.0 / (COUPLING * 2.0 * np.sinh(kappa))
    steps = np.stack([np.exp(-kappa * d) for d in (1, 2, 4, 8, 16)] + [scale] + [scale * 0] * 2)
    at = np.arange(40)[:, None]
    grow = scale * np.exp(-kappa * at) * (at < 34)
    fall = scale * np.exp(-kappa * (33.0 - at)) * (at < 34)
    whole = CR * n_in
    blocks = np.stack(
        [
            np.exp(-kappa * CR),
            np.exp(-kappa * whole),
            1.0 / (1.0 - np.exp(-kappa * 2 * whole)),
            scale * np.exp(-kappa),
        ]
    ).reshape(4, n_cr, 128)
    spread = np.zeros((2 * CC, EC))
    for lane in range(EC):
        col = ((lane if lane >= 64 else lane + EC) - 128) // DEC
        if -1 <= col <= CC:
            spread[16 + col, lane] = 1
    group = np.zeros((CD, CC))
    group[np.arange(CD), np.arange(CD) // DEC] = 1
    f = np.float32
    return dict(
        forward=np2(forward), steps=steps.astype(f), grow=grow.astype(f),
        fall=fall.astype(f), blocks=blocks.astype(f), spread=spread.astype(NPB), group=group.astype(NPB),
    )


def moved(x, lane, to):
    turn = (to - lane) % x.shape[1]
    return pltpu.roll(x, turn, 1) if turn else x


def pack_columns_kernel(amp, v_in, m_in, d_in, out0, out1, a, v, m, d, sems):
    copies = []
    for side, at in enumerate((0, CD - 128)):
        span = pl.ds(at, 128)
        copies.append(pltpu.make_async_copy(amp.at[:, :, span], a.at[side], sems.at[side, 0]))
        copies.append(pltpu.make_async_copy(v_in.at[:, span], v.at[side], sems.at[side, 1]))
        copies.append(pltpu.make_async_copy(m_in.at[:, span], m.at[side], sems.at[side, 2]))
        copies.append(pltpu.make_async_copy(d_in.at[:, span], d.at[side], sems.at[side, 3]))
    for c in copies:
        c.start()
    lane = lax.broadcasted_iota(jnp.int32, (RD, 128), 1)
    for c in copies:
        c.wait()
    for side, out in enumerate((out0, out1)):
        low = 125 if side else 0
        weight = m[side].astype(F32)
        source = weight * (d[side].astype(F32) - 0.5 * (K - 1))
        end = 127 if side else 0
        total = jnp.where(lane == 54, moved(weight, end, 54), moved(source, end, 55))
        for part, value in enumerate(parts3(v[side])):
            value = value.astype(F32)
            for l in range(2):
                to = 48 + 3 * l + part
                total = jnp.where(lane == to, moved(value, (126 if side else 0) + l, to), total)
        for s in range(K):
            total = jnp.where((lane >= 3 * s) & (lane < 3 * s + 3), moved(a[side, s].astype(F32), low, 3 * s), total)
        out[...] = jnp.where(lane < 56, total, 0.0).astype(BF16)


def pack_columns(amplitudes, iterate, mask, depth):
    hbm = pl.BlockSpec(memory_space=pltpu.HBM)
    out = jax.ShapeDtypeStruct((RD, 128), BF16)
    return pl.pallas_call(
        pack_columns_kernel, in_specs=[hbm] * 4,
        out_specs=[pl.BlockSpec(memory_space=VMEM)] * 2, out_shape=[out, out],
        scratch_shapes=[
            VMEM((2, K, RD, 128), BF16), VMEM((2, RD, 128), F32), VMEM((2, RD, 128), jnp.int32),
            VMEM((2, RD, 128), jnp.int32), pltpu.SemaphoreType.DMA((2, 4)),
        ],
        compiler_params=pltpu.CompilerParams(vmem_limit_bytes=60 * 1024 * 1024),
        cost_estimate=pl.CostEstimate(flops=10**7, bytes_accessed=3 * 10**6, transcendentals=0),
        name="pack_columns",
    )(amplitudes, iterate, mask, depth)


def pack_rows_kernel(lines, left, right, mix, lanes, out0, out1):
    for side, out in enumerate((out0, out1)):
        out[:, 128:] = lines[side]
        total = jnp.zeros((MSG, 128), F32)
        for halo, which in ((left, 1), (right, 0)):
            edge = halo[RD - 16 : RD].astype(F32)[13:16] if side else halo[0:16].astype(F32)[0:3]
            for k in range(3):
                term = mix[side, k].astype(F32) * edge[k : k + 1]
                total += dot(term.astype(BF16), lanes[which])
        out[:, 0:128] = total.astype(BF16)


def pack_rows(lines, left, right, mix, lanes):
    vmem = pl.BlockSpec(memory_space=VMEM)
    out = jax.ShapeDtypeStruct((MSG, EC), BF16)
    return pl.pallas_call(
        pack_rows_kernel, in_specs=[vmem] * 5, out_specs=[vmem] * 2, out_shape=[out, out],
        compiler_params=pltpu.CompilerParams(vmem_limit_bytes=54 * 1024 * 1024),
        cost_estimate=pl.CostEstimate(flops=10**7, bytes_accessed=10**6, transcendentals=0),
        name="pack_rows",
    )(lines, left, right, mix, lanes)


def row_band(rows, window, lead):
    at = lax.broadcasted_iota(jnp.int32, (rows, window), 0) + lead
    to = lax.broadcasted_iota(jnp.int32, (rows, window), 1)
    return jnp.where(to == at + 1, 1.0, jnp.where(to == at - 1, -1.0, 0.0)).astype(BF16)


def gradient_sums(window, band, span, off, take):
    total = None
    for s in range(K):
        x = window(s)
        n = x.shape[1]
        middle = x[span]
        gc = pltpu.roll(middle, n - 1, 1).astype(F32) - pltpu.roll(middle, 1, 1).astype(F32)
        gc = gc[:, off : off + take]
        gi = dot(band, x[:, off : off + take])
        terms = (gi * gi, gi * gc, gc * gc)
        total = terms if total is None else tuple(t + u for t, u in zip(total, terms))
    return total


def edge_lines(side, a, v, m, d, rows):
    at = lax.broadcasted_iota(jnp.int32, (MSG, CD), 0)
    middle = dot(rows[side], a.reshape(K * 16, CD))
    split = [p.astype(F32) for p in parts3(v)]
    for l in range(2):
        row = 6 + l if side else l
        for part in range(3):
            middle = jnp.where(at == 48 + 3 * l + part, split[part][row : row + 1], middle)
    row = 7 if side else 0
    weight = m[row : row + 1].astype(F32)
    source = weight * (d[row : row + 1].astype(F32) - 0.5 * (K - 1))
    return jnp.where(at == 54, weight, jnp.where(at == 55, source, middle)).astype(BF16)


def inner_kernel(first, steps, edge, amp, *rest):
    if edge:
        v_in, m_in, d_in, rows_t, sii_o, sic_o, scc_o, edge_o, lines_o, a, sems, ends, v, m, d, end_sems = rest
    else:
        sii_o, sic_o, scc_o, edge_o, a, sems = rest
    base = 16 * (first - 1)
    rows = 16 * (steps + 2)
    bounds = [(0, 48), (48, 48), (96, rows - 96)]
    copies = [
        pltpu.make_async_copy(amp.at[:, pl.ds(base + r, n)], a.at[:, pl.ds(r, n)], sems.at[i])
        for i, (r, n) in enumerate(bounds)
    ]
    for c in copies:
        c.start()
    if edge:
        more = [pltpu.make_async_copy(amp.at[:, pl.ds(RD - 16, 16)], ends, end_sems.at[0])]
        for side in range(2):
            for i, (source, to) in enumerate(((v_in, v), (m_in, m), (d_in, d))):
                span = pl.ds(side * (RD - 8), 8)
                more.append(pltpu.make_async_copy(source.at[span], to.at[side], end_sems.at[1 + 3 * side + i]))
        for c in more:
            c.start()
    lane = lax.broadcasted_iota(jnp.int32, (16, 128), 1)
    band = row_band(16, 48, 16)

    def step(t, carry):
        at = pl.multiple_of(16 * t, 16)
        for part in range(2):
            lanes = slice(0, 640) if part == 0 else slice(384, CD)
            off = 0 if part == 0 else 128
            sums = gradient_sums(lambda s: a[s, pl.ds(at, 48), lanes], band, slice(16, 32), off, 512)
            for o, value in zip((sii_o, sic_o, scc_o), sums):
                o[pl.ds(at, 16), 512 * part : 512 * part + 512] = value
        return carry

    def edges(t, carry):
        at = pl.ds(pl.multiple_of(16 * t, 16), 16)
        begin = 128 * (base > 0) - base
        source = pl.ds(pl.multiple_of(16 * t + begin, 16), 16)
        for s in range(K):
            low = moved(a[s, source, 0:128].astype(F32), 0, 35)
            high = moved(a[s, source, CD - 128 : CD].astype(F32), 125, 64)
            tile = jnp.where((lane >= 35) & (lane < 38), low, jnp.where((lane >= 64) & (lane < 67), high, 0.0))
            edge_o[s, at, :] = tile.astype(BF16)
        return carry

    done = 0
    for i, (r, n) in enumerate(bounds):
        copies[i].wait()
        until = min(steps, (r + n) // 16 - 2)
        lax.fori_loop(done, until, step, 0)
        done = until
    lax.fori_loop(0, 8, edges, 0)
    if edge:
        for c in more:
            c.wait()
        lines_o[0] = edge_lines(0, a[:, 0:16, :], v[0], m[0], d[0], rows_t)
        lines_o[1] = edge_lines(1, ends[...], v[1], m[1], d[1], rows_t)


def inner_stage(first, steps, amplitudes, more=()):
    rows = 16 * (steps + 2)
    hbm, vmem = pl.BlockSpec(memory_space=pltpu.HBM), pl.BlockSpec(memory_space=VMEM)
    flat = jax.ShapeDtypeStruct((16 * steps, CD), F32)
    out_shape = [flat, flat, flat, jax.ShapeDtypeStruct((K, 128, 128), BF16)]
    scratch = [VMEM((K, rows, CD), BF16), pltpu.SemaphoreType.DMA((3,))]
    in_specs = [hbm]
    if more:
        out_shape += [jax.ShapeDtypeStruct((2, MSG, CD), BF16)]
        scratch += [
            VMEM((K, 16, CD), BF16), VMEM((2, 8, CD), F32), VMEM((2, 8, CD), jnp.int32),
            VMEM((2, 8, CD), jnp.int32), pltpu.SemaphoreType.DMA((7,)),
        ]
        in_specs += [hbm, hbm, hbm, vmem]
    return pl.pallas_call(
        functools.partial(inner_kernel, first, steps, bool(more)),
        in_specs=in_specs, out_specs=[vmem] * len(out_shape), out_shape=out_shape, scratch_shapes=scratch,
        compiler_params=pltpu.CompilerParams(vmem_limit_bytes=(57 if more else 55) * 1024 * 1024),
        cost_estimate=pl.CostEstimate(flops=10**8, bytes_accessed=6 * 10**6, transcendentals=0),
        name="inner_stage",
    )(amplitudes, *more)


def block_sums(rows, group):
    return sum(dot(part, group) for part in parts3(rows))


def tensor_kernel(
    n_in, n_cr, cuts, pos, amp, v_in, mask, depth, up, down, left, right, put, group, *rest
):
    inner_refs, rest = rest[: 4 * len(cuts)], rest[4 * len(cuts) :]
    (ta_o, tb_o, tc_o, z_o, r_o, rd_o, blocks_o, sums_o,
     tops, rim, v_ext, w_ext, s_ext, fd, fr, rowsum, sems) = rest
    inner = (slice(16, 16 + RD), slice(128, EC))
    copies = [
        pltpu.make_async_copy(amp.at[:, 0:32], tops.at[0, :, 16:48, 128:EC], sems.at[0]),
        pltpu.make_async_copy(amp.at[:, RD - 32 : RD], tops.at[1, :, 0:32, 128:EC], sems.at[1]),
        pltpu.make_async_copy(v_in, v_ext.at[16 : 16 + RD, 128:EC], sems.at[2]),
    ]
    for c in copies:
        c.start()
    weight = mask[...].astype(F32)
    w_ext[inner] = weight
    s_ext[inner] = weight * (depth[...].astype(F32) - 0.5 * (K - 1))
    lane = lax.broadcasted_iota(jnp.int32, (RD, 128), 1)
    before, after = left[...].astype(F32), right[...].astype(F32)
    here = slice(16, 16 + RD)
    value = jnp.zeros((RD, 128), F32)
    for l in range(2):
        for halo, to in ((before, 126 + l), (after, l)):
            got = sum(moved(halo, 48 + 3 * l + part, to) for part in range(3))
            value = jnp.where(lane == to, got, value)
    v_ext[here, 0:128] = value
    for o, message in ((w_ext, 54), (s_ext, 55)):
        value = jnp.where(lane == 127, moved(before, message, 127), 0.0)
        o[here, 0:128] = jnp.where(lane == 0, moved(after, message, 0), value)
    for s in range(K):
        value = jnp.where(lane < 3, moved(after, 3 * s, 0), 0.0)
        value = jnp.where(lane >= 125, moved(before, 3 * s, 125), value).astype(BF16)
        tops[0, s, 16:48, 0:128] = value[0:32]
        tops[1, s, 0:32, 0:128] = value[RD - 32 : RD]
    for c in range(2):
        span = slice(128 * c, 128 * c + 128)
        turned, turned_after, tile = before[span], after[span], lane[span]
        for s in range(K):
            value = inner_refs[4 * c + 3][s].astype(F32)
            value = jnp.where((tile >= 32) & (tile < 35), moved(turned, 3 * s, 32), value)
            value = jnp.where((tile >= 67) & (tile < 70), moved(turned_after, 3 * s, 67), value)
            rim[s, span, :] = value.astype(BF16)
    for side, halo, row in ((1, up, 0), (0, down, 16 + RD)):
        lines = dot(put[side], halo[...])
        for s in range(K):
            tops[1 - side, s, 32 - 32 * side : 48 - 32 * side, :] = lines[16 * s : 16 * s + 16].astype(BF16)
        v_ext[row : row + 16, :] = lines[256:272]
        w_ext[row : row + 16, :] = lines[272:288]
        s_ext[row : row + 16, :] = lines[288:304]
    for c in copies:
        c.wait()
    at_lane = lax.broadcasted_iota(jnp.int32, (1, EC), 1)
    col = pos[1] * CD + jnp.where(at_lane < 64, at_lane + CD, at_lane - 128)
    valid_right = ((col >= 0) & (col < n_cr * CD - 1)).astype(F32)
    row_iota = lax.broadcasted_iota(jnp.int32, (16, 1), 0)
    tile_lane = lax.broadcasted_iota(jnp.int32, (16, 128), 1)

    def left_of(x):
        return pltpu.roll(x, 1, 1)

    def right_of(x):
        return pltpu.roll(x, EC - 1, 1)

    def finish(at, sums):
        sii, sic, scc = (0.25 * x for x in sums)
        inv = 1.0 / (sii + scc + 2.0)
        row = pos[0] * RD - 16 + at + row_iota
        valid_down = ((row >= 0) & (row < n_in * RD - 1)).astype(F32)
        ta = valid_down * ((scc + 1.0) * inv)
        tb = (valid_down * valid_right) * (-sic * inv)
        tc = valid_right * ((sii + 1.0) * inv)
        value = v_ext[pl.ds(at, 24), :]
        here = value[0:16]
        dd = value[1:17] - here
        dr = right_of(here) - here
        to = pl.ds(at, 16)
        ta_o[to, :] = ta
        tb_o[to, :] = tb
        tc_o[to, :] = tc
        fd[to, :] = ta * dd + tb * dr
        fr[to, :] = tb * dd + tc * dr

    for side in range(2):
        for half in range(2):
            lead = 16 * (side + half)
            sums = gradient_sums(
                lambda s, side=side: tops[side, s], row_band(16, 48, lead), slice(lead, lead + 16), 0, EC
            )
            finish((RD if side else 0) + 16 * half, sums)

    band = row_band(16, 48, 16)
    for c, (first, steps) in enumerate(cuts):
        sii, sic, scc = inner_refs[4 * c : 4 * c + 3]

        def step(t, carry, sii=sii, sic=sic, scc=scc, first=first):
            local = pl.ds(pl.multiple_of(16 * (t - first), 16), 16)
            at = pl.multiple_of(16 * t - 16, 16)
            edge = gradient_sums(lambda s: rim[s, pl.ds(at, 48), :], band, slice(16, 32), 0, 128)
            sums = []
            for ref, e in zip((sii, sic, scc), edge):
                low, high = pltpu.roll(e, 93, 1), pltpu.roll(e, 61, 1)
                x = ref[local, :]
                sums.append(
                    jnp.concatenate(
                        [
                            jnp.where(tile_lane < 64, high, low),
                            jnp.where(tile_lane == 0, low, x[:, 0:128]),
                            x[:, 128 : CD - 128],
                            jnp.where(tile_lane == 127, high, x[:, CD - 128 :]),
                        ],
                        axis=1,
                    )
                )
            finish(pl.multiple_of(16 * t + 16, 16), sums)
            return carry

        lax.fori_loop(first, first + steps, step, 0)

    def residuals(at, n):
        before = pl.ds(pl.multiple_of(at - 8, 8), n + 8)
        here = pl.ds(at, n)
        fdw, taw = fd[before, :], ta_o[before, :]
        tc, right_flux, weight = tc_o[here, :], fr[here, :], w_ext[here, :]
        image = fdw[7 : n + 7] - fdw[8 : n + 8] + left_of(right_flux) - right_flux + weight * v_ext[here, :]
        r = s_ext[here, :] - image
        diag = taw[8 : n + 8] + 2.0 * tb_o[here, :] + tc + taw[7 : n + 7] + left_of(tc) + weight
        inv = jnp.where(diag != 0.0, 1.0 / diag, 0.0)
        z = r * inv
        z_o[here, :] = z
        return r, inv, z

    def own(e, total):
        at = pl.multiple_of(16 + 16 * e, 16)
        r, inv, z = (x[:, 128:] for x in residuals(at, 16))
        to = pl.ds(pl.multiple_of(16 * e, 16), 16)
        r_o[to, :] = r
        rd_o[to, :] = inv
        rowsum[pl.ds(2 * e, 1), :] = jnp.sum(r[0:8], axis=0, keepdims=True)
        rowsum[pl.ds(2 * e + 1, 1), :] = jnp.sum(r[8:16], axis=0, keepdims=True)
        rz = r * z
        rz = rz[0:8] + rz[8:16]
        return total + sum(rz[:, k * 128 : k * 128 + 128] for k in range(CD // 128))

    residuals(8, 8)
    residuals(16 + RD, 8)
    sums_o[...] = lax.fori_loop(0, RD // 16, own, jnp.zeros((8, 128), F32))
    sums = block_sums(rowsum[...], group[...])
    for j in range(n_cr):
        blocks_o[j] = sums


def tensor_stage(n_in, n_cr, cuts, pos, amp, v, mask, depth, up, down, left, right, put, group, sums):
    vmem = pl.BlockSpec(memory_space=VMEM)
    hbm = pl.BlockSpec(memory_space=pltpu.HBM)
    ext = jax.ShapeDtypeStruct((ER, EC), F32)
    flat = jax.ShapeDtypeStruct((RD, CD), F32)
    return pl.pallas_call(
        functools.partial(tensor_kernel, n_in, n_cr, cuts),
        in_specs=[pl.BlockSpec(memory_space=pltpu.SMEM), hbm, hbm] + [vmem] * (8 + len(sums)),
        out_specs=[vmem] * 8,
        out_shape=[
            ext, ext, ext, ext, flat, flat,
            jax.ShapeDtypeStruct((n_cr, CR, CC), F32),
            jax.ShapeDtypeStruct((8, 128), F32),
        ],
        scratch_shapes=[
            VMEM((2, K, 48, EC), BF16), VMEM((K, RD, 128), BF16), VMEM((ER + 8, EC), F32), VMEM((ER, EC), F32),
            VMEM((ER, EC), F32), VMEM((ER, EC), F32), VMEM((ER, EC), F32), VMEM((CR, CD), F32),
            pltpu.SemaphoreType.DMA((3,)),
        ],
        compiler_params=pltpu.CompilerParams(vmem_limit_bytes=36 * 1024 * 1024),
        cost_estimate=pl.CostEstimate(flops=10**8, bytes_accessed=2 * 10**7, transcendentals=0),
        name="tensor_stage",
    )(pos, amp, v, mask, depth, up, down, left, right, put, group, *sums)


def moments_kernel(n_in, n_cr, extra, blocks, fwd_hi, fwd_lo, steps, pay_o, own_o):
    x = jnp.concatenate([blocks[j, :CR] for j in range(n_cr)], axis=1)
    hi, lo = parts2(x)
    span = slice(16, 16 + x.shape[1])
    both = dot(jnp.concatenate([hi, lo], axis=0), fwd_hi[span, :])
    x = both[:CR] + both[CR:] + dot(hi, fwd_lo[span, :])
    width = x.shape[1]
    forth, back = x, x
    for i in range(5):
        d = 1 << i
        zero = jnp.zeros((d, width), F32)
        decay = steps[i : i + 1]
        forth = forth + decay * jnp.concatenate([zero, forth[:-d]], axis=0)
        back = back + decay * jnp.concatenate([back[d:], zero], axis=0)
    decay, scale = steps[0:1], steps[5:6]
    zero = jnp.zeros((1, width), F32)
    inside = forth + decay * jnp.concatenate([back[1:], zero], axis=0)
    inside = scale * inside
    own_o[...] = jnp.concatenate(
        [scale * decay * back[0:1], inside, scale * decay * forth[CR - 1 :], jnp.zeros((6, width), F32)],
        axis=0,
    )
    f = jnp.concatenate([forth[CR - 1 :, 128 * k : 128 * k + 128] for k in range(n_cr)], axis=0)
    b = jnp.concatenate([back[0:1, 128 * k : 128 * k + 128] for k in range(n_cr)], axis=0)
    for i in range(n_in):
        pay_o[i, 0:n_cr] = f
        pay_o[i, n_cr : 2 * n_cr] = b
    if extra:
        sums = sum(blocks[j, CR : CR + 8] for j in range(n_cr))
        energy = jnp.sum(x * inside, axis=0, keepdims=True)
        energy = sum(energy[:, 128 * k : 128 * k + 128] for k in range(n_cr))
        at = lax.broadcasted_iota(jnp.int32, (8, 128), 0)
        sums = jnp.where(at == 3, energy, sums)
        for i in range(n_in):
            pay_o[i, 2 * n_cr : 2 * n_cr + 8] = sums


def moments_stage(n_in, n_cr, extra, blocks, fwd_hi, fwd_lo, steps):
    vmem = pl.BlockSpec(memory_space=VMEM)
    return pl.pallas_call(
        functools.partial(moments_kernel, n_in, n_cr, extra),
        in_specs=[vmem] * 4, out_specs=[vmem] * 2,
        out_shape=[
            jax.ShapeDtypeStruct((n_in, 2 * n_cr + 8 * extra, 128), F32),
            jax.ShapeDtypeStruct((40, CC * n_cr), F32),
        ],
        compiler_params=pltpu.CompilerParams(vmem_limit_bytes=32 * 1024 * 1024),
        cost_estimate=pl.CostEstimate(flops=2 * 10**8, bytes_accessed=5 * 10**6, transcendentals=0),
        name="moments_stage",
    )(blocks, fwd_hi, fwd_lo, steps)


def coarse_values(n_in, n_cr, pos, moments, own, grow, fall, blocks, fwd_hi, fwd_lo, spread):
    mine = pos[0]
    r32, whole, series, link = (blocks[i] for i in range(4))
    f = [moments[i, 0:n_cr] for i in range(n_in)]
    b = [moments[i, n_cr : 2 * n_cr] for i in range(n_in)]
    hf, hb = f[0], b[n_in - 1]
    for i in range(1, n_in):
        hf = r32 * hf + f[i]
        hb = r32 * hb + b[n_in - 1 - i]
    above = (hb + whole * hf) * series
    below = (hf + whole * hb) * series
    mine_above, mine_below = jnp.zeros_like(above), jnp.zeros_like(below)
    energy = jnp.zeros_like(above)
    for i in range(n_in):
        k = n_in - 1 - i
        mine_above = jnp.where(mine == i, above, mine_above)
        mine_below = jnp.where(mine == k, below, mine_below)
        energy += above * b[i] + below * f[k]
        above = r32 * above + f[i]
        below = r32 * below + b[k]
    energy = energy * link
    a_row = jnp.concatenate([mine_above[k : k + 1] for k in range(n_cr)], axis=1)
    b_row = jnp.concatenate([mine_below[k : k + 1] for k in range(n_cr)], axis=1)
    u = own[...] + a_row * grow[...] + b_row * fall[...]
    hi, lo = parts2(u)
    span = pl.ds(pl.multiple_of(pos[1] * CC, CC), 2 * CC)
    turned = (((1,), (1,)), ((), ()))
    both = lax.dot_general(jnp.concatenate([hi, lo], axis=0), fwd_hi[span, :], turned, preferred_element_type=F32)
    values = both[:40] + both[40:] + lax.dot_general(hi, fwd_lo[span, :], turned, preferred_element_type=F32)
    three = dot(jnp.concatenate(parts3(values), axis=0), spread[...])
    return values, three[:40] + three[40:80] + three[80:], energy


def image_kernel(
    n_in, n_cr, pos, moments, own, grow, fall, blocks, fwd_hi, fwd_lo, spread, group,
    ta, tb, tc, z, rd, mask, first_blocks, first_sums,
    p_o, q_o, blocks_o, rowsum, cs,
):
    values, spread_rows, _ = coarse_values(
        n_in, n_cr, pos, moments, own, grow, fall, blocks, fwd_hi, fwd_lo, spread
    )
    cs[...] = spread_rows

    def field(strip):
        at = pl.ds(pl.multiple_of(8 + 8 * strip, 8), 8)
        return z[at, :] + cs[pl.ds(strip, 1), :]

    def fluxes(at, n, value):
        here = value[0:n]
        dd = value[1 : n + 1] - here
        dr = pltpu.roll(here, EC - 1, 1) - here
        at = pl.ds(at, n)
        b = tb[at, :]
        return ta[at, :] * dd + b * dr, b * dd + tc[at, :] * dr

    def images(e, carry):
        pq, qq, strip, above = carry
        following = [field(2 * e + 2), field(2 * e + 3)]
        value = jnp.concatenate([strip] + following, axis=0)
        down, side = fluxes(pl.multiple_of(16 + 16 * e, 16), 16, value)
        flux = jnp.concatenate([above[7:8], down[0:15]], axis=0) - down + pltpu.roll(side, 1, 1) - side
        to = pl.ds(pl.multiple_of(16 * e, 16), 16)
        p = value[0:16, 128:]
        q = flux[:, 128:] + mask[to, :].astype(F32) * p
        p_o[to, :] = p
        q_o[to, :] = q
        rowsum[pl.ds(2 * e, 1), :] = jnp.sum(q[0:8], axis=0, keepdims=True)
        rowsum[pl.ds(2 * e + 1, 1), :] = jnp.sum(q[8:16], axis=0, keepdims=True)
        return pq + folded(p * q), qq + folded(q * q * rd[to, :]), following[1], down[8:16]

    def folded(x):
        x = x[0:8] + x[8:16]
        return sum(x[:, k * 128 : k * 128 + 128] for k in range(CD // 128))

    strip = field(1)
    above, _ = fluxes(8, 8, jnp.concatenate([field(0), strip], axis=0))
    zero = jnp.zeros((8, 128), F32)
    pq, qq, _, _ = lax.fori_loop(0, RD // 16, images, (zero, zero, strip, above))

    def lanes(x):
        return jnp.sum(x, axis=0, keepdims=True)

    rp = jnp.sum(first_sums[...], axis=0, keepdims=True)
    rp += jnp.sum(first_blocks[0] * pltpu.roll(values, 2 * CC - 16, 1)[1 : CR + 1, :CC], axis=0, keepdims=True)
    tail = jnp.concatenate([rp, lanes(pq), lanes(qq), jnp.zeros((5, 128), F32)], axis=0)
    sums = block_sums(rowsum[...], group[...])
    for j in range(n_cr):
        blocks_o[j, 0:CR] = sums
        blocks_o[j, CR : CR + 8] = tail


def final_kernel(
    n_in, n_cr, pos, moments, own, grow, fall, blocks, fwd_hi, fwd_lo, spread,
    p_in, q_in, r_in, rd, v_in, v_o, r_o, d_o, cs,
):
    _, spread_rows, energy = coarse_values(
        n_in, n_cr, pos, moments, own, grow, fall, blocks, fwd_hi, fwd_lo, spread
    )
    cs[...] = spread_rows
    sums = sum(moments[i, 2 * n_cr : 2 * n_cr + 8] for i in range(n_in))
    old = jnp.sum(sums[0:1], axis=1, keepdims=True)
    curvature = jnp.sum(sums[1:2], axis=1, keepdims=True)
    energy = jnp.sum(jnp.sum(energy, axis=0, keepdims=True), axis=1, keepdims=True)
    image = jnp.sum(sums[2:3] + sums[3:4], axis=1, keepdims=True) + energy
    step = old / curvature
    ratio = (step * step * image - old) / old
    more = 1.0 + ratio

    def body(e, carry):
        at = pl.ds(pl.multiple_of(16 * e, 16), 16)
        p, q = p_in[at, :], q_in[at, :]
        coarse = [jnp.broadcast_to(cs[pl.ds(2 * e + k, 1), 128:], (8, CD)) for k in (1, 2)]
        coarse = jnp.concatenate(coarse, axis=0)
        v_o[at, :] = v_in[at, :] + step * p
        r_o[at, :] = r_in[at, :] - step * q
        d_o[at, :] = more * p - step * (q * rd[at, :] + coarse)
        return carry

    lax.fori_loop(0, RD // 16, body, 0)


def coarse_call(kernel, n_in, n_cr, name, out_shape, scratch, pos, moments, own, tables, rest, group=None):
    vmem = pl.BlockSpec(memory_space=VMEM)
    args = [moments, own, tables["grow"], tables["fall"], tables["blocks"], *tables["forward"], tables["spread"]]
    args += ([group] if group is not None else []) + list(rest)
    return pl.pallas_call(
        functools.partial(kernel, n_in, n_cr),
        in_specs=[pl.BlockSpec(memory_space=pltpu.SMEM)] + [vmem] * len(args),
        out_specs=[vmem] * len(out_shape), out_shape=out_shape, scratch_shapes=scratch,
        compiler_params=pltpu.CompilerParams(vmem_limit_bytes=32 * 1024 * 1024),
        cost_estimate=pl.CostEstimate(flops=10**8, bytes_accessed=10**7, transcendentals=0),
        name=name,
    )(pos, *args)


def neighbours(value_low, value_high, axis, count):
    ahead = [(i, i + 1) for i in range(count - 1)]
    behind = [(j, i) for i, j in ahead]
    return lax.ppermute(value_high, axis, ahead), lax.ppermute(value_low, axis, behind)


def per_device(n_in, n_cr, amplitudes, mask, depth, iterate):
    rows, put, mix, lanes = (jnp.asarray(t) for t in line_tables())
    tables = coarse_tables(n_in, n_cr)
    pos = jnp.stack([lax.axis_index("inline"), lax.axis_index("crosslin")]).astype(jnp.int32)
    col_first, col_last = pack_columns(amplitudes, iterate, mask, depth)
    left, right = neighbours(col_first, col_last, "crosslin", n_cr)
    cuts = ((1, 7), (8, 7))
    *inner, lines = inner_stage(*cuts[0], amplitudes, (iterate, mask, depth, rows))
    (left, right), lines = lax.optimization_barrier(((left, right), lines))
    row_first, row_last = pack_rows(lines, left, right, mix, lanes)
    up, down = neighbours(row_first, row_last, "inline", n_in)
    inner += inner_stage(*cuts[1], amplitudes)
    group = jnp.asarray(tables["group"])
    ta, tb, tc, z, r, rd, blocks, sums = tensor_stage(
        n_in, n_cr, cuts, pos, amplitudes, iterate, mask, depth, up, down, left, right, put, group, inner
    )

    def moments_of(payload, extra):
        gathered = lax.all_to_all(payload, "crosslin", 0, 0, tiled=True)
        pay, own = moments_stage(n_in, n_cr, extra, gathered, *tables["forward"], tables["steps"])
        return lax.all_to_all(pay, "inline", 0, 0, tiled=True), own

    flat = jax.ShapeDtypeStruct((RD, CD), F32)
    cs = VMEM((40, EC), F32)
    moments, own = moments_of(blocks, False)
    p, q, payload = coarse_call(
        image_kernel, n_in, n_cr, "image_stage",
        [flat, flat, jax.ShapeDtypeStruct((n_cr, CR + 8, CC), F32)],
        [VMEM((CR, CD), F32), cs],
        pos, moments, own, tables, [ta, tb, tc, z, rd, mask, blocks, sums], group,
    )
    moments, own = moments_of(payload, True)
    return tuple(
        coarse_call(
            final_kernel, n_in, n_cr, "final_stage", [flat, flat, flat], [cs],
            pos, moments, own, tables, [p, q, r, rd, iterate],
        )
    )


def solution(mesh):
    n_in, n_cr = mesh.shape["inline"], mesh.shape["crosslin"]
    flat = P("inline", "crosslin")
    return jax.shard_map(
        functools.partial(per_device, n_in, n_cr), mesh=mesh,
        in_specs=(P(None, "inline", "crosslin"), flat, flat, flat),
        out_specs=(flat, flat, flat), check_vma=False,
    )
```

```python
import functools

import jax
import jax.numpy as jnp
import ml_dtypes
import numpy as np
from jax import lax
from jax.experimental import pallas as pl
from jax.experimental.pallas import tpu as pltpu
from jax.sharding import PartitionSpec as P

K = 16
DEC = 8
CI = 32
COUPLING = 4.0
F32 = jnp.float32
BF16 = jnp.bfloat16
NPB = ml_dtypes.bfloat16
VMEM = pltpu.VMEM

RD = 256
CD = 1024
ER = RD + 32
EC = CD + 128
CR = RD // DEC
CC = CD // DEC
MSG = 64


def in_hbm(x):
    return pltpu.with_memory_space_constraint(x, pltpu.HBM)


def dot(a, b):
    return jnp.dot(a, b, preferred_element_type=F32)


def parts2(x):
    hi = x.astype(BF16)
    return hi, (x - hi.astype(F32)).astype(BF16)


def parts3(x):
    hi = x.astype(BF16)
    rest = x - hi.astype(F32)
    mid = rest.astype(BF16)
    return hi, mid, (rest - mid.astype(F32)).astype(BF16)


def np2(x):
    hi = x.astype(np.float32).astype(NPB)
    return hi, (x - hi.astype(np.float64)).astype(np.float32).astype(NPB)


def line_tables():
    rows = np.zeros((2, MSG, 256), np.float32)
    put = np.zeros((2, 304, MSG), np.float32)
    for s in range(K):
        for k in range(3):
            rows[0, 3 * s + k, 16 * s + k] = 1
            rows[1, 3 * s + k, 16 * s + 13 + k] = 1
    for side in range(2):
        put[side, :256] = rows[side].T
        for l in range(2):
            for part in range(3):
                put[side, 256 + (14 + l if side else l), 48 + 3 * l + part] = 1
        put[side, 272 + (15 if side else 0), 54] = 1
        put[side, 288 + (15 if side else 0), 55] = 1
    mix = np.zeros((2, 3, MSG, 128), np.float32)
    for k in range(3):
        for s in range(K):
            mix[:, k, 3 * s + k, 3 * s : 3 * s + 3] = 1
    for l in range(2):
        for part in range(3):
            for other in range(2):
                mix[0, l, 48 + 3 * l + part, 48 + 3 * other + part] = 1
                mix[1, l + 1, 48 + 3 * l + part, 48 + 3 * other + part] = 1
    for o in (54, 55):
        mix[0, 0, o, o] = 1
        mix[1, 2, o, o] = 1
    lanes = np.zeros((2, 128, 128), np.float32)
    for s in range(K):
        for k in range(3):
            lanes[0, 3 * s + k, k] = 1
            lanes[1, 3 * s + k, 125 + k] = 1
    for l in range(2):
        for part in range(3):
            lanes[0, 48 + 3 * l + part, l] = 1
            lanes[1, 48 + 3 * l + part, 126 + l] = 1
    for o in (54, 55):
        lanes[0, o, 0] = 1
        lanes[1, o, 127] = 1
    return tuple(t.astype(NPB) for t in (rows, put, mix, lanes))


def coarse_tables(n_in, n_cr):
    n = CC * n_cr
    freq = np.arange(n, dtype=np.float64)
    norm = np.where(freq == 0, np.sqrt(1.0 / n), np.sqrt(2.0 / n))

    def cosines(cols):
        phase = (freq[:, None] * (2 * cols[None, :] + 1)) % (4 * n)
        return norm[:, None] * np.cos(np.pi * phase / (2 * n))

    lead = np.arange(n + CC, dtype=np.float64) - 16
    forward = cosines(lead).T * (lead[:, None] >= -1) * (lead[:, None] <= n)
    half = (2.0 - 2.0 * np.cos(np.pi * freq / n) + 1.0 / (CI * CI)) / 2.0
    kappa = np.log1p(half + np.sqrt(half * (half + 2.0)))
    scale = 1.0 / (COUPLING * 2.0 * np.sinh(kappa))
    steps = np.stack([np.exp(-kappa * d) for d in (1, 2, 4, 8, 16)] + [scale] + [scale * 0] * 2)
    at = np.arange(40)[:, None]
    grow = scale * np.exp(-kappa * at) * (at < 34)
    fall = scale * np.exp(-kappa * (33.0 - at)) * (at < 34)
    whole = CR * n_in
    blocks = np.stack(
        [
            np.exp(-kappa * CR),
            np.exp(-kappa * whole),
            1.0 / (1.0 - np.exp(-kappa * 2 * whole)),
            scale * np.exp(-kappa),
        ]
    ).reshape(4, n_cr, 128)
    spread = np.zeros((2 * CC, EC))
    for lane in range(EC):
        col = ((lane if lane >= 64 else lane + EC) - 128) // DEC
        if -1 <= col <= CC:
            spread[16 + col, lane] = 1
    group = np.zeros((CD, CC))
    group[np.arange(CD), np.arange(CD) // DEC] = 1
    f = np.float32
    return dict(
        forward=np2(forward), steps=steps.astype(f), grow=grow.astype(f),
        fall=fall.astype(f), blocks=blocks.astype(f), spread=spread.astype(NPB), group=group.astype(NPB),
    )


def moved(x, lane, to):
    turn = (to - lane) % x.shape[1]
    return pltpu.roll(x, turn, 1) if turn else x


def pack_columns_kernel(amp, v_in, m_in, d_in, out0, out1, a, v, m, d, sems):
    copies = []
    for side, at in enumerate((0, CD - 128)):
        span = pl.ds(at, 128)
        copies.append(pltpu.make_async_copy(amp.at[:, :, span], a.at[side], sems.at[side, 0]))
        copies.append(pltpu.make_async_copy(v_in.at[:, span], v.at[side], sems.at[side, 1]))
        copies.append(pltpu.make_async_copy(m_in.at[:, span], m.at[side], sems.at[side, 2]))
        copies.append(pltpu.make_async_copy(d_in.at[:, span], d.at[side], sems.at[side, 3]))
    for c in copies:
        c.start()
    lane = lax.broadcasted_iota(jnp.int32, (RD, 128), 1)
    for c in copies:
        c.wait()
    for side, out in enumerate((out0, out1)):
        low = 125 if side else 0
        weight = m[side].astype(F32)
        source = weight * (d[side].astype(F32) - 0.5 * (K - 1))
        end = 127 if side else 0
        total = jnp.where(lane == 54, moved(weight, end, 54), moved(source, end, 55))
        for part, value in enumerate(parts3(v[side])):
            value = value.astype(F32)
            for l in range(2):
                to = 48 + 3 * l + part
                total = jnp.where(lane == to, moved(value, (126 if side else 0) + l, to), total)
        for s in range(K):
            total = jnp.where((lane >= 3 * s) & (lane < 3 * s + 3), moved(a[side, s].astype(F32), low, 3 * s), total)
        out[...] = jnp.where(lane < 56, total, 0.0).astype(BF16)


def pack_columns(amplitudes, iterate, mask, depth):
    hbm = pl.BlockSpec(memory_space=pltpu.HBM)
    out = jax.ShapeDtypeStruct((RD, 128), BF16)
    return pl.pallas_call(
        pack_columns_kernel, in_specs=[hbm] * 4,
        out_specs=[pl.BlockSpec(memory_space=VMEM)] * 2, out_shape=[out, out],
        scratch_shapes=[
            VMEM((2, K, RD, 128), BF16), VMEM((2, RD, 128), F32), VMEM((2, RD, 128), jnp.int32),
            VMEM((2, RD, 128), jnp.int32), pltpu.SemaphoreType.DMA((2, 4)),
        ],
        compiler_params=pltpu.CompilerParams(vmem_limit_bytes=32 * 1024 * 1024),
        cost_estimate=pl.CostEstimate(flops=10**7, bytes_accessed=3 * 10**6, transcendentals=0),
        name="pack_columns",
    )(*(in_hbm(x) for x in (amplitudes, iterate, mask, depth)))


def pack_rows_kernel(lines, left, right, mix, lanes, out0, out1):
    for side, out in enumerate((out0, out1)):
        out[:, 128:] = lines[side]
        total = jnp.zeros((MSG, 128), F32)
        for halo, which in ((left, 1), (right, 0)):
            edge = halo[RD - 16 : RD].astype(F32)[13:16] if side else halo[0:16].astype(F32)[0:3]
            for k in range(3):
                term = mix[side, k].astype(F32) * edge[k : k + 1]
                total += dot(term.astype(BF16), lanes[which])
        out[:, 0:128] = total.astype(BF16)


def pack_rows(lines, left, right, mix, lanes):
    vmem = pl.BlockSpec(memory_space=VMEM)
    out = jax.ShapeDtypeStruct((MSG, EC), BF16)
    return pl.pallas_call(
        pack_rows_kernel, in_specs=[vmem] * 5, out_specs=[vmem] * 2, out_shape=[out, out],
        compiler_params=pltpu.CompilerParams(vmem_limit_bytes=32 * 1024 * 1024),
        cost_estimate=pl.CostEstimate(flops=10**7, bytes_accessed=10**6, transcendentals=0),
        name="pack_rows",
    )(lines, left, right, mix, lanes)


def row_band(rows, window, lead):
    at = lax.broadcasted_iota(jnp.int32, (rows, window), 0) + lead
    to = lax.broadcasted_iota(jnp.int32, (rows, window), 1)
    return jnp.where(to == at + 1, 1.0, jnp.where(to == at - 1, -1.0, 0.0)).astype(BF16)


def gradient_sums(window, band, span, off, take):
    total = None
    for s in range(K):
        x = window(s)
        n = x.shape[1]
        middle = x[span]
        gc = pltpu.roll(middle, n - 1, 1).astype(F32) - pltpu.roll(middle, 1, 1).astype(F32)
        gc = gc[:, off : off + take]
        gi = dot(band, x[:, off : off + take])
        terms = (gi * gi, gi * gc, gc * gc)
        total = terms if total is None else tuple(t + u for t, u in zip(total, terms))
    return total


def edge_lines(side, a, v, m, d, rows):
    at = lax.broadcasted_iota(jnp.int32, (MSG, CD), 0)
    middle = dot(rows[side], a.reshape(K * 16, CD))
    split = [p.astype(F32) for p in parts3(v)]
    for l in range(2):
        row = 6 + l if side else l
        for part in range(3):
            middle = jnp.where(at == 48 + 3 * l + part, split[part][row : row + 1], middle)
    row = 7 if side else 0
    weight = m[row : row + 1].astype(F32)
    source = weight * (d[row : row + 1].astype(F32) - 0.5 * (K - 1))
    return jnp.where(at == 54, weight, jnp.where(at == 55, source, middle)).astype(BF16)


def inner_kernel(first, steps, edge, amp, *rest):
    if edge:
        v_in, m_in, d_in, rows_t, sii_o, sic_o, scc_o, edge_o, lines_o, a, sems, ends, v, m, d, end_sems = rest
    else:
        sii_o, sic_o, scc_o, edge_o, a, sems = rest
    base = 16 * (first - 1)
    rows = 16 * (steps + 2)
    bounds = [(0, 48), (48, 48), (96, rows - 96)]
    copies = [
        pltpu.make_async_copy(amp.at[:, pl.ds(base + r, n)], a.at[:, pl.ds(r, n)], sems.at[i])
        for i, (r, n) in enumerate(bounds)
    ]
    for c in copies:
        c.start()
    if edge:
        more = [pltpu.make_async_copy(amp.at[:, pl.ds(RD - 16, 16)], ends, end_sems.at[0])]
        for side in range(2):
            for i, (source, to) in enumerate(((v_in, v), (m_in, m), (d_in, d))):
                span = pl.ds(side * (RD - 8), 8)
                more.append(pltpu.make_async_copy(source.at[span], to.at[side], end_sems.at[1 + 3 * side + i]))
        for c in more:
            c.start()
    lane = lax.broadcasted_iota(jnp.int32, (16, 128), 1)
    band = row_band(16, 48, 16)

    def step(t, carry):
        at = pl.multiple_of(16 * t, 16)
        for part in range(2):
            lanes = slice(0, 640) if part == 0 else slice(384, CD)
            off = 0 if part == 0 else 128
            sums = gradient_sums(lambda s: a[s, pl.ds(at, 48), lanes], band, slice(16, 32), off, 512)
            for o, value in zip((sii_o, sic_o, scc_o), sums):
                o[pl.ds(at, 16), 512 * part : 512 * part + 512] = value
        return carry

    def edges(t, carry):
        at = pl.ds(pl.multiple_of(16 * t, 16), 16)
        begin = 128 * (base > 0) - base
        source = pl.ds(pl.multiple_of(16 * t + begin, 16), 16)
        for s in range(K):
            low = moved(a[s, source, 0:128].astype(F32), 0, 35)
            high = moved(a[s, source, CD - 128 : CD].astype(F32), 125, 64)
            tile = jnp.where((lane >= 35) & (lane < 38), low, jnp.where((lane >= 64) & (lane < 67), high, 0.0))
            edge_o[s, at, :] = tile.astype(BF16)
        return carry

    done = 0
    for i, (r, n) in enumerate(bounds):
        copies[i].wait()
        until = min(steps, (r + n) // 16 - 2)
        lax.fori_loop(done, until, step, 0)
        done = until
    lax.fori_loop(0, 8, edges, 0)
    if edge:
        for c in more:
            c.wait()
        lines_o[0] = edge_lines(0, a[:, 0:16, :], v[0], m[0], d[0], rows_t)
        lines_o[1] = edge_lines(1, ends[...], v[1], m[1], d[1], rows_t)


def inner_stage(first, steps, amplitudes, more=()):
    rows = 16 * (steps + 2)
    hbm, vmem = pl.BlockSpec(memory_space=pltpu.HBM), pl.BlockSpec(memory_space=VMEM)
    flat = jax.ShapeDtypeStruct((16 * steps, CD), F32)
    out_shape = [flat, flat, flat, jax.ShapeDtypeStruct((K, 128, 128), BF16)]
    scratch = [VMEM((K, rows, CD), BF16), pltpu.SemaphoreType.DMA((3,))]
    in_specs = [hbm]
    if more:
        out_shape += [jax.ShapeDtypeStruct((2, MSG, CD), BF16)]
        scratch += [
            VMEM((K, 16, CD), BF16), VMEM((2, 8, CD), F32), VMEM((2, 8, CD), jnp.int32),
            VMEM((2, 8, CD), jnp.int32), pltpu.SemaphoreType.DMA((7,)),
        ]
        in_specs += [hbm, hbm, hbm, vmem]
    return pl.pallas_call(
        functools.partial(inner_kernel, first, steps, bool(more)),
        in_specs=in_specs, out_specs=[vmem] * len(out_shape), out_shape=out_shape, scratch_shapes=scratch,
        compiler_params=pltpu.CompilerParams(vmem_limit_bytes=32 * 1024 * 1024),
        cost_estimate=pl.CostEstimate(flops=10**8, bytes_accessed=6 * 10**6, transcendentals=0),
        name="inner_stage",
    )(in_hbm(amplitudes), *(in_hbm(x) for x in more[:3]), *more[3:])


def block_sums(rows, group):
    return sum(dot(part, group) for part in parts3(rows))


def tensor_kernel(
    n_in, n_cr, cuts, pos, amp, v_in, mask, depth, up, down, left, right, put, group, *rest
):
    inner_refs, rest = rest[: 4 * len(cuts)], rest[4 * len(cuts) :]
    (ta_o, tb_o, tc_o, z_o, r_o, rd_o, blocks_o, sums_o,
     tops, rim, v_ext, w_ext, s_ext, fd, fr, rowsum, sems) = rest
    inner = (slice(16, 16 + RD), slice(128, EC))
    copies = [
        pltpu.make_async_copy(amp.at[:, 0:32], tops.at[0, :, 16:48, 128:EC], sems.at[0]),
        pltpu.make_async_copy(amp.at[:, RD - 32 : RD], tops.at[1, :, 0:32, 128:EC], sems.at[1]),
        pltpu.make_async_copy(v_in, v_ext.at[16 : 16 + RD, 128:EC], sems.at[2]),
    ]
    for c in copies:
        c.start()
    weight = mask[...].astype(F32)
    w_ext[inner] = weight
    s_ext[inner] = weight * (depth[...].astype(F32) - 0.5 * (K - 1))
    lane = lax.broadcasted_iota(jnp.int32, (RD, 128), 1)
    before, after = left[...].astype(F32), right[...].astype(F32)
    here = slice(16, 16 + RD)
    value = jnp.zeros((RD, 128), F32)
    for l in range(2):
        for halo, to in ((before, 126 + l), (after, l)):
            got = sum(moved(halo, 48 + 3 * l + part, to) for part in range(3))
            value = jnp.where(lane == to, got, value)
    v_ext[here, 0:128] = value
    for o, message in ((w_ext, 54), (s_ext, 55)):
        value = jnp.where(lane == 127, moved(before, message, 127), 0.0)
        o[here, 0:128] = jnp.where(lane == 0, moved(after, message, 0), value)
    for s in range(K):
        value = jnp.where(lane < 3, moved(after, 3 * s, 0), 0.0)
        value = jnp.where(lane >= 125, moved(before, 3 * s, 125), value).astype(BF16)
        tops[0, s, 16:48, 0:128] = value[0:32]
        tops[1, s, 0:32, 0:128] = value[RD - 32 : RD]
    for c in range(2):
        span = slice(128 * c, 128 * c + 128)
        turned, turned_after, tile = before[span], after[span], lane[span]
        for s in range(K):
            value = inner_refs[4 * c + 3][s].astype(F32)
            value = jnp.where((tile >= 32) & (tile < 35), moved(turned, 3 * s, 32), value)
            value = jnp.where((tile >= 67) & (tile < 70), moved(turned_after, 3 * s, 67), value)
            rim[s, span, :] = value.astype(BF16)
    for side, halo, row in ((1, up, 0), (0, down, 16 + RD)):
        lines = dot(put[side], halo[...])
        for s in range(K):
            tops[1 - side, s, 32 - 32 * side : 48 - 32 * side, :] = lines[16 * s : 16 * s + 16].astype(BF16)
        v_ext[row : row + 16, :] = lines[256:272]
        w_ext[row : row + 16, :] = lines[272:288]
        s_ext[row : row + 16, :] = lines[288:304]
    for c in copies:
        c.wait()
    at_lane = lax.broadcasted_iota(jnp.int32, (1, EC), 1)
    col = pos[1] * CD + jnp.where(at_lane < 64, at_lane + CD, at_lane - 128)
    valid_right = ((col >= 0) & (col < n_cr * CD - 1)).astype(F32)
    row_iota = lax.broadcasted_iota(jnp.int32, (16, 1), 0)
    tile_lane = lax.broadcasted_iota(jnp.int32, (16, 128), 1)

    def left_of(x):
        return pltpu.roll(x, 1, 1)

    def right_of(x):
        return pltpu.roll(x, EC - 1, 1)

    def finish(at, sums):
        sii, sic, scc = (0.25 * x for x in sums)
        inv = 1.0 / (sii + scc + 2.0)
        row = pos[0] * RD - 16 + at + row_iota
        valid_down = ((row >= 0) & (row < n_in * RD - 1)).astype(F32)
        ta = valid_down * ((scc + 1.0) * inv)
        tb = (valid_down * valid_right) * (-sic * inv)
        tc = valid_right * ((sii + 1.0) * inv)
        value = v_ext[pl.ds(at, 24), :]
        here = value[0:16]
        dd = value[1:17] - here
        dr = right_of(here) - here
        to = pl.ds(at, 16)
        ta_o[to, :] = ta
        tb_o[to, :] = tb
        tc_o[to, :] = tc
        fd[to, :] = ta * dd + tb * dr
        fr[to, :] = tb * dd + tc * dr

    for side in range(2):
        for half in range(2):
            lead = 16 * (side + half)
            sums = gradient_sums(
                lambda s, side=side: tops[side, s], row_band(16, 48, lead), slice(lead, lead + 16), 0, EC
            )
            finish((RD if side else 0) + 16 * half, sums)

    band = row_band(16, 48, 16)
    for c, (first, steps) in enumerate(cuts):
        sii, sic, scc = inner_refs[4 * c : 4 * c + 3]

        def step(t, carry, sii=sii, sic=sic, scc=scc, first=first):
            local = pl.ds(pl.multiple_of(16 * (t - first), 16), 16)
            at = pl.multiple_of(16 * t - 16, 16)
            edge = gradient_sums(lambda s: rim[s, pl.ds(at, 48), :], band, slice(16, 32), 0, 128)
            sums = []
            for ref, e in zip((sii, sic, scc), edge):
                low, high = pltpu.roll(e, 93, 1), pltpu.roll(e, 61, 1)
                x = ref[local, :]
                sums.append(
                    jnp.concatenate(
                        [
                            jnp.where(tile_lane < 64, high, low),
                            jnp.where(tile_lane == 0, low, x[:, 0:128]),
                            x[:, 128 : CD - 128],
                            jnp.where(tile_lane == 127, high, x[:, CD - 128 :]),
                        ],
                        axis=1,
                    )
                )
            finish(pl.multiple_of(16 * t + 16, 16), sums)
            return carry

        lax.fori_loop(first, first + steps, step, 0)

    def residuals(at, n):
        before = pl.ds(pl.multiple_of(at - 8, 8), n + 8)
        here = pl.ds(at, n)
        fdw, taw = fd[before, :], ta_o[before, :]
        tc, right_flux, weight = tc_o[here, :], fr[here, :], w_ext[here, :]
        image = fdw[7 : n + 7] - fdw[8 : n + 8] + left_of(right_flux) - right_flux + weight * v_ext[here, :]
        r = s_ext[here, :] - image
        diag = taw[8 : n + 8] + 2.0 * tb_o[here, :] + tc + taw[7 : n + 7] + left_of(tc) + weight
        inv = jnp.where(diag != 0.0, 1.0 / diag, 0.0)
        z = r * inv
        z_o[here, :] = z
        return r, inv, z

    def own(e, total):
        at = pl.multiple_of(16 + 16 * e, 16)
        r, inv, z = (x[:, 128:] for x in residuals(at, 16))
        to = pl.ds(pl.multiple_of(16 * e, 16), 16)
        r_o[to, :] = r
        rd_o[to, :] = inv
        rowsum[pl.ds(2 * e, 1), :] = jnp.sum(r[0:8], axis=0, keepdims=True)
        rowsum[pl.ds(2 * e + 1, 1), :] = jnp.sum(r[8:16], axis=0, keepdims=True)
        rz = r * z
        rz = rz[0:8] + rz[8:16]
        return total + sum(rz[:, k * 128 : k * 128 + 128] for k in range(CD // 128))

    residuals(8, 8)
    residuals(16 + RD, 8)
    sums_o[...] = lax.fori_loop(0, RD // 16, own, jnp.zeros((8, 128), F32))
    sums = block_sums(rowsum[...], group[...])
    for j in range(n_cr):
        blocks_o[j] = sums


def tensor_stage(n_in, n_cr, cuts, pos, amp, v, mask, depth, up, down, left, right, put, group, sums):
    vmem = pl.BlockSpec(memory_space=VMEM)
    hbm = pl.BlockSpec(memory_space=pltpu.HBM)
    ext = jax.ShapeDtypeStruct((ER, EC), F32)
    flat = jax.ShapeDtypeStruct((RD, CD), F32)
    return pl.pallas_call(
        functools.partial(tensor_kernel, n_in, n_cr, cuts),
        in_specs=[pl.BlockSpec(memory_space=pltpu.SMEM), hbm, hbm] + [vmem] * (8 + len(sums)),
        out_specs=[vmem] * 8,
        out_shape=[
            ext, ext, ext, ext, flat, flat,
            jax.ShapeDtypeStruct((n_cr, CR, CC), F32),
            jax.ShapeDtypeStruct((8, 128), F32),
        ],
        scratch_shapes=[
            VMEM((2, K, 48, EC), BF16), VMEM((K, RD, 128), BF16), VMEM((ER + 8, EC), F32), VMEM((ER, EC), F32),
            VMEM((ER, EC), F32), VMEM((ER, EC), F32), VMEM((ER, EC), F32), VMEM((CR, CD), F32),
            pltpu.SemaphoreType.DMA((3,)),
        ],
        compiler_params=pltpu.CompilerParams(vmem_limit_bytes=32 * 1024 * 1024),
        cost_estimate=pl.CostEstimate(flops=10**8, bytes_accessed=2 * 10**7, transcendentals=0),
        name="tensor_stage",
    )(pos, in_hbm(amp), in_hbm(v), mask, depth, up, down, left, right, put, group, *sums)


def moments_kernel(n_in, n_cr, extra, blocks, fwd_hi, fwd_lo, steps, pay_o, own_o):
    x = jnp.concatenate([blocks[j, :CR] for j in range(n_cr)], axis=1)
    hi, lo = parts2(x)
    span = slice(16, 16 + x.shape[1])
    both = dot(jnp.concatenate([hi, lo], axis=0), fwd_hi[span, :])
    x = both[:CR] + both[CR:] + dot(hi, fwd_lo[span, :])
    width = x.shape[1]
    forth, back = x, x
    for i in range(5):
        d = 1 << i
        zero = jnp.zeros((d, width), F32)
        decay = steps[i : i + 1]
        forth = forth + decay * jnp.concatenate([zero, forth[:-d]], axis=0)
        back = back + decay * jnp.concatenate([back[d:], zero], axis=0)
    decay, scale = steps[0:1], steps[5:6]
    zero = jnp.zeros((1, width), F32)
    inside = forth + decay * jnp.concatenate([back[1:], zero], axis=0)
    inside = scale * inside
    own_o[...] = jnp.concatenate(
        [scale * decay * back[0:1], inside, scale * decay * forth[CR - 1 :], jnp.zeros((6, width), F32)],
        axis=0,
    )
    f = jnp.concatenate([forth[CR - 1 :, 128 * k : 128 * k + 128] for k in range(n_cr)], axis=0)
    b = jnp.concatenate([back[0:1, 128 * k : 128 * k + 128] for k in range(n_cr)], axis=0)
    for i in range(n_in):
        pay_o[i, 0:n_cr] = f
        pay_o[i, n_cr : 2 * n_cr] = b
    if extra:
        sums = sum(blocks[j, CR : CR + 8] for j in range(n_cr))
        energy = jnp.sum(x * inside, axis=0, keepdims=True)
        energy = sum(energy[:, 128 * k : 128 * k + 128] for k in range(n_cr))
        at = lax.broadcasted_iota(jnp.int32, (8, 128), 0)
        sums = jnp.where(at == 3, energy, sums)
        for i in range(n_in):
            pay_o[i, 2 * n_cr : 2 * n_cr + 8] = sums


def moments_stage(n_in, n_cr, extra, blocks, fwd_hi, fwd_lo, steps):
    vmem = pl.BlockSpec(memory_space=VMEM)
    return pl.pallas_call(
        functools.partial(moments_kernel, n_in, n_cr, extra),
        in_specs=[vmem] * 4, out_specs=[vmem] * 2,
        out_shape=[
            jax.ShapeDtypeStruct((n_in, 2 * n_cr + 8 * extra, 128), F32),
            jax.ShapeDtypeStruct((40, CC * n_cr), F32),
        ],
        compiler_params=pltpu.CompilerParams(vmem_limit_bytes=32 * 1024 * 1024),
        cost_estimate=pl.CostEstimate(flops=2 * 10**8, bytes_accessed=5 * 10**6, transcendentals=0),
        name="moments_stage",
    )(blocks, fwd_hi, fwd_lo, steps)


def coarse_values(n_in, n_cr, pos, moments, own, grow, fall, blocks, fwd_hi, fwd_lo, spread):
    mine = pos[0]
    r32, whole, series, link = (blocks[i] for i in range(4))
    f = [moments[i, 0:n_cr] for i in range(n_in)]
    b = [moments[i, n_cr : 2 * n_cr] for i in range(n_in)]
    hf, hb = f[0], b[n_in - 1]
    for i in range(1, n_in):
        hf = r32 * hf + f[i]
        hb = r32 * hb + b[n_in - 1 - i]
    above = (hb + whole * hf) * series
    below = (hf + whole * hb) * series
    mine_above, mine_below = jnp.zeros_like(above), jnp.zeros_like(below)
    energy = jnp.zeros_like(above)
    for i in range(n_in):
        k = n_in - 1 - i
        mine_above = jnp.where(mine == i, above, mine_above)
        mine_below = jnp.where(mine == k, below, mine_below)
        energy += above * b[i] + below * f[k]
        above = r32 * above + f[i]
        below = r32 * below + b[k]
    energy = energy * link
    a_row = jnp.concatenate([mine_above[k : k + 1] for k in range(n_cr)], axis=1)
    b_row = jnp.concatenate([mine_below[k : k + 1] for k in range(n_cr)], axis=1)
    u = own[...] + a_row * grow[...] + b_row * fall[...]
    hi, lo = parts2(u)
    span = pl.ds(pl.multiple_of(pos[1] * CC, CC), 2 * CC)
    turned = (((1,), (1,)), ((), ()))
    both = lax.dot_general(jnp.concatenate([hi, lo], axis=0), fwd_hi[span, :], turned, preferred_element_type=F32)
    values = both[:40] + both[40:] + lax.dot_general(hi, fwd_lo[span, :], turned, preferred_element_type=F32)
    three = dot(jnp.concatenate(parts3(values), axis=0), spread[...])
    return values, three[:40] + three[40:80] + three[80:], energy


def image_kernel(
    n_in, n_cr, pos, moments, own, grow, fall, blocks, fwd_hi, fwd_lo, spread, group,
    ta, tb, tc, z, rd, mask, first_blocks, first_sums,
    p_o, q_o, blocks_o, rowsum, cs,
):
    values, spread_rows, _ = coarse_values(
        n_in, n_cr, pos, moments, own, grow, fall, blocks, fwd_hi, fwd_lo, spread
    )
    cs[...] = spread_rows

    def field(strip):
        at = pl.ds(pl.multiple_of(8 + 8 * strip, 8), 8)
        return z[at, :] + cs[pl.ds(strip, 1), :]

    def fluxes(at, n, value):
        here = value[0:n]
        dd = value[1 : n + 1] - here
        dr = pltpu.roll(here, EC - 1, 1) - here
        at = pl.ds(at, n)
        b = tb[at, :]
        return ta[at, :] * dd + b * dr, b * dd + tc[at, :] * dr

    def images(e, carry):
        pq, qq, strip, above = carry
        following = [field(2 * e + 2), field(2 * e + 3)]
        value = jnp.concatenate([strip] + following, axis=0)
        down, side = fluxes(pl.multiple_of(16 + 16 * e, 16), 16, value)
        flux = jnp.concatenate([above[7:8], down[0:15]], axis=0) - down + pltpu.roll(side, 1, 1) - side
        to = pl.ds(pl.multiple_of(16 * e, 16), 16)
        p = value[0:16, 128:]
        q = flux[:, 128:] + mask[to, :].astype(F32) * p
        p_o[to, :] = p
        q_o[to, :] = q
        rowsum[pl.ds(2 * e, 1), :] = jnp.sum(q[0:8], axis=0, keepdims=True)
        rowsum[pl.ds(2 * e + 1, 1), :] = jnp.sum(q[8:16], axis=0, keepdims=True)
        return pq + folded(p * q), qq + folded(q * q * rd[to, :]), following[1], down[8:16]

    def folded(x):
        x = x[0:8] + x[8:16]
        return sum(x[:, k * 128 : k * 128 + 128] for k in range(CD // 128))

    strip = field(1)
    above, _ = fluxes(8, 8, jnp.concatenate([field(0), strip], axis=0))
    zero = jnp.zeros((8, 128), F32)
    pq, qq, _, _ = lax.fori_loop(0, RD // 16, images, (zero, zero, strip, above))

    def lanes(x):
        return jnp.sum(x, axis=0, keepdims=True)

    rp = jnp.sum(first_sums[...], axis=0, keepdims=True)
    rp += jnp.sum(first_blocks[0] * pltpu.roll(values, 2 * CC - 16, 1)[1 : CR + 1, :CC], axis=0, keepdims=True)
    tail = jnp.concatenate([rp, lanes(pq), lanes(qq), jnp.zeros((5, 128), F32)], axis=0)
    sums = block_sums(rowsum[...], group[...])
    for j in range(n_cr):
        blocks_o[j, 0:CR] = sums
        blocks_o[j, CR : CR + 8] = tail


def final_kernel(
    n_in, n_cr, pos, moments, own, grow, fall, blocks, fwd_hi, fwd_lo, spread,
    p_in, q_in, r_in, rd, v_in, v_o, r_o, d_o, cs,
):
    _, spread_rows, energy = coarse_values(
        n_in, n_cr, pos, moments, own, grow, fall, blocks, fwd_hi, fwd_lo, spread
    )
    cs[...] = spread_rows
    sums = sum(moments[i, 2 * n_cr : 2 * n_cr + 8] for i in range(n_in))
    old = jnp.sum(sums[0:1], axis=1, keepdims=True)
    curvature = jnp.sum(sums[1:2], axis=1, keepdims=True)
    energy = jnp.sum(jnp.sum(energy, axis=0, keepdims=True), axis=1, keepdims=True)
    image = jnp.sum(sums[2:3] + sums[3:4], axis=1, keepdims=True) + energy
    step = old / curvature
    ratio = (step * step * image - old) / old
    more = 1.0 + ratio

    def body(e, carry):
        at = pl.ds(pl.multiple_of(16 * e, 16), 16)
        p, q = p_in[at, :], q_in[at, :]
        coarse = [jnp.broadcast_to(cs[pl.ds(2 * e + k, 1), 128:], (8, CD)) for k in (1, 2)]
        coarse = jnp.concatenate(coarse, axis=0)
        v_o[at, :] = v_in[at, :] + step * p
        r_o[at, :] = r_in[at, :] - step * q
        d_o[at, :] = more * p - step * (q * rd[at, :] + coarse)
        return carry

    lax.fori_loop(0, RD // 16, body, 0)


def coarse_call(kernel, n_in, n_cr, name, out_shape, scratch, pos, moments, own, tables, rest, group=None):
    vmem = pl.BlockSpec(memory_space=VMEM)
    args = [moments, own, tables["grow"], tables["fall"], tables["blocks"], *tables["forward"], tables["spread"]]
    args += ([group] if group is not None else []) + list(rest)
    return pl.pallas_call(
        functools.partial(kernel, n_in, n_cr),
        in_specs=[pl.BlockSpec(memory_space=pltpu.SMEM)] + [vmem] * len(args),
        out_specs=[vmem] * len(out_shape), out_shape=out_shape, scratch_shapes=scratch,
        compiler_params=pltpu.CompilerParams(vmem_limit_bytes=32 * 1024 * 1024),
        cost_estimate=pl.CostEstimate(flops=10**8, bytes_accessed=10**7, transcendentals=0),
        name=name,
    )(pos, *args)


def neighbours(value_low, value_high, axis, count):
    ahead = [(i, i + 1) for i in range(count - 1)]
    behind = [(j, i) for i, j in ahead]
    return lax.ppermute(value_high, axis, ahead), lax.ppermute(value_low, axis, behind)


def per_device(n_in, n_cr, amplitudes, mask, depth, iterate):
    rows, put, mix, lanes = (jnp.asarray(t) for t in line_tables())
    tables = coarse_tables(n_in, n_cr)
    pos = jnp.stack([lax.axis_index("inline"), lax.axis_index("crosslin")]).astype(jnp.int32)
    col_first, col_last = pack_columns(amplitudes, iterate, mask, depth)
    left, right = neighbours(col_first, col_last, "crosslin", n_cr)
    cuts = ((1, 7), (8, 7))
    *inner, lines = inner_stage(*cuts[0], amplitudes, (iterate, mask, depth, rows))
    (left, right), lines = lax.optimization_barrier(((left, right), lines))
    row_first, row_last = pack_rows(lines, left, right, mix, lanes)
    up, down = neighbours(row_first, row_last, "inline", n_in)
    inner += inner_stage(*cuts[1], amplitudes)
    group = jnp.asarray(tables["group"])
    ta, tb, tc, z, r, rd, blocks, sums = tensor_stage(
        n_in, n_cr, cuts, pos, amplitudes, iterate, mask, depth, up, down, left, right, put, group, inner
    )

    def moments_of(payload, extra):
        gathered = lax.all_to_all(payload, "crosslin", 0, 0, tiled=True)
        pay, own = moments_stage(n_in, n_cr, extra, gathered, *tables["forward"], tables["steps"])
        return lax.all_to_all(pay, "inline", 0, 0, tiled=True), own

    flat = jax.ShapeDtypeStruct((RD, CD), F32)
    cs = VMEM((40, EC), F32)
    moments, own = moments_of(blocks, False)
    p, q, payload = coarse_call(
        image_kernel, n_in, n_cr, "image_stage",
        [flat, flat, jax.ShapeDtypeStruct((n_cr, CR + 8, CC), F32)],
        [VMEM((CR, CD), F32), cs],
        pos, moments, own, tables, [ta, tb, tc, z, rd, mask, blocks, sums], group,
    )
    moments, own = moments_of(payload, True)
    return tuple(
        coarse_call(
            final_kernel, n_in, n_cr, "final_stage", [flat, flat, flat], [cs],
            pos, moments, own, tables, [p, q, r, rd, iterate],
        )
    )


def solution(mesh):
    n_in, n_cr = mesh.shape["inline"], mesh.shape["crosslin"]
    flat = P("inline", "crosslin")
    return jax.shard_map(
        functools.partial(per_device, n_in, n_cr), mesh=mesh,
        in_specs=(P(None, "inline", "crosslin"), flat, flat, flat),
        out_specs=(flat, flat, flat), check_vma=False,
    )
```

```python
import functools

import jax
import jax.numpy as jnp
import ml_dtypes
import numpy as np
from jax import lax
from jax.experimental import pallas as pl
from jax.experimental.pallas import tpu as pltpu
from jax.sharding import PartitionSpec as P

K = 16
DEC = 8
CI = 32
COUPLING = 4.0
F32 = jnp.float32
BF16 = jnp.bfloat16
NPB = ml_dtypes.bfloat16
VMEM = pltpu.VMEM

RD = 256
CD = 1024
ER = RD + 32
EC = CD + 128
CR = RD // DEC
CC = CD // DEC
MSG = 64


def in_hbm(x):
    return pltpu.with_memory_space_constraint(x, pltpu.HBM)


def dot(a, b):
    return jnp.dot(a, b, preferred_element_type=F32)


def parts2(x):
    hi = x.astype(BF16)
    return hi, (x - hi.astype(F32)).astype(BF16)


def parts3(x):
    hi = x.astype(BF16)
    rest = x - hi.astype(F32)
    mid = rest.astype(BF16)
    return hi, mid, (rest - mid.astype(F32)).astype(BF16)


def np2(x):
    hi = x.astype(np.float32).astype(NPB)
    return hi, (x - hi.astype(np.float64)).astype(np.float32).astype(NPB)


def line_tables():
    rows = np.zeros((2, MSG, 256), np.float32)
    put = np.zeros((2, 304, MSG), np.float32)
    for s in range(K):
        for k in range(3):
            rows[0, 3 * s + k, 16 * s + k] = 1
            rows[1, 3 * s + k, 16 * s + 13 + k] = 1
    for side in range(2):
        put[side, :256] = rows[side].T
        for l in range(2):
            for part in range(3):
                put[side, 256 + (14 + l if side else l), 48 + 3 * l + part] = 1
        put[side, 272 + (15 if side else 0), 54] = 1
        put[side, 288 + (15 if side else 0), 55] = 1
    mix = np.zeros((2, 3, MSG, 128), np.float32)
    for k in range(3):
        for s in range(K):
            mix[:, k, 3 * s + k, 3 * s : 3 * s + 3] = 1
    for l in range(2):
        for part in range(3):
            for other in range(2):
                mix[0, l, 48 + 3 * l + part, 48 + 3 * other + part] = 1
                mix[1, l + 1, 48 + 3 * l + part, 48 + 3 * other + part] = 1
    for o in (54, 55):
        mix[0, 0, o, o] = 1
        mix[1, 2, o, o] = 1
    lanes = np.zeros((2, 128, 128), np.float32)
    for s in range(K):
        for k in range(3):
            lanes[0, 3 * s + k, k] = 1
            lanes[1, 3 * s + k, 125 + k] = 1
    for l in range(2):
        for part in range(3):
            lanes[0, 48 + 3 * l + part, l] = 1
            lanes[1, 48 + 3 * l + part, 126 + l] = 1
    for o in (54, 55):
        lanes[0, o, 0] = 1
        lanes[1, o, 127] = 1
    return tuple(t.astype(NPB) for t in (rows, put, mix, lanes))


def coarse_tables(n_in, n_cr):
    n = CC * n_cr
    freq = np.arange(n, dtype=np.float64)
    norm = np.where(freq == 0, np.sqrt(1.0 / n), np.sqrt(2.0 / n))

    def cosines(cols):
        phase = (freq[:, None] * (2 * cols[None, :] + 1)) % (4 * n)
        return norm[:, None] * np.cos(np.pi * phase / (2 * n))

    lead = np.arange(n + CC, dtype=np.float64) - 16
    forward = cosines(lead).T * (lead[:, None] >= -1) * (lead[:, None] <= n)
    half = (2.0 - 2.0 * np.cos(np.pi * freq / n) + 1.0 / (CI * CI)) / 2.0
    kappa = np.log1p(half + np.sqrt(half * (half + 2.0)))
    scale = 1.0 / (COUPLING * 2.0 * np.sinh(kappa))
    steps = np.stack([np.exp(-kappa * d) for d in (1, 2, 4, 8, 16)] + [scale] + [scale * 0] * 2)
    at = np.arange(40)[:, None]
    grow = scale * np.exp(-kappa * at) * (at < 34)
    fall = scale * np.exp(-kappa * (33.0 - at)) * (at < 34)
    whole = CR * n_in
    blocks = np.stack(
        [
            np.exp(-kappa * CR),
            np.exp(-kappa * whole),
            1.0 / (1.0 - np.exp(-kappa * 2 * whole)),
            scale * np.exp(-kappa),
        ]
    ).reshape(4, n_cr, 128)
    spread = np.zeros((2 * CC, EC))
    for lane in range(EC):
        col = ((lane if lane >= 64 else lane + EC) - 128) // DEC
        if -1 <= col <= CC:
            spread[16 + col, lane] = 1
    group = np.zeros((CD, CC))
    group[np.arange(CD), np.arange(CD) // DEC] = 1
    f = np.float32
    return dict(
        forward=np2(forward), steps=steps.astype(f), grow=grow.astype(f),
        fall=fall.astype(f), blocks=blocks.astype(f), spread=spread.astype(NPB), group=group.astype(NPB),
    )


def moved(x, lane, to):
    turn = (to - lane) % x.shape[1]
    return pltpu.roll(x, turn, 1) if turn else x


def pack_columns_kernel(amp, v_in, m_in, d_in, out0, out1, amp_o, v, m, d, sems, rest_sem):
    copies = []
    for side, at in enumerate((0, CD - 128)):
        span = pl.ds(at, 128)
        copies.append(pltpu.make_async_copy(amp.at[:, :, span], amp_o.at[:, :, span], sems.at[side, 0]))
        copies.append(pltpu.make_async_copy(v_in.at[:, span], v.at[side], sems.at[side, 1]))
        copies.append(pltpu.make_async_copy(m_in.at[:, span], m.at[side], sems.at[side, 2]))
        copies.append(pltpu.make_async_copy(d_in.at[:, span], d.at[side], sems.at[side, 3]))
    middle = pl.ds(128, CD - 256)
    rest = pltpu.make_async_copy(amp.at[:, :, middle], amp_o.at[:, :, middle], rest_sem)
    for c in copies:
        c.start()
    rest.start()
    lane = lax.broadcasted_iota(jnp.int32, (RD, 128), 1)
    for c in copies:
        c.wait()
    for side, out in enumerate((out0, out1)):
        low = 125 if side else 0

        def edge(s, side=side):
            return amp_o[s, :, CD - 128 :] if side else amp_o[s, :, 0:128]

        weight = m[side].astype(F32)
        source = weight * (d[side].astype(F32) - 0.5 * (K - 1))
        end = 127 if side else 0
        total = jnp.where(lane == 54, moved(weight, end, 54), moved(source, end, 55))
        for part, value in enumerate(parts3(v[side])):
            value = value.astype(F32)
            for l in range(2):
                to = 48 + 3 * l + part
                total = jnp.where(lane == to, moved(value, (126 if side else 0) + l, to), total)
        for s in range(K):
            total = jnp.where((lane >= 3 * s) & (lane < 3 * s + 3), moved(edge(s).astype(F32), low, 3 * s), total)
        out[...] = jnp.where(lane < 56, total, 0.0).astype(BF16)
    rest.wait()


def pack_columns(amplitudes, iterate, mask, depth):
    hbm = pl.BlockSpec(memory_space=pltpu.HBM)
    out = jax.ShapeDtypeStruct((RD, 128), BF16)
    return pl.pallas_call(
        pack_columns_kernel, in_specs=[hbm] * 4,
        out_specs=[pl.BlockSpec(memory_space=VMEM)] * 3,
        out_shape=[out, out, jax.ShapeDtypeStruct((K, RD, CD), BF16)],
        scratch_shapes=[
            VMEM((2, RD, 128), F32), VMEM((2, RD, 128), jnp.int32),
            VMEM((2, RD, 128), jnp.int32), pltpu.SemaphoreType.DMA((2, 4)), pltpu.SemaphoreType.DMA,
        ],
        compiler_params=pltpu.CompilerParams(vmem_limit_bytes=12 * 1024 * 1024),
        cost_estimate=pl.CostEstimate(flops=10**7, bytes_accessed=3 * 10**6, transcendentals=0),
        name="pack_columns",
    )(*(in_hbm(x) for x in (amplitudes, iterate, mask, depth)))


def pack_rows_kernel(lines, left, right, mix, lanes, out0, out1):
    for side, out in enumerate((out0, out1)):
        out[:, 128:] = lines[side]
        total = jnp.zeros((MSG, 128), F32)
        for halo, which in ((left, 1), (right, 0)):
            edge = halo[RD - 16 : RD].astype(F32)[13:16] if side else halo[0:16].astype(F32)[0:3]
            for k in range(3):
                term = mix[side, k].astype(F32) * edge[k : k + 1]
                total += dot(term.astype(BF16), lanes[which])
        out[:, 0:128] = total.astype(BF16)


def pack_rows(lines, left, right, mix, lanes):
    vmem = pl.BlockSpec(memory_space=VMEM)
    out = jax.ShapeDtypeStruct((MSG, EC), BF16)
    return pl.pallas_call(
        pack_rows_kernel, in_specs=[vmem] * 5, out_specs=[vmem] * 2, out_shape=[out, out],
        compiler_params=pltpu.CompilerParams(vmem_limit_bytes=12 * 1024 * 1024),
        cost_estimate=pl.CostEstimate(flops=10**7, bytes_accessed=10**6, transcendentals=0),
        name="pack_rows",
    )(lines, left, right, mix, lanes)


def row_band(rows, window, lead):
    at = lax.broadcasted_iota(jnp.int32, (rows, window), 0) + lead
    to = lax.broadcasted_iota(jnp.int32, (rows, window), 1)
    return jnp.where(to == at + 1, 1.0, jnp.where(to == at - 1, -1.0, 0.0)).astype(BF16)


def gradient_sums(window, band, span, off, take):
    total = None
    for s in range(K):
        x = window(s)
        n = x.shape[1]
        middle = x[span]
        gc = pltpu.roll(middle, n - 1, 1).astype(F32) - pltpu.roll(middle, 1, 1).astype(F32)
        gc = gc[:, off : off + take]
        gi = dot(band, x[:, off : off + take])
        terms = (gi * gi, gi * gc, gc * gc)
        total = terms if total is None else tuple(t + u for t, u in zip(total, terms))
    return total


def edge_lines(side, a, v, m, d, rows):
    at = lax.broadcasted_iota(jnp.int32, (MSG, CD), 0)
    middle = dot(rows[side], a.reshape(K * 16, CD))
    split = [p.astype(F32) for p in parts3(v)]
    for l in range(2):
        row = 6 + l if side else l
        for part in range(3):
            middle = jnp.where(at == 48 + 3 * l + part, split[part][row : row + 1], middle)
    row = 7 if side else 0
    weight = m[row : row + 1].astype(F32)
    source = weight * (d[row : row + 1].astype(F32) - 0.5 * (K - 1))
    return jnp.where(at == 54, weight, jnp.where(at == 55, source, middle)).astype(BF16)


def inner_kernel(first, steps, edge, amp, *rest):
    if edge:
        v_in, m_in, d_in, rows_t, sii_o, sic_o, scc_o, edge_o, lines_o, v, m, d, end_sems = rest
    else:
        sii_o, sic_o, scc_o, edge_o = rest
    base = 16 * (first - 1)
    if edge:
        more = []
        for side in range(2):
            for i, (source, to) in enumerate(((v_in, v), (m_in, m), (d_in, d))):
                span = pl.ds(side * (RD - 8), 8)
                more.append(pltpu.make_async_copy(source.at[span], to.at[side], end_sems.at[3 * side + i]))
        for c in more:
            c.start()
    lane = lax.broadcasted_iota(jnp.int32, (16, 128), 1)
    band = row_band(16, 48, 16)

    def step(t, carry):
        at = pl.multiple_of(16 * t, 16)
        window = pl.ds(pl.multiple_of(base + 16 * t, 16), 48)
        for part in range(2):
            lanes = slice(0, 640) if part == 0 else slice(384, CD)
            off = 0 if part == 0 else 128
            sums = gradient_sums(lambda s: amp[s, window, lanes], band, slice(16, 32), off, 512)
            for o, value in zip((sii_o, sic_o, scc_o), sums):
                o[pl.ds(at, 16), 512 * part : 512 * part + 512] = value
        return carry

    def edges(t, carry):
        at = pl.ds(pl.multiple_of(16 * t, 16), 16)
        source = pl.ds(pl.multiple_of(16 * t + 128 * (base > 0), 16), 16)
        for s in range(K):
            low = moved(amp[s, source, 0:128].astype(F32), 0, 35)
            high = moved(amp[s, source, CD - 128 : CD].astype(F32), 125, 64)
            tile = jnp.where((lane >= 35) & (lane < 38), low, jnp.where((lane >= 64) & (lane < 67), high, 0.0))
            edge_o[s, at, :] = tile.astype(BF16)
        return carry

    lax.fori_loop(0, steps, step, 0)
    lax.fori_loop(0, 8, edges, 0)
    if edge:
        for c in more:
            c.wait()
        lines_o[0] = edge_lines(0, amp[:, 0:16, :], v[0], m[0], d[0], rows_t)
        lines_o[1] = edge_lines(1, amp[:, RD - 16 :, :], v[1], m[1], d[1], rows_t)


def inner_stage(first, steps, amplitudes, more=()):
    hbm, vmem = pl.BlockSpec(memory_space=pltpu.HBM), pl.BlockSpec(memory_space=VMEM)
    flat = jax.ShapeDtypeStruct((16 * steps, CD), F32)
    out_shape = [flat, flat, flat, jax.ShapeDtypeStruct((K, 128, 128), BF16)]
    scratch = []
    in_specs = [vmem]
    if more:
        out_shape += [jax.ShapeDtypeStruct((2, MSG, CD), BF16)]
        scratch += [
            VMEM((2, 8, CD), F32), VMEM((2, 8, CD), jnp.int32), VMEM((2, 8, CD), jnp.int32),
            pltpu.SemaphoreType.DMA((6,)),
        ]
        in_specs += [hbm, hbm, hbm, vmem]
    return pl.pallas_call(
        functools.partial(inner_kernel, first, steps, bool(more)),
        in_specs=in_specs, out_specs=[vmem] * len(out_shape), out_shape=out_shape, scratch_shapes=scratch,
        compiler_params=pltpu.CompilerParams(vmem_limit_bytes=14 * 1024 * 1024),
        cost_estimate=pl.CostEstimate(flops=10**8, bytes_accessed=6 * 10**6, transcendentals=0),
        name="inner_stage",
    )(amplitudes, *(in_hbm(x) for x in more[:3]), *more[3:])


def block_sums(rows, group):
    return sum(dot(part, group) for part in parts3(rows))


def tensor_kernel(
    n_in, n_cr, cuts, pos, amp, v_in, mask, depth, up, down, left, right, put, group, *rest
):
    inner_refs, rest = rest[: 4 * len(cuts)], rest[4 * len(cuts) :]
    (ta_o, tb_o, tc_o, z_o, r_o, rd_o, blocks_o, sums_o,
     tops, rim, rim_sums, v_ext, w_ext, s_ext, fd, fr, rowsum, sems) = rest
    inner = (slice(16, 16 + RD), slice(128, EC))
    copies = [
        pltpu.make_async_copy(amp.at[:, 0:32], tops.at[0, :, 16:48, 128:EC], sems.at[0]),
        pltpu.make_async_copy(amp.at[:, RD - 32 : RD], tops.at[1, :, 0:32, 128:EC], sems.at[1]),
        pltpu.make_async_copy(v_in, v_ext.at[16 : 16 + RD, 128:EC], sems.at[2]),
    ]
    for c in copies:
        c.start()
    weight = mask[...].astype(F32)
    w_ext[inner] = weight
    s_ext[inner] = weight * (depth[...].astype(F32) - 0.5 * (K - 1))
    lane = lax.broadcasted_iota(jnp.int32, (RD, 128), 1)
    before, after = left[...].astype(F32), right[...].astype(F32)
    here = slice(16, 16 + RD)
    value = jnp.zeros((RD, 128), F32)
    for l in range(2):
        for halo, to in ((before, 126 + l), (after, l)):
            got = sum(moved(halo, 48 + 3 * l + part, to) for part in range(3))
            value = jnp.where(lane == to, got, value)
    v_ext[here, 0:128] = value
    for o, message in ((w_ext, 54), (s_ext, 55)):
        value = jnp.where(lane == 127, moved(before, message, 127), 0.0)
        o[here, 0:128] = jnp.where(lane == 0, moved(after, message, 0), value)
    for s in range(K):
        value = jnp.where(lane < 3, moved(after, 3 * s, 0), 0.0)
        value = jnp.where(lane >= 125, moved(before, 3 * s, 125), value).astype(BF16)
        tops[0, s, 16:48, 0:128] = value[0:32]
        tops[1, s, 0:32, 0:128] = value[RD - 32 : RD]
    for c in range(2):
        span = slice(128 * c, 128 * c + 128)
        turned, turned_after, tile = before[span], after[span], lane[span]
        for s in range(K):
            value = inner_refs[4 * c + 3][s].astype(F32)
            value = jnp.where((tile >= 32) & (tile < 35), moved(turned, 3 * s, 32), value)
            value = jnp.where((tile >= 67) & (tile < 70), moved(turned_after, 3 * s, 67), value)
            rim[s, span, :] = value.astype(BF16)
    for side, halo, row in ((1, up, 0), (0, down, 16 + RD)):
        lines = dot(put[side], halo[...])
        for s in range(K):
            tops[1 - side, s, 32 - 32 * side : 48 - 32 * side, :] = lines[16 * s : 16 * s + 16].astype(BF16)
        v_ext[row : row + 16, :] = lines[256:272]
        w_ext[row : row + 16, :] = lines[272:288]
        s_ext[row : row + 16, :] = lines[288:304]
    for c in copies:
        c.wait()
    at_lane = lax.broadcasted_iota(jnp.int32, (1, EC), 1)
    col = pos[1] * CD + jnp.where(at_lane < 64, at_lane + CD, at_lane - 128)
    valid_right = ((col >= 0) & (col < n_cr * CD - 1)).astype(F32)
    row_iota = lax.broadcasted_iota(jnp.int32, (16, 1), 0)
    tile_lane = lax.broadcasted_iota(jnp.int32, (16, 128), 1)

    def left_of(x):
        return pltpu.roll(x, 1, 1)

    def right_of(x):
        return pltpu.roll(x, EC - 1, 1)

    def finish(at, sums):
        sii, sic, scc = (0.25 * x for x in sums)
        inv = 1.0 / (sii + scc + 2.0)
        row = pos[0] * RD - 16 + at + row_iota
        valid_down = ((row >= 0) & (row < n_in * RD - 1)).astype(F32)
        ta = valid_down * ((scc + 1.0) * inv)
        tb = (valid_down * valid_right) * (-sic * inv)
        tc = valid_right * ((sii + 1.0) * inv)
        value = v_ext[pl.ds(at, 24), :]
        here = value[0:16]
        dd = value[1:17] - here
        dr = right_of(here) - here
        to = pl.ds(at, 16)
        ta_o[to, :] = ta
        tb_o[to, :] = tb
        tc_o[to, :] = tc
        fd[to, :] = ta * dd + tb * dr
        fr[to, :] = tb * dd + tc * dr

    for side in range(2):
        for half in range(2):
            lead = 16 * (side + half)
            sums = gradient_sums(
                lambda s, side=side: tops[side, s], row_band(16, 48, lead), slice(lead, lead + 16), 0, EC
            )
            finish((RD if side else 0) + 16 * half, sums)

    wide = row_band(32, 64, 16)

    def rim_step(t, carry):
        at = pl.multiple_of(32 * t, 32)
        edge = gradient_sums(lambda s: rim[s, pl.ds(at, 64), :], wide, slice(16, 48), 0, 128)
        for i, e in enumerate(edge):
            rim_sums[i, pl.ds(pl.multiple_of(at + 16, 16), 32), :] = e
        return carry

    lax.fori_loop(0, RD // 32 - 1, rim_step, 0)

    for c, (first, steps) in enumerate(cuts):
        sii, sic, scc = inner_refs[4 * c : 4 * c + 3]

        def step(t, carry, sii=sii, sic=sic, scc=scc, first=first):
            local = pl.ds(pl.multiple_of(16 * (t - first), 16), 16)
            at = pl.ds(pl.multiple_of(16 * t, 16), 16)
            sums = []
            for ref, e in zip((sii, sic, scc), (rim_sums[i, at, :] for i in range(3))):
                low, high = pltpu.roll(e, 93, 1), pltpu.roll(e, 61, 1)
                x = ref[local, :]
                sums.append(
                    jnp.concatenate(
                        [
                            jnp.where(tile_lane < 64, high, low),
                            jnp.where(tile_lane == 0, low, x[:, 0:128]),
                            x[:, 128 : CD - 128],
                            jnp.where(tile_lane == 127, high, x[:, CD - 128 :]),
                        ],
                        axis=1,
                    )
                )
            finish(pl.multiple_of(16 * t + 16, 16), sums)
            return carry

        lax.fori_loop(first, first + steps, step, 0)

    def residuals(at, n):
        before = pl.ds(pl.multiple_of(at - 8, 8), n + 8)
        here = pl.ds(at, n)
        fdw, taw = fd[before, :], ta_o[before, :]
        tc, right_flux, weight = tc_o[here, :], fr[here, :], w_ext[here, :]
        image = fdw[7 : n + 7] - fdw[8 : n + 8] + left_of(right_flux) - right_flux + weight * v_ext[here, :]
        r = s_ext[here, :] - image
        diag = taw[8 : n + 8] + 2.0 * tb_o[here, :] + tc + taw[7 : n + 7] + left_of(tc) + weight
        inv = jnp.where(diag != 0.0, 1.0 / diag, 0.0)
        z = r * inv
        z_o[here, :] = z
        return r, inv, z

    def own(e, total):
        at = pl.multiple_of(16 + 16 * e, 16)
        r, inv, z = (x[:, 128:] for x in residuals(at, 16))
        to = pl.ds(pl.multiple_of(16 * e, 16), 16)
        r_o[to, :] = r
        rd_o[to, :] = inv
        rowsum[pl.ds(2 * e, 1), :] = jnp.sum(r[0:8], axis=0, keepdims=True)
        rowsum[pl.ds(2 * e + 1, 1), :] = jnp.sum(r[8:16], axis=0, keepdims=True)
        rz = r * z
        rz = rz[0:8] + rz[8:16]
        return total + sum(rz[:, k * 128 : k * 128 + 128] for k in range(CD // 128))

    residuals(8, 8)
    residuals(16 + RD, 8)
    sums_o[...] = lax.fori_loop(0, RD // 16, own, jnp.zeros((8, 128), F32))
    sums = block_sums(rowsum[...], group[...])
    for j in range(n_cr):
        blocks_o[j] = sums


def tensor_stage(n_in, n_cr, cuts, pos, amp, v, mask, depth, up, down, left, right, put, group, sums):
    vmem = pl.BlockSpec(memory_space=VMEM)
    hbm = pl.BlockSpec(memory_space=pltpu.HBM)
    ext = jax.ShapeDtypeStruct((ER, EC), F32)
    flat = jax.ShapeDtypeStruct((RD, CD), F32)
    return pl.pallas_call(
        functools.partial(tensor_kernel, n_in, n_cr, cuts),
        in_specs=[pl.BlockSpec(memory_space=pltpu.SMEM), pl.BlockSpec(memory_space=pl.ANY), hbm] + [vmem] * (8 + len(sums)),
        out_specs=[vmem] * 8,
        out_shape=[
            ext, ext, ext, ext, flat, flat,
            jax.ShapeDtypeStruct((n_cr, CR, CC), F32),
            jax.ShapeDtypeStruct((8, 128), F32),
        ],
        scratch_shapes=[
            VMEM((2, K, 48, EC), BF16), VMEM((K, RD, 128), BF16), VMEM((3, RD, 128), F32), VMEM((ER + 8, EC), F32), VMEM((ER, EC), F32),
            VMEM((ER, EC), F32), VMEM((ER, EC), F32), VMEM((ER, EC), F32), VMEM((CR, CD), F32),
            pltpu.SemaphoreType.DMA((3,)),
        ],
        compiler_params=pltpu.CompilerParams(vmem_limit_bytes=28 * 1024 * 1024),
        cost_estimate=pl.CostEstimate(flops=10**8, bytes_accessed=2 * 10**7, transcendentals=0),
        name="tensor_stage",
    )(pos, amp, in_hbm(v), mask, depth, up, down, left, right, put, group, *sums)


def moments_kernel(n_in, n_cr, extra, blocks, fwd_hi, fwd_lo, steps, pay_o, own_o):
    x = jnp.concatenate([blocks[j, :CR] for j in range(n_cr)], axis=1)
    hi, lo = parts2(x)
    span = slice(16, 16 + x.shape[1])
    both = dot(jnp.concatenate([hi, lo], axis=0), fwd_hi[span, :])
    x = both[:CR] + both[CR:] + dot(hi, fwd_lo[span, :])
    width = x.shape[1]
    forth, back = x, x
    for i in range(5):
        d = 1 << i
        zero = jnp.zeros((d, width), F32)
        decay = steps[i : i + 1]
        forth = forth + decay * jnp.concatenate([zero, forth[:-d]], axis=0)
        back = back + decay * jnp.concatenate([back[d:], zero], axis=0)
    decay, scale = steps[0:1], steps[5:6]
    zero = jnp.zeros((1, width), F32)
    inside = forth + decay * jnp.concatenate([back[1:], zero], axis=0)
    inside = scale * inside
    own_o[...] = jnp.concatenate(
        [scale * decay * back[0:1], inside, scale * decay * forth[CR - 1 :], jnp.zeros((6, width), F32)],
        axis=0,
    )
    f = jnp.concatenate([forth[CR - 1 :, 128 * k : 128 * k + 128] for k in range(n_cr)], axis=0)
    b = jnp.concatenate([back[0:1, 128 * k : 128 * k + 128] for k in range(n_cr)], axis=0)
    for i in range(n_in):
        pay_o[i, 0:n_cr] = f
        pay_o[i, n_cr : 2 * n_cr] = b
    if extra:
        sums = sum(blocks[j, CR : CR + 8] for j in range(n_cr))
        energy = jnp.sum(x * inside, axis=0, keepdims=True)
        energy = sum(energy[:, 128 * k : 128 * k + 128] for k in range(n_cr))
        at = lax.broadcasted_iota(jnp.int32, (8, 128), 0)
        sums = jnp.where(at == 3, energy, sums)
        for i in range(n_in):
            pay_o[i, 2 * n_cr : 2 * n_cr + 8] = sums


def moments_stage(n_in, n_cr, extra, blocks, fwd_hi, fwd_lo, steps):
    vmem = pl.BlockSpec(memory_space=VMEM)
    return pl.pallas_call(
        functools.partial(moments_kernel, n_in, n_cr, extra),
        in_specs=[vmem] * 4, out_specs=[vmem] * 2,
        out_shape=[
            jax.ShapeDtypeStruct((n_in, 2 * n_cr + 8 * extra, 128), F32),
            jax.ShapeDtypeStruct((40, CC * n_cr), F32),
        ],
        compiler_params=pltpu.CompilerParams(vmem_limit_bytes=12 * 1024 * 1024),
        cost_estimate=pl.CostEstimate(flops=2 * 10**8, bytes_accessed=5 * 10**6, transcendentals=0),
        name="moments_stage",
    )(blocks, fwd_hi, fwd_lo, steps)


def coarse_values(n_in, n_cr, pos, moments, own, grow, fall, blocks, fwd_hi, fwd_lo, spread):
    mine = pos[0]
    r32, whole, series, link = (blocks[i] for i in range(4))
    f = [moments[i, 0:n_cr] for i in range(n_in)]
    b = [moments[i, n_cr : 2 * n_cr] for i in range(n_in)]
    hf, hb = f[0], b[n_in - 1]
    for i in range(1, n_in):
        hf = r32 * hf + f[i]
        hb = r32 * hb + b[n_in - 1 - i]
    above = (hb + whole * hf) * series
    below = (hf + whole * hb) * series
    mine_above, mine_below = jnp.zeros_like(above), jnp.zeros_like(below)
    energy = jnp.zeros_like(above)
    for i in range(n_in):
        k = n_in - 1 - i
        mine_above = jnp.where(mine == i, above, mine_above)
        mine_below = jnp.where(mine == k, below, mine_below)
        energy += above * b[i] + below * f[k]
        above = r32 * above + f[i]
        below = r32 * below + b[k]
    energy = energy * link
    a_row = jnp.concatenate([mine_above[k : k + 1] for k in range(n_cr)], axis=1)
    b_row = jnp.concatenate([mine_below[k : k + 1] for k in range(n_cr)], axis=1)
    u = own[...] + a_row * grow[...] + b_row * fall[...]
    hi, lo = parts2(u)
    span = pl.ds(pl.multiple_of(pos[1] * CC, CC), 2 * CC)
    turned = (((1,), (1,)), ((), ()))
    both = lax.dot_general(jnp.concatenate([hi, lo], axis=0), fwd_hi[span, :], turned, preferred_element_type=F32)
    values = both[:40] + both[40:] + lax.dot_general(hi, fwd_lo[span, :], turned, preferred_element_type=F32)
    three = dot(jnp.concatenate(parts3(values), axis=0), spread[...])
    return values, three[:40] + three[40:80] + three[80:], energy


def image_kernel(
    n_in, n_cr, pos, moments, own, grow, fall, blocks, fwd_hi, fwd_lo, spread, group,
    ta, tb, tc, z, rd, mask, first_blocks, first_sums,
    p_o, q_o, blocks_o, rowsum, cs,
):
    values, spread_rows, _ = coarse_values(
        n_in, n_cr, pos, moments, own, grow, fall, blocks, fwd_hi, fwd_lo, spread
    )
    cs[...] = spread_rows

    def field(strip):
        at = pl.ds(pl.multiple_of(8 + 8 * strip, 8), 8)
        return z[at, :] + cs[pl.ds(strip, 1), :]

    def fluxes(at, n, value):
        here = value[0:n]
        dd = value[1 : n + 1] - here
        dr = pltpu.roll(here, EC - 1, 1) - here
        at = pl.ds(at, n)
        b = tb[at, :]
        return ta[at, :] * dd + b * dr, b * dd + tc[at, :] * dr

    def images(e, carry):
        pq, qq, strip, above = carry
        following = [field(2 * e + 2), field(2 * e + 3)]
        value = jnp.concatenate([strip] + following, axis=0)
        down, side = fluxes(pl.multiple_of(16 + 16 * e, 16), 16, value)
        flux = jnp.concatenate([above[7:8], down[0:15]], axis=0) - down + pltpu.roll(side, 1, 1) - side
        to = pl.ds(pl.multiple_of(16 * e, 16), 16)
        p = value[0:16, 128:]
        q = flux[:, 128:] + mask[to, :].astype(F32) * p
        p_o[to, :] = p
        q_o[to, :] = q
        rowsum[pl.ds(2 * e, 1), :] = jnp.sum(q[0:8], axis=0, keepdims=True)
        rowsum[pl.ds(2 * e + 1, 1), :] = jnp.sum(q[8:16], axis=0, keepdims=True)
        return pq + folded(p * q), qq + folded(q * q * rd[to, :]), following[1], down[8:16]

    def folded(x):
        x = x[0:8] + x[8:16]
        return sum(x[:, k * 128 : k * 128 + 128] for k in range(CD // 128))

    strip = field(1)
    above, _ = fluxes(8, 8, jnp.concatenate([field(0), strip], axis=0))
    zero = jnp.zeros((8, 128), F32)
    pq, qq, _, _ = lax.fori_loop(0, RD // 16, images, (zero, zero, strip, above))

    def lanes(x):
        return jnp.sum(x, axis=0, keepdims=True)

    rp = jnp.sum(first_sums[...], axis=0, keepdims=True)
    rp += jnp.sum(first_blocks[0] * pltpu.roll(values, 2 * CC - 16, 1)[1 : CR + 1, :CC], axis=0, keepdims=True)
    tail = jnp.concatenate([rp, lanes(pq), lanes(qq), jnp.zeros((5, 128), F32)], axis=0)
    sums = block_sums(rowsum[...], group[...])
    for j in range(n_cr):
        blocks_o[j, 0:CR] = sums
        blocks_o[j, CR : CR + 8] = tail


def final_kernel(
    n_in, n_cr, pos, moments, own, grow, fall, blocks, fwd_hi, fwd_lo, spread,
    p_in, q_in, r_in, rd, v_in, v_o, r_o, d_o, cs,
):
    _, spread_rows, energy = coarse_values(
        n_in, n_cr, pos, moments, own, grow, fall, blocks, fwd_hi, fwd_lo, spread
    )
    cs[...] = spread_rows
    sums = sum(moments[i, 2 * n_cr : 2 * n_cr + 8] for i in range(n_in))
    old = jnp.sum(sums[0:1], axis=1, keepdims=True)
    curvature = jnp.sum(sums[1:2], axis=1, keepdims=True)
    energy = jnp.sum(jnp.sum(energy, axis=0, keepdims=True), axis=1, keepdims=True)
    image = jnp.sum(sums[2:3] + sums[3:4], axis=1, keepdims=True) + energy
    step = old / curvature
    ratio = (step * step * image - old) / old
    more = 1.0 + ratio

    def body(e, carry):
        at = pl.ds(pl.multiple_of(16 * e, 16), 16)
        p, q = p_in[at, :], q_in[at, :]
        coarse = [jnp.broadcast_to(cs[pl.ds(2 * e + k, 1), 128:], (8, CD)) for k in (1, 2)]
        coarse = jnp.concatenate(coarse, axis=0)
        v_o[at, :] = v_in[at, :] + step * p
        r_o[at, :] = r_in[at, :] - step * q
        d_o[at, :] = more * p - step * (q * rd[at, :] + coarse)
        return carry

    lax.fori_loop(0, RD // 16, body, 0)


def coarse_call(kernel, n_in, n_cr, name, out_shape, scratch, pos, moments, own, tables, rest, group=None):
    vmem = pl.BlockSpec(memory_space=VMEM)
    args = [moments, own, tables["grow"], tables["fall"], tables["blocks"], *tables["forward"], tables["spread"]]
    args += ([group] if group is not None else []) + list(rest)
    return pl.pallas_call(
        functools.partial(kernel, n_in, n_cr),
        in_specs=[pl.BlockSpec(memory_space=pltpu.SMEM)] + [vmem] * len(args),
        out_specs=[vmem] * len(out_shape), out_shape=out_shape, scratch_shapes=scratch,
        compiler_params=pltpu.CompilerParams(vmem_limit_bytes=22 * 1024 * 1024),
        cost_estimate=pl.CostEstimate(flops=10**8, bytes_accessed=10**7, transcendentals=0),
        name=name,
    )(pos, *args)


def neighbours(value_low, value_high, axis, count):
    ahead = [(i, i + 1) for i in range(count - 1)]
    behind = [(j, i) for i, j in ahead]
    return lax.ppermute(value_high, axis, ahead), lax.ppermute(value_low, axis, behind)


def per_device(n_in, n_cr, amplitudes, mask, depth, iterate):
    rows, put, mix, lanes = (jnp.asarray(t) for t in line_tables())
    tables = coarse_tables(n_in, n_cr)
    pos = jnp.stack([lax.axis_index("inline"), lax.axis_index("crosslin")]).astype(jnp.int32)
    col_first, col_last, local = pack_columns(amplitudes, iterate, mask, depth)
    left, right = neighbours(col_first, col_last, "crosslin", n_cr)
    cuts = ((1, 7), (8, 7))
    *inner, lines = inner_stage(*cuts[0], local, (iterate, mask, depth, rows))
    (left, right), lines = lax.optimization_barrier(((left, right), lines))
    row_first, row_last = pack_rows(lines, left, right, mix, lanes)
    up, down = neighbours(row_first, row_last, "inline", n_in)
    inner += inner_stage(*cuts[1], local)
    group = jnp.asarray(tables["group"])
    ta, tb, tc, z, r, rd, blocks, sums = tensor_stage(
        n_in, n_cr, cuts, pos, local, iterate, mask, depth, up, down, left, right, put, group, inner
    )

    def moments_of(payload, extra):
        gathered = lax.all_to_all(payload, "crosslin", 0, 0, tiled=True)
        pay, own = moments_stage(n_in, n_cr, extra, gathered, *tables["forward"], tables["steps"])
        return lax.all_to_all(pay, "inline", 0, 0, tiled=True), own

    flat = jax.ShapeDtypeStruct((RD, CD), F32)
    cs = VMEM((40, EC), F32)
    moments, own = moments_of(blocks, False)
    p, q, payload = coarse_call(
        image_kernel, n_in, n_cr, "image_stage",
        [flat, flat, jax.ShapeDtypeStruct((n_cr, CR + 8, CC), F32)],
        [VMEM((CR, CD), F32), cs],
        pos, moments, own, tables, [ta, tb, tc, z, rd, mask, blocks, sums], group,
    )
    moments, own = moments_of(payload, True)
    return tuple(
        coarse_call(
            final_kernel, n_in, n_cr, "final_stage", [flat, flat, flat], [cs],
            pos, moments, own, tables, [p, q, r, rd, iterate],
        )
    )


def solution(mesh):
    n_in, n_cr = mesh.shape["inline"], mesh.shape["crosslin"]
    flat = P("inline", "crosslin")
    return jax.shard_map(
        functools.partial(per_device, n_in, n_cr), mesh=mesh,
        in_specs=(P(None, "inline", "crosslin"), flat, flat, flat),
        out_specs=(flat, flat, flat), check_vma=False,
    )
```

```python
import functools

import jax
import jax.numpy as jnp
import ml_dtypes
import numpy as np
from jax import lax
from jax.experimental import pallas as pl
from jax.experimental.pallas import tpu as pltpu
from jax.sharding import PartitionSpec as P

K = 16
DEC = 8
CI = 32
COUPLING = 4.0
F32 = jnp.float32
BF16 = jnp.bfloat16
NPB = ml_dtypes.bfloat16
VMEM = pltpu.VMEM

RD = 256
CD = 1024
ER = RD + 32
EC = CD + 128
CR = RD // DEC
CC = CD // DEC
MSG = 64


def in_hbm(x):
    return pltpu.with_memory_space_constraint(x, pltpu.HBM)


def dot(a, b):
    return jnp.dot(a, b, preferred_element_type=F32)


def parts2(x):
    hi = x.astype(BF16)
    return hi, (x - hi.astype(F32)).astype(BF16)


def parts3(x):
    hi = x.astype(BF16)
    rest = x - hi.astype(F32)
    mid = rest.astype(BF16)
    return hi, mid, (rest - mid.astype(F32)).astype(BF16)


def np2(x):
    hi = x.astype(np.float32).astype(NPB)
    return hi, (x - hi.astype(np.float64)).astype(np.float32).astype(NPB)


def line_tables():
    rows = np.zeros((2, MSG, 256), np.float32)
    put = np.zeros((2, 304, MSG), np.float32)
    for s in range(K):
        for k in range(3):
            rows[0, 3 * s + k, 16 * s + k] = 1
            rows[1, 3 * s + k, 16 * s + 13 + k] = 1
    for side in range(2):
        put[side, :256] = rows[side].T
        for l in range(2):
            for part in range(3):
                put[side, 256 + (14 + l if side else l), 48 + 3 * l + part] = 1
        put[side, 272 + (15 if side else 0), 54] = 1
        put[side, 288 + (15 if side else 0), 55] = 1
    mix = np.zeros((2, 3, MSG, 128), np.float32)
    for k in range(3):
        for s in range(K):
            mix[:, k, 3 * s + k, 3 * s : 3 * s + 3] = 1
    for l in range(2):
        for part in range(3):
            for other in range(2):
                mix[0, l, 48 + 3 * l + part, 48 + 3 * other + part] = 1
                mix[1, l + 1, 48 + 3 * l + part, 48 + 3 * other + part] = 1
    for o in (54, 55):
        mix[0, 0, o, o] = 1
        mix[1, 2, o, o] = 1
    lanes = np.zeros((2, 128, 128), np.float32)
    for s in range(K):
        for k in range(3):
            lanes[0, 3 * s + k, k] = 1
            lanes[1, 3 * s + k, 125 + k] = 1
    for l in range(2):
        for part in range(3):
            lanes[0, 48 + 3 * l + part, l] = 1
            lanes[1, 48 + 3 * l + part, 126 + l] = 1
    for o in (54, 55):
        lanes[0, o, 0] = 1
        lanes[1, o, 127] = 1
    return tuple(t.astype(NPB) for t in (rows, put, mix, lanes))


def coarse_tables(n_in, n_cr):
    n = CC * n_cr
    freq = np.arange(n, dtype=np.float64)
    norm = np.where(freq == 0, np.sqrt(1.0 / n), np.sqrt(2.0 / n))

    def cosines(cols):
        phase = (freq[:, None] * (2 * cols[None, :] + 1)) % (4 * n)
        return norm[:, None] * np.cos(np.pi * phase / (2 * n))

    lead = np.arange(n + CC, dtype=np.float64) - 16
    forward = cosines(lead).T * (lead[:, None] >= -1) * (lead[:, None] <= n)
    half = (2.0 - 2.0 * np.cos(np.pi * freq / n) + 1.0 / (CI * CI)) / 2.0
    kappa = np.log1p(half + np.sqrt(half * (half + 2.0)))
    scale = 1.0 / (COUPLING * 2.0 * np.sinh(kappa))
    steps = np.stack([np.exp(-kappa * d) for d in (1, 2, 4, 8, 16)] + [scale] + [scale * 0] * 2)
    at = np.arange(40)[:, None]
    grow = scale * np.exp(-kappa * at) * (at < 34)
    fall = scale * np.exp(-kappa * (33.0 - at)) * (at < 34)
    whole = CR * n_in
    blocks = np.stack(
        [
            np.exp(-kappa * CR),
            np.exp(-kappa * whole),
            1.0 / (1.0 - np.exp(-kappa * 2 * whole)),
            scale * np.exp(-kappa),
        ]
    ).reshape(4, n_cr, 128)
    spread = np.zeros((2 * CC, EC))
    for lane in range(EC):
        col = ((lane if lane >= 64 else lane + EC) - 128) // DEC
        if -1 <= col <= CC:
            spread[16 + col, lane] = 1
    group = np.zeros((CD, CC))
    group[np.arange(CD), np.arange(CD) // DEC] = 1
    f = np.float32
    return dict(
        forward=np2(forward), steps=steps.astype(f), grow=grow.astype(f),
        fall=fall.astype(f), blocks=blocks.astype(f), spread=spread.astype(NPB), group=group.astype(NPB),
    )


def moved(x, lane, to):
    turn = (to - lane) % x.shape[1]
    return pltpu.roll(x, turn, 1) if turn else x


def pack_columns_kernel(amp, v_in, m_in, d_in, out0, out1, amp_o, v, m, d, sems, rest_sem):
    copies = []
    for side, at in enumerate((0, CD - 128)):
        span = pl.ds(at, 128)
        copies.append(pltpu.make_async_copy(amp.at[:, :, span], amp_o.at[:, :, span], sems.at[side, 0]))
        copies.append(pltpu.make_async_copy(v_in.at[:, span], v.at[side], sems.at[side, 1]))
        copies.append(pltpu.make_async_copy(m_in.at[:, span], m.at[side], sems.at[side, 2]))
        copies.append(pltpu.make_async_copy(d_in.at[:, span], d.at[side], sems.at[side, 3]))
    middle = pl.ds(128, CD - 256)
    rest = pltpu.make_async_copy(amp.at[:, :, middle], amp_o.at[:, :, middle], rest_sem)
    for c in copies:
        c.start()
    rest.start()
    lane = lax.broadcasted_iota(jnp.int32, (RD, 128), 1)
    for c in copies:
        c.wait()
    for side, out in enumerate((out0, out1)):
        low = 125 if side else 0

        def edge(s, side=side):
            return amp_o[s, :, CD - 128 :] if side else amp_o[s, :, 0:128]

        weight = m[side].astype(F32)
        source = weight * (d[side].astype(F32) - 0.5 * (K - 1))
        end = 127 if side else 0
        total = jnp.where(lane == 54, moved(weight, end, 54), moved(source, end, 55))
        for part, value in enumerate(parts3(v[side])):
            value = value.astype(F32)
            for l in range(2):
                to = 48 + 3 * l + part
                total = jnp.where(lane == to, moved(value, (126 if side else 0) + l, to), total)
        for s in range(K):
            total = jnp.where((lane >= 3 * s) & (lane < 3 * s + 3), moved(edge(s).astype(F32), low, 3 * s), total)
        out[...] = jnp.where(lane < 56, total, 0.0).astype(BF16)
    rest.wait()


def pack_columns(amplitudes, iterate, mask, depth):
    hbm = pl.BlockSpec(memory_space=pltpu.HBM)
    out = jax.ShapeDtypeStruct((RD, 128), BF16)
    return pl.pallas_call(
        pack_columns_kernel, in_specs=[hbm] * 4,
        out_specs=[pl.BlockSpec(memory_space=VMEM)] * 3,
        out_shape=[out, out, jax.ShapeDtypeStruct((K, RD, CD), BF16)],
        scratch_shapes=[
            VMEM((2, RD, 128), F32), VMEM((2, RD, 128), jnp.int32),
            VMEM((2, RD, 128), jnp.int32), pltpu.SemaphoreType.DMA((2, 4)), pltpu.SemaphoreType.DMA,
        ],
        compiler_params=pltpu.CompilerParams(vmem_limit_bytes=12 * 1024 * 1024),
        cost_estimate=pl.CostEstimate(flops=10**7, bytes_accessed=3 * 10**6, transcendentals=0),
        name="pack_columns",
    )(*(in_hbm(x) for x in (amplitudes, iterate, mask, depth)))


def pack_rows_kernel(lines, left, right, mix, lanes, out0, out1):
    for side, out in enumerate((out0, out1)):
        out[:, 128:] = lines[side]
        total = jnp.zeros((MSG, 128), F32)
        for halo, which in ((left, 1), (right, 0)):
            edge = halo[RD - 16 : RD].astype(F32)[13:16] if side else halo[0:16].astype(F32)[0:3]
            for k in range(3):
                term = mix[side, k].astype(F32) * edge[k : k + 1]
                total += dot(term.astype(BF16), lanes[which])
        out[:, 0:128] = total.astype(BF16)


def pack_rows(lines, left, right, mix, lanes):
    vmem = pl.BlockSpec(memory_space=VMEM)
    out = jax.ShapeDtypeStruct((MSG, EC), BF16)
    return pl.pallas_call(
        pack_rows_kernel, in_specs=[vmem] * 5, out_specs=[vmem] * 2, out_shape=[out, out],
        compiler_params=pltpu.CompilerParams(vmem_limit_bytes=12 * 1024 * 1024),
        cost_estimate=pl.CostEstimate(flops=10**7, bytes_accessed=10**6, transcendentals=0),
        name="pack_rows",
    )(lines, left, right, mix, lanes)


def row_band(rows, window, lead):
    at = lax.broadcasted_iota(jnp.int32, (rows, window), 0) + lead
    to = lax.broadcasted_iota(jnp.int32, (rows, window), 1)
    return jnp.where(to == at + 1, 1.0, jnp.where(to == at - 1, -1.0, 0.0)).astype(BF16)


def gradient_sums(window, band, span, off, take):
    total = None
    for s in range(K):
        x = window(s)
        n = x.shape[1]
        middle = x[span]
        gc = pltpu.roll(middle, n - 1, 1).astype(F32) - pltpu.roll(middle, 1, 1).astype(F32)
        gc = gc[:, off : off + take]
        gi = dot(band, x[:, off : off + take])
        terms = (gi * gi, gi * gc, gc * gc)
        total = terms if total is None else tuple(t + u for t, u in zip(total, terms))
    return total


def edge_lines(side, a, v, m, d, rows):
    at = lax.broadcasted_iota(jnp.int32, (MSG, CD), 0)
    middle = dot(rows[side], a.reshape(K * 16, CD))
    split = [p.astype(F32) for p in parts3(v)]
    for l in range(2):
        row = 6 + l if side else l
        for part in range(3):
            middle = jnp.where(at == 48 + 3 * l + part, split[part][row : row + 1], middle)
    row = 7 if side else 0
    weight = m[row : row + 1].astype(F32)
    source = weight * (d[row : row + 1].astype(F32) - 0.5 * (K - 1))
    return jnp.where(at == 54, weight, jnp.where(at == 55, source, middle)).astype(BF16)


def inner_kernel(first, steps, edge, amp, *rest):
    if edge:
        v_in, m_in, d_in, rows_t, sii_o, sic_o, scc_o, edge_o, lines_o, v, m, d, end_sems = rest
    else:
        sii_o, sic_o, scc_o, edge_o, local, sems = rest
    base = 16 * (first - 1)
    skip = 0 if edge else 128 - base
    bounds = [] if edge else [(0, 48), (48, 48), (96, 16 * (steps + 2) - 96)]
    copies = [
        pltpu.make_async_copy(amp.at[:, pl.ds(base + r, n)], local.at[:, pl.ds(r, n)], sems.at[i])
        for i, (r, n) in enumerate(bounds)
    ]
    for c in copies:
        c.start()
    if not edge:
        amp, base = local, 0
    if edge:
        more = []
        for side in range(2):
            for i, (source, to) in enumerate(((v_in, v), (m_in, m), (d_in, d))):
                span = pl.ds(side * (RD - 8), 8)
                more.append(pltpu.make_async_copy(source.at[span], to.at[side], end_sems.at[3 * side + i]))
        for c in more:
            c.start()
    lane = lax.broadcasted_iota(jnp.int32, (16, 128), 1)
    band = row_band(16, 48, 16)

    def step(t, carry):
        at = pl.multiple_of(16 * t, 16)
        window = pl.ds(pl.multiple_of(base + 16 * t, 16), 48)
        for part in range(2):
            lanes = slice(0, 640) if part == 0 else slice(384, CD)
            off = 0 if part == 0 else 128
            sums = gradient_sums(lambda s: amp[s, window, lanes], band, slice(16, 32), off, 512)
            for o, value in zip((sii_o, sic_o, scc_o), sums):
                o[pl.ds(at, 16), 512 * part : 512 * part + 512] = value
        return carry

    def edges(t, carry):
        at = pl.ds(pl.multiple_of(16 * t, 16), 16)
        source = pl.ds(pl.multiple_of(16 * t + skip, 16), 16)
        for s in range(K):
            low = moved(amp[s, source, 0:128].astype(F32), 0, 35)
            high = moved(amp[s, source, CD - 128 : CD].astype(F32), 125, 64)
            tile = jnp.where((lane >= 35) & (lane < 38), low, jnp.where((lane >= 64) & (lane < 67), high, 0.0))
            edge_o[s, at, :] = tile.astype(BF16)
        return carry

    done = 0
    for i, (r, n) in enumerate(bounds):
        copies[i].wait()
        until = min(steps, (r + n) // 16 - 2)
        lax.fori_loop(done, until, step, 0)
        done = until
    lax.fori_loop(done, steps, step, 0)
    lax.fori_loop(0, 8, edges, 0, unroll=4)
    if edge:
        for c in more:
            c.wait()
        lines_o[0] = edge_lines(0, amp[:, 0:16, :], v[0], m[0], d[0], rows_t)
        lines_o[1] = edge_lines(1, amp[:, RD - 16 :, :], v[1], m[1], d[1], rows_t)


def inner_stage(first, steps, amplitudes, more=()):
    hbm, vmem = pl.BlockSpec(memory_space=pltpu.HBM), pl.BlockSpec(memory_space=VMEM)
    flat = jax.ShapeDtypeStruct((16 * steps, CD), F32)
    out_shape = [flat, flat, flat, jax.ShapeDtypeStruct((K, 128, 128), BF16)]
    scratch = [] if more else [VMEM((K, 16 * (steps + 2), CD), BF16), pltpu.SemaphoreType.DMA((3,))]
    in_specs = [vmem if more else hbm]
    if more:
        out_shape += [jax.ShapeDtypeStruct((2, MSG, CD), BF16)]
        scratch += [
            VMEM((2, 8, CD), F32), VMEM((2, 8, CD), jnp.int32), VMEM((2, 8, CD), jnp.int32),
            pltpu.SemaphoreType.DMA((6,)),
        ]
        in_specs += [hbm, hbm, hbm, vmem]
    return pl.pallas_call(
        functools.partial(inner_kernel, first, steps, bool(more)),
        in_specs=in_specs, out_specs=[vmem] * len(out_shape), out_shape=out_shape, scratch_shapes=scratch,
        compiler_params=pltpu.CompilerParams(vmem_limit_bytes=14 * 1024 * 1024),
        cost_estimate=pl.CostEstimate(flops=10**8, bytes_accessed=6 * 10**6, transcendentals=0),
        name="inner_stage",
    )(amplitudes if more else in_hbm(amplitudes), *(in_hbm(x) for x in more[:3]), *more[3:])


def block_sums(rows, group):
    return sum(dot(part, group) for part in parts3(rows))


def tensor_kernel(
    n_in, n_cr, cuts, pos, amp, v_in, mask, depth, up, down, left, right, put, group, *rest
):
    inner_refs, rest = rest[: 4 * len(cuts)], rest[4 * len(cuts) :]
    (ta_o, tb_o, tc_o, z_o, r_o, rd_o, blocks_o, sums_o,
     tops, rim, rim_sums, v_ext, w_ext, s_ext, fd, fr, rowsum, sems) = rest
    inner = (slice(16, 16 + RD), slice(128, EC))
    copies = [
        pltpu.make_async_copy(amp.at[:, 0:32], tops.at[0, :, 16:48, 128:EC], sems.at[0]),
        pltpu.make_async_copy(amp.at[:, RD - 32 : RD], tops.at[1, :, 0:32, 128:EC], sems.at[1]),
        pltpu.make_async_copy(v_in, v_ext.at[16 : 16 + RD, 128:EC], sems.at[2]),
    ]
    for c in copies:
        c.start()
    weight = mask[...].astype(F32)
    w_ext[inner] = weight
    s_ext[inner] = weight * (depth[...].astype(F32) - 0.5 * (K - 1))
    lane = lax.broadcasted_iota(jnp.int32, (RD, 128), 1)
    before, after = left[...].astype(F32), right[...].astype(F32)
    here = slice(16, 16 + RD)
    value = jnp.zeros((RD, 128), F32)
    for l in range(2):
        for halo, to in ((before, 126 + l), (after, l)):
            got = sum(moved(halo, 48 + 3 * l + part, to) for part in range(3))
            value = jnp.where(lane == to, got, value)
    v_ext[here, 0:128] = value
    for o, message in ((w_ext, 54), (s_ext, 55)):
        value = jnp.where(lane == 127, moved(before, message, 127), 0.0)
        o[here, 0:128] = jnp.where(lane == 0, moved(after, message, 0), value)
    for s in range(K):
        value = jnp.where(lane < 3, moved(after, 3 * s, 0), 0.0)
        value = jnp.where(lane >= 125, moved(before, 3 * s, 125), value).astype(BF16)
        tops[0, s, 16:48, 0:128] = value[0:32]
        tops[1, s, 0:32, 0:128] = value[RD - 32 : RD]
    for c in range(2):
        span = slice(128 * c, 128 * c + 128)
        turned, turned_after, tile = before[span], after[span], lane[span]
        for s in range(K):
            value = inner_refs[4 * c + 3][s].astype(F32)
            value = jnp.where((tile >= 32) & (tile < 35), moved(turned, 3 * s, 32), value)
            value = jnp.where((tile >= 67) & (tile < 70), moved(turned_after, 3 * s, 67), value)
            rim[s, span, :] = value.astype(BF16)
    for side, halo, row in ((1, up, 0), (0, down, 16 + RD)):
        lines = dot(put[side], halo[...])
        for s in range(K):
            tops[1 - side, s, 32 - 32 * side : 48 - 32 * side, :] = lines[16 * s : 16 * s + 16].astype(BF16)
        v_ext[row : row + 16, :] = lines[256:272]
        w_ext[row : row + 16, :] = lines[272:288]
        s_ext[row : row + 16, :] = lines[288:304]
    for c in copies:
        c.wait()
    at_lane = lax.broadcasted_iota(jnp.int32, (1, EC), 1)
    col = pos[1] * CD + jnp.where(at_lane < 64, at_lane + CD, at_lane - 128)
    valid_right = ((col >= 0) & (col < n_cr * CD - 1)).astype(F32)
    row_iota = lax.broadcasted_iota(jnp.int32, (16, 1), 0)
    tile_lane = lax.broadcasted_iota(jnp.int32, (16, 128), 1)

    def left_of(x):
        return pltpu.roll(x, 1, 1)

    def right_of(x):
        return pltpu.roll(x, EC - 1, 1)

    def finish(at, sums):
        sii, sic, scc = (0.25 * x for x in sums)
        inv = 1.0 / (sii + scc + 2.0)
        row = pos[0] * RD - 16 + at + row_iota
        valid_down = ((row >= 0) & (row < n_in * RD - 1)).astype(F32)
        ta = valid_down * ((scc + 1.0) * inv)
        tb = (valid_down * valid_right) * (-sic * inv)
        tc = valid_right * ((sii + 1.0) * inv)
        value = v_ext[pl.ds(at, 24), :]
        here = value[0:16]
        dd = value[1:17] - here
        dr = right_of(here) - here
        to = pl.ds(at, 16)
        ta_o[to, :] = ta
        tb_o[to, :] = tb
        tc_o[to, :] = tc
        fd[to, :] = ta * dd + tb * dr
        fr[to, :] = tb * dd + tc * dr

    for side in range(2):
        for half in range(2):
            lead = 16 * (side + half)
            sums = gradient_sums(
                lambda s, side=side: tops[side, s], row_band(16, 48, lead), slice(lead, lead + 16), 0, EC
            )
            finish((RD if side else 0) + 16 * half, sums)

    wide = row_band(32, 64, 16)

    def rim_step(t, carry):
        at = pl.multiple_of(32 * t, 32)
        edge = gradient_sums(lambda s: rim[s, pl.ds(at, 64), :], wide, slice(16, 48), 0, 128)
        for i, e in enumerate(edge):
            rim_sums[i, pl.ds(pl.multiple_of(at + 16, 16), 32), :] = e
        return carry

    lax.fori_loop(0, RD // 32 - 1, rim_step, 0, unroll=7)

    for c, (first, steps) in enumerate(cuts):
        sii, sic, scc = inner_refs[4 * c : 4 * c + 3]

        def step(t, carry, sii=sii, sic=sic, scc=scc, first=first):
            local = pl.ds(pl.multiple_of(16 * (t - first), 16), 16)
            at = pl.ds(pl.multiple_of(16 * t, 16), 16)
            sums = []
            for ref, e in zip((sii, sic, scc), (rim_sums[i, at, :] for i in range(3))):
                low, high = pltpu.roll(e, 93, 1), pltpu.roll(e, 61, 1)
                x = ref[local, :]
                sums.append(
                    jnp.concatenate(
                        [
                            jnp.where(tile_lane < 64, high, low),
                            jnp.where(tile_lane == 0, low, x[:, 0:128]),
                            x[:, 128 : CD - 128],
                            jnp.where(tile_lane == 127, high, x[:, CD - 128 :]),
                        ],
                        axis=1,
                    )
                )
            finish(pl.multiple_of(16 * t + 16, 16), sums)
            return carry

        lax.fori_loop(first, first + steps, step, 0, unroll=7)

    def residuals(at, n):
        before = pl.ds(pl.multiple_of(at - 8, 8), n + 8)
        here = pl.ds(at, n)
        fdw, taw = fd[before, :], ta_o[before, :]
        tc, right_flux, weight = tc_o[here, :], fr[here, :], w_ext[here, :]
        image = fdw[7 : n + 7] - fdw[8 : n + 8] + left_of(right_flux) - right_flux + weight * v_ext[here, :]
        r = s_ext[here, :] - image
        diag = taw[8 : n + 8] + 2.0 * tb_o[here, :] + tc + taw[7 : n + 7] + left_of(tc) + weight
        inv = jnp.where(diag != 0.0, 1.0 / diag, 0.0)
        z = r * inv
        z_o[here, :] = z
        return r, inv, z

    def own(e, total):
        at = pl.multiple_of(16 + 16 * e, 16)
        r, inv, z = (x[:, 128:] for x in residuals(at, 16))
        to = pl.ds(pl.multiple_of(16 * e, 16), 16)
        r_o[to, :] = r
        rd_o[to, :] = inv
        rowsum[pl.ds(2 * e, 1), :] = jnp.sum(r[0:8], axis=0, keepdims=True)
        rowsum[pl.ds(2 * e + 1, 1), :] = jnp.sum(r[8:16], axis=0, keepdims=True)
        rz = r * z
        rz = rz[0:8] + rz[8:16]
        return total + sum(rz[:, k * 128 : k * 128 + 128] for k in range(CD // 128))

    residuals(8, 8)
    residuals(16 + RD, 8)
    sums_o[...] = lax.fori_loop(0, RD // 16, own, jnp.zeros((8, 128), F32), unroll=4)
    sums = block_sums(rowsum[...], group[...])
    for j in range(n_cr):
        blocks_o[j] = sums


def tensor_stage(n_in, n_cr, cuts, pos, amp, v, mask, depth, up, down, left, right, put, group, sums):
    vmem = pl.BlockSpec(memory_space=VMEM)
    hbm = pl.BlockSpec(memory_space=pltpu.HBM)
    ext = jax.ShapeDtypeStruct((ER, EC), F32)
    flat = jax.ShapeDtypeStruct((RD, CD), F32)
    return pl.pallas_call(
        functools.partial(tensor_kernel, n_in, n_cr, cuts),
        in_specs=[pl.BlockSpec(memory_space=pltpu.SMEM), hbm, hbm] + [vmem] * (8 + len(sums)),
        out_specs=[vmem] * 8,
        out_shape=[
            ext, ext, ext, ext, flat, flat,
            jax.ShapeDtypeStruct((n_cr, CR, CC), F32),
            jax.ShapeDtypeStruct((8, 128), F32),
        ],
        scratch_shapes=[
            VMEM((2, K, 48, EC), BF16), VMEM((K, RD, 128), BF16), VMEM((3, RD, 128), F32), VMEM((ER + 8, EC), F32), VMEM((ER, EC), F32),
            VMEM((ER, EC), F32), VMEM((ER, EC), F32), VMEM((ER, EC), F32), VMEM((CR, CD), F32),
            pltpu.SemaphoreType.DMA((3,)),
        ],
        compiler_params=pltpu.CompilerParams(vmem_limit_bytes=28 * 1024 * 1024),
        cost_estimate=pl.CostEstimate(flops=10**8, bytes_accessed=2 * 10**7, transcendentals=0),
        name="tensor_stage",
    )(pos, in_hbm(amp), in_hbm(v), mask, depth, up, down, left, right, put, group, *sums)


def moments_kernel(n_in, n_cr, extra, blocks, fwd_hi, fwd_lo, steps, pay_o, own_o):
    x = jnp.concatenate([blocks[j, :CR] for j in range(n_cr)], axis=1)
    hi, lo = parts2(x)
    span = slice(16, 16 + x.shape[1])
    both = dot(jnp.concatenate([hi, lo], axis=0), fwd_hi[span, :])
    x = both[:CR] + both[CR:] + dot(hi, fwd_lo[span, :])
    width = x.shape[1]
    forth, back = x, x
    for i in range(5):
        d = 1 << i
        zero = jnp.zeros((d, width), F32)
        decay = steps[i : i + 1]
        forth = forth + decay * jnp.concatenate([zero, forth[:-d]], axis=0)
        back = back + decay * jnp.concatenate([back[d:], zero], axis=0)
    decay, scale = steps[0:1], steps[5:6]
    zero = jnp.zeros((1, width), F32)
    inside = forth + decay * jnp.concatenate([back[1:], zero], axis=0)
    inside = scale * inside
    own_o[...] = jnp.concatenate(
        [scale * decay * back[0:1], inside, scale * decay * forth[CR - 1 :], jnp.zeros((6, width), F32)],
        axis=0,
    )
    f = jnp.concatenate([forth[CR - 1 :, 128 * k : 128 * k + 128] for k in range(n_cr)], axis=0)
    b = jnp.concatenate([back[0:1, 128 * k : 128 * k + 128] for k in range(n_cr)], axis=0)
    for i in range(n_in):
        pay_o[i, 0:n_cr] = f
        pay_o[i, n_cr : 2 * n_cr] = b
    if extra:
        sums = sum(blocks[j, CR : CR + 8] for j in range(n_cr))
        energy = jnp.sum(x * inside, axis=0, keepdims=True)
        energy = sum(energy[:, 128 * k : 128 * k + 128] for k in range(n_cr))
        at = lax.broadcasted_iota(jnp.int32, (8, 128), 0)
        sums = jnp.where(at == 3, energy, sums)
        for i in range(n_in):
            pay_o[i, 2 * n_cr : 2 * n_cr + 8] = sums


def moments_stage(n_in, n_cr, extra, blocks, fwd_hi, fwd_lo, steps):
    vmem = pl.BlockSpec(memory_space=VMEM)
    return pl.pallas_call(
        functools.partial(moments_kernel, n_in, n_cr, extra),
        in_specs=[vmem] * 4, out_specs=[vmem] * 2,
        out_shape=[
            jax.ShapeDtypeStruct((n_in, 2 * n_cr + 8 * extra, 128), F32),
            jax.ShapeDtypeStruct((40, CC * n_cr), F32),
        ],
        compiler_params=pltpu.CompilerParams(vmem_limit_bytes=12 * 1024 * 1024),
        cost_estimate=pl.CostEstimate(flops=2 * 10**8, bytes_accessed=5 * 10**6, transcendentals=0),
        name="moments_stage",
    )(blocks, fwd_hi, fwd_lo, steps)


def coarse_values(n_in, n_cr, pos, moments, own, grow, fall, blocks, fwd_hi, fwd_lo, spread):
    mine = pos[0]
    r32, whole, series, link = (blocks[i] for i in range(4))
    f = [moments[i, 0:n_cr] for i in range(n_in)]
    b = [moments[i, n_cr : 2 * n_cr] for i in range(n_in)]
    hf, hb = f[0], b[n_in - 1]
    for i in range(1, n_in):
        hf = r32 * hf + f[i]
        hb = r32 * hb + b[n_in - 1 - i]
    above = (hb + whole * hf) * series
    below = (hf + whole * hb) * series
    mine_above, mine_below = jnp.zeros_like(above), jnp.zeros_like(below)
    energy = jnp.zeros_like(above)
    for i in range(n_in):
        k = n_in - 1 - i
        mine_above = jnp.where(mine == i, above, mine_above)
        mine_below = jnp.where(mine == k, below, mine_below)
        energy += above * b[i] + below * f[k]
        above = r32 * above + f[i]
        below = r32 * below + b[k]
    energy = energy * link
    a_row = jnp.concatenate([mine_above[k : k + 1] for k in range(n_cr)], axis=1)
    b_row = jnp.concatenate([mine_below[k : k + 1] for k in range(n_cr)], axis=1)
    u = own[...] + a_row * grow[...] + b_row * fall[...]
    hi, lo = parts2(u)
    span = pl.ds(pl.multiple_of(pos[1] * CC, CC), 2 * CC)
    turned = (((1,), (1,)), ((), ()))
    both = lax.dot_general(jnp.concatenate([hi, lo], axis=0), fwd_hi[span, :], turned, preferred_element_type=F32)
    values = both[:40] + both[40:] + lax.dot_general(hi, fwd_lo[span, :], turned, preferred_element_type=F32)
    three = dot(jnp.concatenate(parts3(values), axis=0), spread[...])
    return values, three[:40] + three[40:80] + three[80:], energy


def image_kernel(
    n_in, n_cr, pos, moments, own, grow, fall, blocks, fwd_hi, fwd_lo, spread, group,
    ta, tb, tc, z, rd, mask, first_blocks, first_sums,
    p_o, q_o, blocks_o, rowsum, cs,
):
    values, spread_rows, _ = coarse_values(
        n_in, n_cr, pos, moments, own, grow, fall, blocks, fwd_hi, fwd_lo, spread
    )
    cs[...] = spread_rows

    def field(strip):
        at = pl.ds(pl.multiple_of(8 + 8 * strip, 8), 8)
        return z[at, :] + cs[pl.ds(strip, 1), :]

    def fluxes(at, n, value):
        here = value[0:n]
        dd = value[1 : n + 1] - here
        dr = pltpu.roll(here, EC - 1, 1) - here
        at = pl.ds(at, n)
        b = tb[at, :]
        return ta[at, :] * dd + b * dr, b * dd + tc[at, :] * dr

    def images(e, carry):
        pq, qq, strip, above = carry
        following = [field(2 * e + 2), field(2 * e + 3)]
        value = jnp.concatenate([strip] + following, axis=0)
        down, side = fluxes(pl.multiple_of(16 + 16 * e, 16), 16, value)
        flux = jnp.concatenate([above[7:8], down[0:15]], axis=0) - down + pltpu.roll(side, 1, 1) - side
        to = pl.ds(pl.multiple_of(16 * e, 16), 16)
        p = value[0:16, 128:]
        q = flux[:, 128:] + mask[to, :].astype(F32) * p
        p_o[to, :] = p
        q_o[to, :] = q
        rowsum[pl.ds(2 * e, 1), :] = jnp.sum(q[0:8], axis=0, keepdims=True)
        rowsum[pl.ds(2 * e + 1, 1), :] = jnp.sum(q[8:16], axis=0, keepdims=True)
        return pq + folded(p * q), qq + folded(q * q * rd[to, :]), following[1], down[8:16]

    def folded(x):
        x = x[0:8] + x[8:16]
        return sum(x[:, k * 128 : k * 128 + 128] for k in range(CD // 128))

    strip = field(1)
    above, _ = fluxes(8, 8, jnp.concatenate([field(0), strip], axis=0))
    zero = jnp.zeros((8, 128), F32)
    pq, qq, _, _ = lax.fori_loop(0, RD // 16, images, (zero, zero, strip, above), unroll=4)

    def lanes(x):
        return jnp.sum(x, axis=0, keepdims=True)

    rp = jnp.sum(first_sums[...], axis=0, keepdims=True)
    rp += jnp.sum(first_blocks[0] * pltpu.roll(values, 2 * CC - 16, 1)[1 : CR + 1, :CC], axis=0, keepdims=True)
    tail = jnp.concatenate([rp, lanes(pq), lanes(qq), jnp.zeros((5, 128), F32)], axis=0)
    sums = block_sums(rowsum[...], group[...])
    for j in range(n_cr):
        blocks_o[j, 0:CR] = sums
        blocks_o[j, CR : CR + 8] = tail


def final_kernel(
    n_in, n_cr, pos, moments, own, grow, fall, blocks, fwd_hi, fwd_lo, spread,
    p_in, q_in, r_in, rd, v_in, v_o, r_o, d_o, cs,
):
    _, spread_rows, energy = coarse_values(
        n_in, n_cr, pos, moments, own, grow, fall, blocks, fwd_hi, fwd_lo, spread
    )
    cs[...] = spread_rows
    sums = sum(moments[i, 2 * n_cr : 2 * n_cr + 8] for i in range(n_in))
    old = jnp.sum(sums[0:1], axis=1, keepdims=True)
    curvature = jnp.sum(sums[1:2], axis=1, keepdims=True)
    energy = jnp.sum(jnp.sum(energy, axis=0, keepdims=True), axis=1, keepdims=True)
    image = jnp.sum(sums[2:3] + sums[3:4], axis=1, keepdims=True) + energy
    step = old / curvature
    ratio = (step * step * image - old) / old
    more = 1.0 + ratio

    def body(e, carry):
        at = pl.ds(pl.multiple_of(16 * e, 16), 16)
        p, q = p_in[at, :], q_in[at, :]
        coarse = [jnp.broadcast_to(cs[pl.ds(2 * e + k, 1), 128:], (8, CD)) for k in (1, 2)]
        coarse = jnp.concatenate(coarse, axis=0)
        v_o[at, :] = v_in[at, :] + step * p
        r_o[at, :] = r_in[at, :] - step * q
        d_o[at, :] = more * p - step * (q * rd[at, :] + coarse)
        return carry

    lax.fori_loop(0, RD // 16, body, 0, unroll=4)


def coarse_call(kernel, n_in, n_cr, name, out_shape, scratch, pos, moments, own, tables, rest, group=None):
    vmem = pl.BlockSpec(memory_space=VMEM)
    args = [moments, own, tables["grow"], tables["fall"], tables["blocks"], *tables["forward"], tables["spread"]]
    args += ([group] if group is not None else []) + list(rest)
    return pl.pallas_call(
        functools.partial(kernel, n_in, n_cr),
        in_specs=[pl.BlockSpec(memory_space=pltpu.SMEM)] + [vmem] * len(args),
        out_specs=[vmem] * len(out_shape), out_shape=out_shape, scratch_shapes=scratch,
        compiler_params=pltpu.CompilerParams(vmem_limit_bytes=22 * 1024 * 1024),
        cost_estimate=pl.CostEstimate(flops=10**8, bytes_accessed=10**7, transcendentals=0),
        name=name,
    )(pos, *args)


def neighbours(value_low, value_high, axis, count):
    ahead = [(i, i + 1) for i in range(count - 1)]
    behind = [(j, i) for i, j in ahead]
    return lax.ppermute(value_high, axis, ahead), lax.ppermute(value_low, axis, behind)


def per_device(n_in, n_cr, amplitudes, mask, depth, iterate):
    rows, put, mix, lanes = (jnp.asarray(t) for t in line_tables())
    tables = coarse_tables(n_in, n_cr)
    pos = jnp.stack([lax.axis_index("inline"), lax.axis_index("crosslin")]).astype(jnp.int32)
    col_first, col_last, local = pack_columns(amplitudes, iterate, mask, depth)
    left, right = neighbours(col_first, col_last, "crosslin", n_cr)
    cuts = ((1, 7), (8, 7))
    *inner, lines = inner_stage(*cuts[0], local, (iterate, mask, depth, rows))
    (left, right), lines = lax.optimization_barrier(((left, right), lines))
    row_first, row_last = pack_rows(lines, left, right, mix, lanes)
    up, down = neighbours(row_first, row_last, "inline", n_in)
    inner += inner_stage(*cuts[1], amplitudes)
    group = jnp.asarray(tables["group"])
    ta, tb, tc, z, r, rd, blocks, sums = tensor_stage(
        n_in, n_cr, cuts, pos, amplitudes, iterate, mask, depth, up, down, left, right, put, group, inner
    )

    def moments_of(payload, extra):
        gathered = lax.all_to_all(payload, "crosslin", 0, 0, tiled=True)
        pay, own = moments_stage(n_in, n_cr, extra, gathered, *tables["forward"], tables["steps"])
        return lax.all_to_all(pay, "inline", 0, 0, tiled=True), own

    flat = jax.ShapeDtypeStruct((RD, CD), F32)
    cs = VMEM((40, EC), F32)
    moments, own = moments_of(blocks, False)
    p, q, payload = coarse_call(
        image_kernel, n_in, n_cr, "image_stage",
        [flat, flat, jax.ShapeDtypeStruct((n_cr, CR + 8, CC), F32)],
        [VMEM((CR, CD), F32), cs],
        pos, moments, own, tables, [ta, tb, tc, z, rd, mask, blocks, sums], group,
    )
    moments, own = moments_of(payload, True)
    return tuple(
        coarse_call(
            final_kernel, n_in, n_cr, "final_stage", [flat, flat, flat], [cs],
            pos, moments, own, tables, [p, q, r, rd, iterate],
        )
    )


def solution(mesh):
    n_in, n_cr = mesh.shape["inline"], mesh.shape["crosslin"]
    flat = P("inline", "crosslin")
    return jax.shard_map(
        functools.partial(per_device, n_in, n_cr), mesh=mesh,
        in_specs=(P(None, "inline", "crosslin"), flat, flat, flat),
        out_specs=(flat, flat, flat), check_vma=False,
    )
```

```python
import functools

import jax
import jax.numpy as jnp
import ml_dtypes
import numpy as np
from jax import lax
from jax.experimental import pallas as pl
from jax.experimental.pallas import tpu as pltpu
from jax.sharding import PartitionSpec as P

K = 16
DEC = 8
CI = 32
COUPLING = 4.0
F32 = jnp.float32
BF16 = jnp.bfloat16
NPB = ml_dtypes.bfloat16
VMEM = pltpu.VMEM

RD = 256
CD = 1024
ER = RD + 32
EC = CD + 128
CR = RD // DEC
CC = CD // DEC
MSG = 64


def in_hbm(x):
    return pltpu.with_memory_space_constraint(x, pltpu.HBM)


def dot(a, b):
    return jnp.dot(a, b, preferred_element_type=F32)


def parts2(x):
    hi = x.astype(BF16)
    return hi, (x - hi.astype(F32)).astype(BF16)


def parts3(x):
    hi = x.astype(BF16)
    rest = x - hi.astype(F32)
    mid = rest.astype(BF16)
    return hi, mid, (rest - mid.astype(F32)).astype(BF16)


def np2(x):
    hi = x.astype(np.float32).astype(NPB)
    return hi, (x - hi.astype(np.float64)).astype(np.float32).astype(NPB)


def line_tables():
    rows = np.zeros((2, MSG, 256), np.float32)
    put = np.zeros((2, 304, MSG), np.float32)
    for s in range(K):
        for k in range(3):
            rows[0, 3 * s + k, 16 * s + k] = 1
            rows[1, 3 * s + k, 16 * s + 13 + k] = 1
    for side in range(2):
        put[side, :256] = rows[side].T
        for l in range(2):
            for part in range(3):
                put[side, 256 + (14 + l if side else l), 48 + 3 * l + part] = 1
        put[side, 272 + (15 if side else 0), 54] = 1
        put[side, 288 + (15 if side else 0), 55] = 1
    mix = np.zeros((2, 3, MSG, 128), np.float32)
    for k in range(3):
        for s in range(K):
            mix[:, k, 3 * s + k, 3 * s : 3 * s + 3] = 1
    for l in range(2):
        for part in range(3):
            for other in range(2):
                mix[0, l, 48 + 3 * l + part, 48 + 3 * other + part] = 1
                mix[1, l + 1, 48 + 3 * l + part, 48 + 3 * other + part] = 1
    for o in (54, 55):
        mix[0, 0, o, o] = 1
        mix[1, 2, o, o] = 1
    lanes = np.zeros((2, 128, 128), np.float32)
    for s in range(K):
        for k in range(3):
            lanes[0, 3 * s + k, k] = 1
            lanes[1, 3 * s + k, 125 + k] = 1
    for l in range(2):
        for part in range(3):
            lanes[0, 48 + 3 * l + part, l] = 1
            lanes[1, 48 + 3 * l + part, 126 + l] = 1
    for o in (54, 55):
        lanes[0, o, 0] = 1
        lanes[1, o, 127] = 1
    return tuple(t.astype(NPB) for t in (rows, put, mix, lanes))


def coarse_tables(n_in, n_cr):
    n = CC * n_cr
    freq = np.arange(n, dtype=np.float64)
    norm = np.where(freq == 0, np.sqrt(1.0 / n), np.sqrt(2.0 / n))

    def cosines(cols):
        phase = (freq[:, None] * (2 * cols[None, :] + 1)) % (4 * n)
        return norm[:, None] * np.cos(np.pi * phase / (2 * n))

    lead = np.arange(n + CC, dtype=np.float64) - 16
    forward = cosines(lead).T * (lead[:, None] >= -1) * (lead[:, None] <= n)
    half = (2.0 - 2.0 * np.cos(np.pi * freq / n) + 1.0 / (CI * CI)) / 2.0
    kappa = np.log1p(half + np.sqrt(half * (half + 2.0)))
    scale = 1.0 / (COUPLING * 2.0 * np.sinh(kappa))
    steps = np.stack([np.exp(-kappa * d) for d in (1, 2, 4, 8, 16)] + [scale] + [scale * 0] * 2)
    at = np.arange(40)[:, None]
    grow = scale * np.exp(-kappa * at) * (at < 34)
    fall = scale * np.exp(-kappa * (33.0 - at)) * (at < 34)
    whole = CR * n_in
    blocks = np.stack(
        [
            np.exp(-kappa * CR),
            np.exp(-kappa * whole),
            1.0 / (1.0 - np.exp(-kappa * 2 * whole)),
            scale * np.exp(-kappa),
        ]
    ).reshape(4, n_cr, 128)
    spread = np.zeros((2 * CC, EC))
    for lane in range(EC):
        col = ((lane if lane >= 64 else lane + EC) - 128) // DEC
        if -1 <= col <= CC:
            spread[16 + col, lane] = 1
    group = np.zeros((CD, CC))
    group[np.arange(CD), np.arange(CD) // DEC] = 1
    f = np.float32
    return dict(
        forward=np2(forward), steps=steps.astype(f), grow=grow.astype(f),
        fall=fall.astype(f), blocks=blocks.astype(f), spread=spread.astype(NPB), group=group.astype(NPB),
    )


def moved(x, lane, to):
    turn = (to - lane) % x.shape[1]
    return pltpu.roll(x, turn, 1) if turn else x


def pack_columns_kernel(amp, v_in, m_in, d_in, out0, out1, amp_o, v, m, d, sems, rest_sem):
    copies = []
    for side, at in enumerate((0, CD - 128)):
        span = pl.ds(at, 128)
        copies.append(pltpu.make_async_copy(amp.at[:, :, span], amp_o.at[:, :, span], sems.at[side, 0]))
        copies.append(pltpu.make_async_copy(v_in.at[:, span], v.at[side], sems.at[side, 1]))
        copies.append(pltpu.make_async_copy(m_in.at[:, span], m.at[side], sems.at[side, 2]))
        copies.append(pltpu.make_async_copy(d_in.at[:, span], d.at[side], sems.at[side, 3]))
    middle = pl.ds(128, CD - 256)
    rest = [
        pltpu.make_async_copy(amp.at[:, span, middle], amp_o.at[:, span, middle], rest_sem.at[i])
        for i, span in enumerate((pl.ds(0, 144), pl.ds(RD - 16, 16)))
    ]
    for c in copies:
        c.start()
    for c in rest:
        c.start()
    lane = lax.broadcasted_iota(jnp.int32, (RD, 128), 1)
    for c in copies:
        c.wait()
    for side, out in enumerate((out0, out1)):
        low = 125 if side else 0

        def edge(s, side=side):
            return amp_o[s, :, CD - 128 :] if side else amp_o[s, :, 0:128]

        weight = m[side].astype(F32)
        source = weight * (d[side].astype(F32) - 0.5 * (K - 1))
        end = 127 if side else 0
        total = jnp.where(lane == 54, moved(weight, end, 54), moved(source, end, 55))
        for part, value in enumerate(parts3(v[side])):
            value = value.astype(F32)
            for l in range(2):
                to = 48 + 3 * l + part
                total = jnp.where(lane == to, moved(value, (126 if side else 0) + l, to), total)
        for s in range(K):
            total = jnp.where((lane >= 3 * s) & (lane < 3 * s + 3), moved(edge(s).astype(F32), low, 3 * s), total)
        out[...] = jnp.where(lane < 56, total, 0.0).astype(BF16)
    for c in rest:
        c.wait()


def pack_columns(amplitudes, iterate, mask, depth):
    hbm = pl.BlockSpec(memory_space=pltpu.HBM)
    out = jax.ShapeDtypeStruct((RD, 128), BF16)
    return pl.pallas_call(
        pack_columns_kernel, in_specs=[hbm] * 4,
        out_specs=[pl.BlockSpec(memory_space=VMEM)] * 3,
        out_shape=[out, out, jax.ShapeDtypeStruct((K, RD, CD), BF16)],
        scratch_shapes=[
            VMEM((2, RD, 128), F32), VMEM((2, RD, 128), jnp.int32),
            VMEM((2, RD, 128), jnp.int32), pltpu.SemaphoreType.DMA((2, 4)), pltpu.SemaphoreType.DMA((2,)),
        ],
        compiler_params=pltpu.CompilerParams(vmem_limit_bytes=12 * 1024 * 1024),
        cost_estimate=pl.CostEstimate(flops=10**7, bytes_accessed=3 * 10**6, transcendentals=0),
        name="pack_columns",
    )(*(in_hbm(x) for x in (amplitudes, iterate, mask, depth)))


def pack_rows_kernel(lines, left, right, mix, lanes, out0, out1):
    for side, out in enumerate((out0, out1)):
        out[:, 128:] = lines[side]
        total = jnp.zeros((MSG, 128), F32)
        for halo, which in ((left, 1), (right, 0)):
            edge = halo[RD - 16 : RD].astype(F32)[13:16] if side else halo[0:16].astype(F32)[0:3]
            for k in range(3):
                term = mix[side, k].astype(F32) * edge[k : k + 1]
                total += dot(term.astype(BF16), lanes[which])
        out[:, 0:128] = total.astype(BF16)


def pack_rows(lines, left, right, mix, lanes):
    vmem = pl.BlockSpec(memory_space=VMEM)
    out = jax.ShapeDtypeStruct((MSG, EC), BF16)
    return pl.pallas_call(
        pack_rows_kernel, in_specs=[vmem] * 5, out_specs=[vmem] * 2, out_shape=[out, out],
        compiler_params=pltpu.CompilerParams(vmem_limit_bytes=12 * 1024 * 1024),
        cost_estimate=pl.CostEstimate(flops=10**7, bytes_accessed=10**6, transcendentals=0),
        name="pack_rows",
    )(lines, left, right, mix, lanes)


def row_band(rows, window, lead):
    at = lax.broadcasted_iota(jnp.int32, (rows, window), 0) + lead
    to = lax.broadcasted_iota(jnp.int32, (rows, window), 1)
    return jnp.where(to == at + 1, 1.0, jnp.where(to == at - 1, -1.0, 0.0)).astype(BF16)


def gradient_sums(window, band, span, off, take, keep=slice(None)):
    total = None
    for s in range(K):
        x = window(s)
        n = x.shape[1]
        middle = x[span]
        gc = pltpu.roll(middle, n - 1, 1).astype(F32) - pltpu.roll(middle, 1, 1).astype(F32)
        gc = gc[keep, off : off + take]
        gi = dot(band, x[:, off : off + take])
        terms = (gi * gi, gi * gc, gc * gc)
        total = terms if total is None else tuple(t + u for t, u in zip(total, terms))
    return total


def edge_lines(side, a, v, m, d, rows):
    at = lax.broadcasted_iota(jnp.int32, (MSG, CD), 0)
    middle = dot(rows[side], a.reshape(K * 16, CD))
    split = [p.astype(F32) for p in parts3(v)]
    for l in range(2):
        row = 6 + l if side else l
        for part in range(3):
            middle = jnp.where(at == 48 + 3 * l + part, split[part][row : row + 1], middle)
    row = 7 if side else 0
    weight = m[row : row + 1].astype(F32)
    source = weight * (d[row : row + 1].astype(F32) - 0.5 * (K - 1))
    return jnp.where(at == 54, weight, jnp.where(at == 55, source, middle)).astype(BF16)


def inner_kernel(first, steps, edge, amp, *rest):
    if edge:
        v_in, m_in, d_in, rows_t, sii_o, sic_o, scc_o, edge_o, lines_o, v, m, d, end_sems = rest
    else:
        sii_o, sic_o, scc_o, edge_o, local, sems = rest
    base = 16 * (first - 1)
    skip = 0 if edge else 128 - base
    bounds = [] if edge else [(0, 48), (48, 48), (96, 16 * (steps + 2) - 96)]
    copies = [
        pltpu.make_async_copy(amp.at[:, pl.ds(base + r, n)], local.at[:, pl.ds(r, n)], sems.at[i])
        for i, (r, n) in enumerate(bounds)
    ]
    for c in copies:
        c.start()
    if not edge:
        amp, base = local, 0
    if edge:
        more = []
        for side in range(2):
            for i, (source, to) in enumerate(((v_in, v), (m_in, m), (d_in, d))):
                span = pl.ds(side * (RD - 8), 8)
                more.append(pltpu.make_async_copy(source.at[span], to.at[side], end_sems.at[3 * side + i]))
        for c in more:
            c.start()
    lane = lax.broadcasted_iota(jnp.int32, (16, 128), 1)
    band = row_band(16, 48, 16)

    def step(t, carry):
        at = pl.multiple_of(16 * t, 16)
        window = pl.ds(pl.multiple_of(base + 16 * t, 16), 48)
        for part in range(2):
            lanes = slice(0, 640) if part == 0 else slice(384, CD)
            off = 0 if part == 0 else 128
            sums = gradient_sums(lambda s: amp[s, window, lanes], band, slice(16, 32), off, 512)
            for o, value in zip((sii_o, sic_o, scc_o), sums):
                o[pl.ds(at, 16), 512 * part : 512 * part + 512] = value
        return carry

    def edges(t, carry):
        at = pl.ds(pl.multiple_of(16 * t, 16), 16)
        source = pl.ds(pl.multiple_of(16 * t + skip, 16), 16)
        for s in range(K):
            low = moved(amp[s, source, 0:128].astype(F32), 0, 35)
            high = moved(amp[s, source, CD - 128 : CD].astype(F32), 125, 64)
            tile = jnp.where((lane >= 35) & (lane < 38), low, jnp.where((lane >= 64) & (lane < 67), high, 0.0))
            edge_o[s, at, :] = tile.astype(BF16)
        return carry

    done = 0
    for i, (r, n) in enumerate(bounds):
        copies[i].wait()
        until = min(steps, (r + n) // 16 - 2)
        lax.fori_loop(done, until, step, 0)
        done = until
    lax.fori_loop(done, steps, step, 0)
    lax.fori_loop(0, 8, edges, 0, unroll=4)
    if edge:
        for c in more:
            c.wait()
        lines_o[0] = edge_lines(0, amp[:, 0:16, :], v[0], m[0], d[0], rows_t)
        lines_o[1] = edge_lines(1, amp[:, RD - 16 :, :], v[1], m[1], d[1], rows_t)


def inner_stage(first, steps, amplitudes, more=()):
    hbm, vmem = pl.BlockSpec(memory_space=pltpu.HBM), pl.BlockSpec(memory_space=VMEM)
    flat = jax.ShapeDtypeStruct((16 * steps, CD), F32)
    out_shape = [flat, flat, flat, jax.ShapeDtypeStruct((K, 128, 128), BF16)]
    scratch = [] if more else [VMEM((K, 16 * (steps + 2), CD), BF16), pltpu.SemaphoreType.DMA((3,))]
    in_specs = [vmem if more else hbm]
    if more:
        out_shape += [jax.ShapeDtypeStruct((2, MSG, CD), BF16)]
        scratch += [
            VMEM((2, 8, CD), F32), VMEM((2, 8, CD), jnp.int32), VMEM((2, 8, CD), jnp.int32),
            pltpu.SemaphoreType.DMA((6,)),
        ]
        in_specs += [hbm, hbm, hbm, vmem]
    return pl.pallas_call(
        functools.partial(inner_kernel, first, steps, bool(more)),
        in_specs=in_specs, out_specs=[vmem] * len(out_shape), out_shape=out_shape, scratch_shapes=scratch,
        compiler_params=pltpu.CompilerParams(vmem_limit_bytes=14 * 1024 * 1024),
        cost_estimate=pl.CostEstimate(flops=10**8, bytes_accessed=6 * 10**6, transcendentals=0),
        name="inner_stage",
    )(amplitudes if more else in_hbm(amplitudes), *(in_hbm(x) for x in more[:3]), *more[3:])


def block_sums(rows, group):
    return sum(dot(part, group) for part in parts3(rows))


def tensor_kernel(
    n_in, n_cr, cuts, pos, amp, v_in, mask, depth, up, down, left, right, put, group, *rest
):
    inner_refs, rest = rest[: 4 * len(cuts)], rest[4 * len(cuts) :]
    (ta_o, tb_o, tc_o, z_o, r_o, rd_o, blocks_o, sums_o,
     tops, rim, rim_sums, v_ext, w_ext, s_ext, fd, fr, rowsum, sems) = rest
    inner = (slice(16, 16 + RD), slice(128, EC))
    copies = [
        pltpu.make_async_copy(amp.at[:, 0:32], tops.at[0, :, 16:48, 128:EC], sems.at[0]),
        pltpu.make_async_copy(amp.at[:, RD - 32 : RD], tops.at[1, :, 0:32, 128:EC], sems.at[1]),
        pltpu.make_async_copy(v_in, v_ext.at[16 : 16 + RD, 128:EC], sems.at[2]),
    ]
    for c in copies:
        c.start()
    weight = mask[...].astype(F32)
    w_ext[inner] = weight
    s_ext[inner] = weight * (depth[...].astype(F32) - 0.5 * (K - 1))
    lane = lax.broadcasted_iota(jnp.int32, (RD, 128), 1)
    before, after = left[...].astype(F32), right[...].astype(F32)
    here = slice(16, 16 + RD)
    value = jnp.zeros((RD, 128), F32)
    for l in range(2):
        for halo, to in ((before, 126 + l), (after, l)):
            got = sum(moved(halo, 48 + 3 * l + part, to) for part in range(3))
            value = jnp.where(lane == to, got, value)
    v_ext[here, 0:128] = value
    for o, message in ((w_ext, 54), (s_ext, 55)):
        value = jnp.where(lane == 127, moved(before, message, 127), 0.0)
        o[here, 0:128] = jnp.where(lane == 0, moved(after, message, 0), value)
    for s in range(K):
        value = jnp.where(lane < 3, moved(after, 3 * s, 0), 0.0)
        value = jnp.where(lane >= 125, moved(before, 3 * s, 125), value).astype(BF16)
        tops[0, s, 16:48, 0:128] = value[0:32]
        tops[1, s, 0:32, 0:128] = value[RD - 32 : RD]
    for c in range(2):
        span = slice(128 * c, 128 * c + 128)
        turned, turned_after, tile = before[span], after[span], lane[span]
        for s in range(K):
            value = inner_refs[4 * c + 3][s].astype(F32)
            value = jnp.where((tile >= 32) & (tile < 35), moved(turned, 3 * s, 32), value)
            value = jnp.where((tile >= 67) & (tile < 70), moved(turned_after, 3 * s, 67), value)
            rim[s, span, :] = value.astype(BF16)
    for side, halo, row in ((1, up, 0), (0, down, 16 + RD)):
        lines = dot(put[side], halo[...])
        for s in range(K):
            tops[1 - side, s, 32 - 32 * side : 48 - 32 * side, :] = lines[16 * s : 16 * s + 16].astype(BF16)
        v_ext[row : row + 16, :] = lines[256:272]
        w_ext[row : row + 16, :] = lines[272:288]
        s_ext[row : row + 16, :] = lines[288:304]
    for c in copies:
        c.wait()
    at_lane = lax.broadcasted_iota(jnp.int32, (1, EC), 1)
    col = pos[1] * CD + jnp.where(at_lane < 64, at_lane + CD, at_lane - 128)
    valid_right = ((col >= 0) & (col < n_cr * CD - 1)).astype(F32)
    row_iota = lax.broadcasted_iota(jnp.int32, (16, 1), 0)
    tile_lane = lax.broadcasted_iota(jnp.int32, (16, 128), 1)

    def left_of(x):
        return pltpu.roll(x, 1, 1)

    def right_of(x):
        return pltpu.roll(x, EC - 1, 1)

    def finish(at, sums, n=16):
        sii, sic, scc = (0.25 * x for x in sums)
        inv = 1.0 / (sii + scc + 2.0)
        row = pos[0] * RD - 16 + at + row_iota[0:n]
        valid_down = ((row >= 0) & (row < n_in * RD - 1)).astype(F32)
        ta = valid_down * ((scc + 1.0) * inv)
        tb = (valid_down * valid_right) * (-sic * inv)
        tc = valid_right * ((sii + 1.0) * inv)
        value = v_ext[pl.ds(at, n + 8), :]
        here = value[0:n]
        dd = value[1 : n + 1] - here
        dr = right_of(here) - here
        to = pl.ds(at, n)
        ta_o[to, :] = ta
        tb_o[to, :] = tb
        tc_o[to, :] = tc
        fd[to, :] = ta * dd + tb * dr
        fr[to, :] = tb * dd + tc * dr

    for side in range(2):
        for lead, n in ((8, 8), (16, 16)) if side == 0 else ((16, 16), (32, 8)):
            tile = slice(lead // 16 * 16, lead // 16 * 16 + 16)
            keep = slice(lead % 16, lead % 16 + n)
            sums = gradient_sums(
                lambda s, side=side: tops[side, s], row_band(n, 48, lead), tile, 0, EC, keep
            )
            finish(lead + side * (RD - 16), sums, n)

    wide = row_band(32, 64, 16)

    def rim_step(t, carry):
        at = pl.multiple_of(32 * t, 32)
        edge = gradient_sums(lambda s: rim[s, pl.ds(at, 64), :], wide, slice(16, 48), 0, 128)
        for i, e in enumerate(edge):
            rim_sums[i, pl.ds(pl.multiple_of(at + 16, 16), 32), :] = e
        return carry

    lax.fori_loop(0, RD // 32 - 1, rim_step, 0, unroll=7)

    for c, (first, steps) in enumerate(cuts):
        sii, sic, scc = inner_refs[4 * c : 4 * c + 3]

        def step(t, carry, sii=sii, sic=sic, scc=scc, first=first):
            local = pl.ds(pl.multiple_of(16 * (t - first), 16), 16)
            at = pl.ds(pl.multiple_of(16 * t, 16), 16)
            sums = []
            for ref, e in zip((sii, sic, scc), (rim_sums[i, at, :] for i in range(3))):
                low, high = pltpu.roll(e, 93, 1), pltpu.roll(e, 61, 1)
                x = ref[local, :]
                sums.append(
                    jnp.concatenate(
                        [
                            jnp.where(tile_lane < 64, high, low),
                            jnp.where(tile_lane == 0, low, x[:, 0:128]),
                            x[:, 128 : CD - 128],
                            jnp.where(tile_lane == 127, high, x[:, CD - 128 :]),
                        ],
                        axis=1,
                    )
                )
            finish(pl.multiple_of(16 * t + 16, 16), sums)
            return carry

        lax.fori_loop(first, first + steps, step, 0, unroll=7)

    def residuals(at, n):
        before = pl.ds(pl.multiple_of(at - 8, 8), n + 8)
        here = pl.ds(at, n)
        fdw, taw = fd[before, :], ta_o[before, :]
        tc, right_flux, weight = tc_o[here, :], fr[here, :], w_ext[here, :]
        image = fdw[7 : n + 7] - fdw[8 : n + 8] + left_of(right_flux) - right_flux + weight * v_ext[here, :]
        r = s_ext[here, :] - image
        diag = taw[8 : n + 8] + 2.0 * tb_o[here, :] + tc + taw[7 : n + 7] + left_of(tc) + weight
        inv = jnp.where(diag != 0.0, 1.0 / diag, 0.0)
        z = r * inv
        z_o[here, :] = z
        return r, inv, z

    def own(e, total):
        at = pl.multiple_of(16 + 16 * e, 16)
        r, inv, z = (x[:, 128:] for x in residuals(at, 16))
        to = pl.ds(pl.multiple_of(16 * e, 16), 16)
        r_o[to, :] = r
        rd_o[to, :] = inv
        rowsum[pl.ds(2 * e, 1), :] = jnp.sum(r[0:8], axis=0, keepdims=True)
        rowsum[pl.ds(2 * e + 1, 1), :] = jnp.sum(r[8:16], axis=0, keepdims=True)
        rz = r * z
        rz = rz[0:8] + rz[8:16]
        return total + sum(rz[:, k * 128 : k * 128 + 128] for k in range(CD // 128))

    residuals(8, 8)
    residuals(16 + RD, 8)
    sums_o[...] = lax.fori_loop(0, RD // 16, own, jnp.zeros((8, 128), F32), unroll=4)
    sums = block_sums(rowsum[...], group[...])
    for j in range(n_cr):
        blocks_o[j] = sums


def tensor_stage(n_in, n_cr, cuts, pos, amp, v, mask, depth, up, down, left, right, put, group, sums):
    vmem = pl.BlockSpec(memory_space=VMEM)
    hbm = pl.BlockSpec(memory_space=pltpu.HBM)
    ext = jax.ShapeDtypeStruct((ER, EC), F32)
    flat = jax.ShapeDtypeStruct((RD, CD), F32)
    return pl.pallas_call(
        functools.partial(tensor_kernel, n_in, n_cr, cuts),
        in_specs=[pl.BlockSpec(memory_space=pltpu.SMEM), hbm, hbm] + [vmem] * (8 + len(sums)),
        out_specs=[vmem] * 8,
        out_shape=[
            ext, ext, ext, ext, flat, flat,
            jax.ShapeDtypeStruct((n_cr, CR, CC), F32),
            jax.ShapeDtypeStruct((8, 128), F32),
        ],
        scratch_shapes=[
            VMEM((2, K, 48, EC), BF16), VMEM((K, RD, 128), BF16), VMEM((3, RD, 128), F32), VMEM((ER + 8, EC), F32), VMEM((ER, EC), F32),
            VMEM((ER, EC), F32), VMEM((ER, EC), F32), VMEM((ER, EC), F32), VMEM((CR, CD), F32),
            pltpu.SemaphoreType.DMA((3,)),
        ],
        compiler_params=pltpu.CompilerParams(vmem_limit_bytes=28 * 1024 * 1024),
        cost_estimate=pl.CostEstimate(flops=10**8, bytes_accessed=2 * 10**7, transcendentals=0),
        name="tensor_stage",
    )(pos, in_hbm(amp), in_hbm(v), mask, depth, up, down, left, right, put, group, *sums)


def moments_kernel(n_in, n_cr, extra, blocks, fwd_hi, fwd_lo, steps, pay_o, own_o):
    x = jnp.concatenate([blocks[j, :CR] for j in range(n_cr)], axis=1)
    hi, lo = parts2(x)
    span = slice(16, 16 + x.shape[1])
    both = dot(jnp.concatenate([hi, lo], axis=0), fwd_hi[span, :])
    x = both[:CR] + both[CR:] + dot(hi, fwd_lo[span, :])
    width = x.shape[1]
    forth, back = x, x
    for i in range(5):
        d = 1 << i
        zero = jnp.zeros((d, width), F32)
        decay = steps[i : i + 1]
        forth = forth + decay * jnp.concatenate([zero, forth[:-d]], axis=0)
        back = back + decay * jnp.concatenate([back[d:], zero], axis=0)
    decay, scale = steps[0:1], steps[5:6]
    zero = jnp.zeros((1, width), F32)
    inside = forth + decay * jnp.concatenate([back[1:], zero], axis=0)
    inside = scale * inside
    own_o[...] = jnp.concatenate(
        [scale * decay * back[0:1], inside, scale * decay * forth[CR - 1 :], jnp.zeros((6, width), F32)],
        axis=0,
    )
    f = jnp.concatenate([forth[CR - 1 :, 128 * k : 128 * k + 128] for k in range(n_cr)], axis=0)
    b = jnp.concatenate([back[0:1, 128 * k : 128 * k + 128] for k in range(n_cr)], axis=0)
    for i in range(n_in):
        pay_o[i, 0:n_cr] = f
        pay_o[i, n_cr : 2 * n_cr] = b
    if extra:
        sums = sum(blocks[j, CR : CR + 8] for j in range(n_cr))
        energy = jnp.sum(x * inside, axis=0, keepdims=True)
        energy = sum(energy[:, 128 * k : 128 * k + 128] for k in range(n_cr))
        at = lax.broadcasted_iota(jnp.int32, (8, 128), 0)
        sums = jnp.where(at == 3, energy, sums)
        for i in range(n_in):
            pay_o[i, 2 * n_cr : 2 * n_cr + 8] = sums


def moments_stage(n_in, n_cr, extra, blocks, fwd_hi, fwd_lo, steps):
    vmem = pl.BlockSpec(memory_space=VMEM)
    return pl.pallas_call(
        functools.partial(moments_kernel, n_in, n_cr, extra),
        in_specs=[vmem] * 4, out_specs=[vmem] * 2,
        out_shape=[
            jax.ShapeDtypeStruct((n_in, 2 * n_cr + 8 * extra, 128), F32),
            jax.ShapeDtypeStruct((40, CC * n_cr), F32),
        ],
        compiler_params=pltpu.CompilerParams(vmem_limit_bytes=12 * 1024 * 1024),
        cost_estimate=pl.CostEstimate(flops=2 * 10**8, bytes_accessed=5 * 10**6, transcendentals=0),
        name="moments_stage",
    )(blocks, fwd_hi, fwd_lo, steps)


def coarse_values(n_in, n_cr, pos, moments, own, grow, fall, blocks, fwd_hi, fwd_lo, spread):
    mine = pos[0]
    r32, whole, series, link = (blocks[i] for i in range(4))
    f = [moments[i, 0:n_cr] for i in range(n_in)]
    b = [moments[i, n_cr : 2 * n_cr] for i in range(n_in)]
    hf, hb = f[0], b[n_in - 1]
    for i in range(1, n_in):
        hf = r32 * hf + f[i]
        hb = r32 * hb + b[n_in - 1 - i]
    above = (hb + whole * hf) * series
    below = (hf + whole * hb) * series
    mine_above, mine_below = jnp.zeros_like(above), jnp.zeros_like(below)
    energy = jnp.zeros_like(above)
    for i in range(n_in):
        k = n_in - 1 - i
        mine_above = jnp.where(mine == i, above, mine_above)
        mine_below = jnp.where(mine == k, below, mine_below)
        energy += above * b[i] + below * f[k]
        above = r32 * above + f[i]
        below = r32 * below + b[k]
    energy = energy * link
    a_row = jnp.concatenate([mine_above[k : k + 1] for k in range(n_cr)], axis=1)
    b_row = jnp.concatenate([mine_below[k : k + 1] for k in range(n_cr)], axis=1)
    u = own[...] + a_row * grow[...] + b_row * fall[...]
    hi, lo = parts2(u)
    span = pl.ds(pl.multiple_of(pos[1] * CC, CC), 2 * CC)
    turned = (((1,), (1,)), ((), ()))
    both = lax.dot_general(jnp.concatenate([hi, lo], axis=0), fwd_hi[span, :], turned, preferred_element_type=F32)
    values = both[:40] + both[40:] + lax.dot_general(hi, fwd_lo[span, :], turned, preferred_element_type=F32)
    three = dot(jnp.concatenate(parts3(values), axis=0), spread[...])
    return values, three[:40] + three[40:80] + three[80:], energy


def image_kernel(
    n_in, n_cr, pos, moments, own, grow, fall, blocks, fwd_hi, fwd_lo, spread, group,
    ta, tb, tc, z, rd, mask, first_blocks, first_sums,
    p_o, q_o, blocks_o, rowsum, cs,
):
    values, spread_rows, _ = coarse_values(
        n_in, n_cr, pos, moments, own, grow, fall, blocks, fwd_hi, fwd_lo, spread
    )
    cs[...] = spread_rows

    def field(strip):
        at = pl.ds(pl.multiple_of(8 + 8 * strip, 8), 8)
        return z[at, :] + cs[pl.ds(strip, 1), :]

    def fluxes(at, n, value):
        here = value[0:n]
        dd = value[1 : n + 1] - here
        dr = pltpu.roll(here, EC - 1, 1) - here
        at = pl.ds(at, n)
        b = tb[at, :]
        return ta[at, :] * dd + b * dr, b * dd + tc[at, :] * dr

    def images(e, carry):
        pq, qq, strip, above = carry
        following = [field(2 * e + 2), field(2 * e + 3)]
        value = jnp.concatenate([strip] + following, axis=0)
        down, side = fluxes(pl.multiple_of(16 + 16 * e, 16), 16, value)
        flux = jnp.concatenate([above[7:8], down[0:15]], axis=0) - down + pltpu.roll(side, 1, 1) - side
        to = pl.ds(pl.multiple_of(16 * e, 16), 16)
        p = value[0:16, 128:]
        q = flux[:, 128:] + mask[to, :].astype(F32) * p
        p_o[to, :] = p
        q_o[to, :] = q
        rowsum[pl.ds(2 * e, 1), :] = jnp.sum(q[0:8], axis=0, keepdims=True)
        rowsum[pl.ds(2 * e + 1, 1), :] = jnp.sum(q[8:16], axis=0, keepdims=True)
        return pq + folded(p * q), qq + folded(q * q * rd[to, :]), following[1], down[8:16]

    def folded(x):
        x = x[0:8] + x[8:16]
        return sum(x[:, k * 128 : k * 128 + 128] for k in range(CD // 128))

    strip = field(1)
    above, _ = fluxes(8, 8, jnp.concatenate([field(0), strip], axis=0))
    zero = jnp.zeros((8, 128), F32)
    pq, qq, _, _ = lax.fori_loop(0, RD // 16, images, (zero, zero, strip, above), unroll=4)

    def lanes(x):
        return jnp.sum(x, axis=0, keepdims=True)

    rp = jnp.sum(first_sums[...], axis=0, keepdims=True)
    rp += jnp.sum(first_blocks[0] * pltpu.roll(values, 2 * CC - 16, 1)[1 : CR + 1, :CC], axis=0, keepdims=True)
    tail = jnp.concatenate([rp, lanes(pq), lanes(qq), jnp.zeros((5, 128), F32)], axis=0)
    sums = block_sums(rowsum[...], group[...])
    for j in range(n_cr):
        blocks_o[j, 0:CR] = sums
        blocks_o[j, CR : CR + 8] = tail


def final_kernel(
    n_in, n_cr, pos, moments, own, grow, fall, blocks, fwd_hi, fwd_lo, spread,
    p_in, q_in, r_in, rd, v_in, v_o, r_o, d_o, cs,
):
    _, spread_rows, energy = coarse_values(
        n_in, n_cr, pos, moments, own, grow, fall, blocks, fwd_hi, fwd_lo, spread
    )
    cs[...] = spread_rows
    sums = sum(moments[i, 2 * n_cr : 2 * n_cr + 8] for i in range(n_in))
    old = jnp.sum(sums[0:1], axis=1, keepdims=True)
    curvature = jnp.sum(sums[1:2], axis=1, keepdims=True)
    energy = jnp.sum(jnp.sum(energy, axis=0, keepdims=True), axis=1, keepdims=True)
    image = jnp.sum(sums[2:3] + sums[3:4], axis=1, keepdims=True) + energy
    step = old / curvature
    ratio = (step * step * image - old) / old
    more = 1.0 + ratio

    def body(e, carry):
        at = pl.ds(pl.multiple_of(16 * e, 16), 16)
        p, q = p_in[at, :], q_in[at, :]
        coarse = [jnp.broadcast_to(cs[pl.ds(2 * e + k, 1), 128:], (8, CD)) for k in (1, 2)]
        coarse = jnp.concatenate(coarse, axis=0)
        v_o[at, :] = v_in[at, :] + step * p
        r_o[at, :] = r_in[at, :] - step * q
        d_o[at, :] = more * p - step * (q * rd[at, :] + coarse)
        return carry

    lax.fori_loop(0, RD // 16, body, 0, unroll=4)


def coarse_call(kernel, n_in, n_cr, name, out_shape, scratch, pos, moments, own, tables, rest, group=None):
    vmem = pl.BlockSpec(memory_space=VMEM)
    args = [moments, own, tables["grow"], tables["fall"], tables["blocks"], *tables["forward"], tables["spread"]]
    args += ([group] if group is not None else []) + list(rest)
    return pl.pallas_call(
        functools.partial(kernel, n_in, n_cr),
        in_specs=[pl.BlockSpec(memory_space=pltpu.SMEM)] + [vmem] * len(args),
        out_specs=[vmem] * len(out_shape), out_shape=out_shape, scratch_shapes=scratch,
        compiler_params=pltpu.CompilerParams(vmem_limit_bytes=22 * 1024 * 1024),
        cost_estimate=pl.CostEstimate(flops=10**8, bytes_accessed=10**7, transcendentals=0),
        name=name,
    )(pos, *args)


def neighbours(value_low, value_high, axis, count):
    ahead = [(i, i + 1) for i in range(count - 1)]
    behind = [(j, i) for i, j in ahead]
    return lax.ppermute(value_high, axis, ahead), lax.ppermute(value_low, axis, behind)


def per_device(n_in, n_cr, amplitudes, mask, depth, iterate):
    rows, put, mix, lanes = (jnp.asarray(t) for t in line_tables())
    tables = coarse_tables(n_in, n_cr)
    pos = jnp.stack([lax.axis_index("inline"), lax.axis_index("crosslin")]).astype(jnp.int32)
    col_first, col_last, local = pack_columns(amplitudes, iterate, mask, depth)
    left, right = neighbours(col_first, col_last, "crosslin", n_cr)
    cuts = ((1, 7), (8, 7))
    *inner, lines = inner_stage(*cuts[0], local, (iterate, mask, depth, rows))
    (left, right), lines = lax.optimization_barrier(((left, right), lines))
    row_first, row_last = pack_rows(lines, left, right, mix, lanes)
    up, down = neighbours(row_first, row_last, "inline", n_in)
    inner += inner_stage(*cuts[1], amplitudes)
    group = jnp.asarray(tables["group"])
    ta, tb, tc, z, r, rd, blocks, sums = tensor_stage(
        n_in, n_cr, cuts, pos, amplitudes, iterate, mask, depth, up, down, left, right, put, group, inner
    )

    def moments_of(payload, extra):
        gathered = lax.all_to_all(payload, "crosslin", 0, 0, tiled=True)
        pay, own = moments_stage(n_in, n_cr, extra, gathered, *tables["forward"], tables["steps"])
        return lax.all_to_all(pay, "inline", 0, 0, tiled=True), own

    flat = jax.ShapeDtypeStruct((RD, CD), F32)
    cs = VMEM((40, EC), F32)
    moments, own = moments_of(blocks, False)
    p, q, payload = coarse_call(
        image_kernel, n_in, n_cr, "image_stage",
        [flat, flat, jax.ShapeDtypeStruct((n_cr, CR + 8, CC), F32)],
        [VMEM((CR, CD), F32), cs],
        pos, moments, own, tables, [ta, tb, tc, z, rd, mask, blocks, sums], group,
    )
    moments, own = moments_of(payload, True)
    return tuple(
        coarse_call(
            final_kernel, n_in, n_cr, "final_stage", [flat, flat, flat], [cs],
            pos, moments, own, tables, [p, q, r, rd, iterate],
        )
    )


def solution(mesh):
    n_in, n_cr = mesh.shape["inline"], mesh.shape["crosslin"]
    flat = P("inline", "crosslin")
    return jax.shard_map(
        functools.partial(per_device, n_in, n_cr), mesh=mesh,
        in_specs=(P(None, "inline", "crosslin"), flat, flat, flat),
        out_specs=(flat, flat, flat), check_vma=False,
    )
```

```python
import functools

import jax
import jax.numpy as jnp
import ml_dtypes
import numpy as np
from jax import lax
from jax.experimental import pallas as pl
from jax.experimental.pallas import tpu as pltpu
from jax.sharding import PartitionSpec as P

K = 16
DEC = 8
CI = 32
COUPLING = 4.0
F32 = jnp.float32
BF16 = jnp.bfloat16
NPB = ml_dtypes.bfloat16
VMEM = pltpu.VMEM

RD = 256
CD = 1024
ER = RD + 32
EC = CD + 128
CR = RD // DEC
CC = CD // DEC
MSG = 64


def in_hbm(x):
    return pltpu.with_memory_space_constraint(x, pltpu.HBM)


def dot(a, b):
    return jnp.dot(a, b, preferred_element_type=F32)


def parts2(x):
    hi = x.astype(BF16)
    return hi, (x - hi.astype(F32)).astype(BF16)


def parts3(x):
    hi = x.astype(BF16)
    rest = x - hi.astype(F32)
    mid = rest.astype(BF16)
    return hi, mid, (rest - mid.astype(F32)).astype(BF16)


def np2(x):
    hi = x.astype(np.float32).astype(NPB)
    return hi, (x - hi.astype(np.float64)).astype(np.float32).astype(NPB)


def line_tables():
    rows = np.zeros((2, MSG, 256), np.float32)
    put = np.zeros((2, 304, MSG), np.float32)
    for s in range(K):
        for k in range(3):
            rows[0, 3 * s + k, 16 * s + k] = 1
            rows[1, 3 * s + k, 16 * s + 13 + k] = 1
    for side in range(2):
        put[side, :256] = rows[side].T
        for l in range(2):
            for part in range(3):
                put[side, 256 + (14 + l if side else l), 48 + 3 * l + part] = 1
        put[side, 272 + (15 if side else 0), 54] = 1
        put[side, 288 + (15 if side else 0), 55] = 1
    mix = np.zeros((2, 3, MSG, 128), np.float32)
    for k in range(3):
        for s in range(K):
            mix[:, k, 3 * s + k, 3 * s : 3 * s + 3] = 1
    for l in range(2):
        for part in range(3):
            for other in range(2):
                mix[0, l, 48 + 3 * l + part, 48 + 3 * other + part] = 1
                mix[1, l + 1, 48 + 3 * l + part, 48 + 3 * other + part] = 1
    for o in (54, 55):
        mix[0, 0, o, o] = 1
        mix[1, 2, o, o] = 1
    lanes = np.zeros((2, 128, 128), np.float32)
    for s in range(K):
        for k in range(3):
            lanes[0, 3 * s + k, k] = 1
            lanes[1, 3 * s + k, 125 + k] = 1
    for l in range(2):
        for part in range(3):
            lanes[0, 48 + 3 * l + part, l] = 1
            lanes[1, 48 + 3 * l + part, 126 + l] = 1
    for o in (54, 55):
        lanes[0, o, 0] = 1
        lanes[1, o, 127] = 1
    return tuple(t.astype(NPB) for t in (rows, put, mix, lanes))


def coarse_tables(n_in, n_cr):
    n = CC * n_cr
    freq = np.arange(n, dtype=np.float64)
    norm = np.where(freq == 0, np.sqrt(1.0 / n), np.sqrt(2.0 / n))

    def cosines(cols):
        phase = (freq[:, None] * (2 * cols[None, :] + 1)) % (4 * n)
        return norm[:, None] * np.cos(np.pi * phase / (2 * n))

    lead = np.arange(n + CC, dtype=np.float64) - 16
    forward = cosines(lead).T * (lead[:, None] >= -1) * (lead[:, None] <= n)
    half = (2.0 - 2.0 * np.cos(np.pi * freq / n) + 1.0 / (CI * CI)) / 2.0
    kappa = np.log1p(half + np.sqrt(half * (half + 2.0)))
    scale = 1.0 / (COUPLING * 2.0 * np.sinh(kappa))
    steps = np.stack([np.exp(-kappa * d) for d in (1, 2, 4, 8, 16)] + [scale] + [scale * 0] * 2)
    at = np.arange(40)[:, None]
    grow = scale * np.exp(-kappa * at) * (at < 34)
    fall = scale * np.exp(-kappa * (33.0 - at)) * (at < 34)
    whole = CR * n_in
    blocks = np.stack(
        [
            np.exp(-kappa * CR),
            np.exp(-kappa * whole),
            1.0 / (1.0 - np.exp(-kappa * 2 * whole)),
            scale * np.exp(-kappa),
        ]
    ).reshape(4, n_cr, 128)
    spread = np.zeros((2 * CC, EC))
    for lane in range(EC):
        col = ((lane if lane >= 64 else lane + EC) - 128) // DEC
        if -1 <= col <= CC:
            spread[16 + col, lane] = 1
    group = np.zeros((CD, CC))
    group[np.arange(CD), np.arange(CD) // DEC] = 1
    f = np.float32
    return dict(
        forward=np2(forward), steps=steps.astype(f), grow=grow.astype(f),
        fall=fall.astype(f), blocks=blocks.astype(f), spread=spread.astype(NPB), group=group.astype(NPB),
    )


def moved(x, lane, to):
    turn = (to - lane) % x.shape[1]
    return pltpu.roll(x, turn, 1) if turn else x


def pack_columns_kernel(amp, v_in, m_in, d_in, out0, out1, amp_o, v, m, d, sems, rest_sem):
    copies = []
    for side, at in enumerate((0, CD - 128)):
        span = pl.ds(at, 128)
        copies.append(pltpu.make_async_copy(amp.at[:, :, span], amp_o.at[:, :, span], sems.at[side, 0]))
        copies.append(pltpu.make_async_copy(v_in.at[:, span], v.at[side], sems.at[side, 1]))
        copies.append(pltpu.make_async_copy(m_in.at[:, span], m.at[side], sems.at[side, 2]))
        copies.append(pltpu.make_async_copy(d_in.at[:, span], d.at[side], sems.at[side, 3]))
    middle = pl.ds(128, CD - 256)
    rest = [
        pltpu.make_async_copy(amp.at[:, span, middle], amp_o.at[:, span, middle], rest_sem.at[i])
        for i, span in enumerate((pl.ds(0, 144), pl.ds(RD - 16, 16)))
    ]
    for c in copies:
        c.start()
    for c in rest:
        c.start()
    lane = lax.broadcasted_iota(jnp.int32, (RD, 128), 1)
    for c in copies:
        c.wait()
    for side, out in enumerate((out0, out1)):
        low = 125 if side else 0

        def edge(s, side=side):
            return amp_o[s, :, CD - 128 :] if side else amp_o[s, :, 0:128]

        weight = m[side].astype(F32)
        source = weight * (d[side].astype(F32) - 0.5 * (K - 1))
        end = 127 if side else 0
        total = jnp.where(lane == 54, moved(weight, end, 54), moved(source, end, 55))
        for part, value in enumerate(parts3(v[side])):
            value = value.astype(F32)
            for l in range(2):
                to = 48 + 3 * l + part
                total = jnp.where(lane == to, moved(value, (126 if side else 0) + l, to), total)
        for s in range(K):
            total = jnp.where((lane >= 3 * s) & (lane < 3 * s + 3), moved(edge(s).astype(F32), low, 3 * s), total)
        out[...] = jnp.where(lane < 56, total, 0.0).astype(BF16)
    for c in rest:
        c.wait()


def pack_columns(amplitudes, iterate, mask, depth):
    hbm = pl.BlockSpec(memory_space=pltpu.HBM)
    out = jax.ShapeDtypeStruct((RD, 128), BF16)
    return pl.pallas_call(
        pack_columns_kernel, in_specs=[hbm] * 4,
        out_specs=[pl.BlockSpec(memory_space=VMEM)] * 3,
        out_shape=[out, out, jax.ShapeDtypeStruct((K, RD, CD), BF16)],
        scratch_shapes=[
            VMEM((2, RD, 128), F32), VMEM((2, RD, 128), jnp.int32),
            VMEM((2, RD, 128), jnp.int32), pltpu.SemaphoreType.DMA((2, 4)), pltpu.SemaphoreType.DMA((2,)),
        ],
        compiler_params=pltpu.CompilerParams(vmem_limit_bytes=12 * 1024 * 1024),
        cost_estimate=pl.CostEstimate(flops=10**7, bytes_accessed=3 * 10**6, transcendentals=0),
        name="pack_columns",
    )(*(in_hbm(x) for x in (amplitudes, iterate, mask, depth)))


def pack_rows_kernel(lines, left, right, mix, lanes, out0, out1):
    for side, out in enumerate((out0, out1)):
        out[:, 128:] = lines[side]
        total = jnp.zeros((MSG, 128), F32)
        for halo, which in ((left, 1), (right, 0)):
            edge = halo[RD - 16 : RD].astype(F32)[13:16] if side else halo[0:16].astype(F32)[0:3]
            for k in range(3):
                term = mix[side, k].astype(F32) * edge[k : k + 1]
                total += dot(term.astype(BF16), lanes[which])
        out[:, 0:128] = total.astype(BF16)


def pack_rows(lines, left, right, mix, lanes):
    vmem = pl.BlockSpec(memory_space=VMEM)
    out = jax.ShapeDtypeStruct((MSG, EC), BF16)
    return pl.pallas_call(
        pack_rows_kernel, in_specs=[vmem] * 5, out_specs=[vmem] * 2, out_shape=[out, out],
        compiler_params=pltpu.CompilerParams(vmem_limit_bytes=12 * 1024 * 1024),
        cost_estimate=pl.CostEstimate(flops=10**7, bytes_accessed=10**6, transcendentals=0),
        name="pack_rows",
    )(lines, left, right, mix, lanes)


def row_band(rows, window, lead):
    at = lax.broadcasted_iota(jnp.int32, (rows, window), 0) + lead
    to = lax.broadcasted_iota(jnp.int32, (rows, window), 1)
    return jnp.where(to == at + 1, 1.0, jnp.where(to == at - 1, -1.0, 0.0)).astype(BF16)


def gradient_sums(window, band, span, off, take, keep=slice(None)):
    total = None
    for s in range(K):
        x = window(s)
        n = x.shape[1]
        middle = x[span]
        gc = pltpu.roll(middle, n - 1, 1).astype(F32) - pltpu.roll(middle, 1, 1).astype(F32)
        gc = gc[keep, off : off + take]
        gi = dot(band, x[:, off : off + take])
        terms = (gi * gi, gi * gc, gc * gc)
        total = terms if total is None else tuple(t + u for t, u in zip(total, terms))
    return total


def edge_lines(side, a, v, m, d, rows):
    at = lax.broadcasted_iota(jnp.int32, (MSG, CD), 0)
    middle = dot(rows[side], a.reshape(K * 16, CD))
    split = [p.astype(F32) for p in parts3(v)]
    for l in range(2):
        row = 6 + l if side else l
        for part in range(3):
            middle = jnp.where(at == 48 + 3 * l + part, split[part][row : row + 1], middle)
    row = 7 if side else 0
    weight = m[row : row + 1].astype(F32)
    source = weight * (d[row : row + 1].astype(F32) - 0.5 * (K - 1))
    return jnp.where(at == 54, weight, jnp.where(at == 55, source, middle)).astype(BF16)


def inner_kernel(first, steps, edge, amp, *rest):
    if edge:
        v_in, m_in, d_in, rows_t, sii_o, sic_o, scc_o, edge_o, lines_o, v, m, d, end_sems = rest
    else:
        sii_o, sic_o, scc_o, edge_o, local, sems = rest
    base = 16 * (first - 1)
    skip = 0 if edge else 128 - base
    bounds = [] if edge else [(0, 48), (48, 48), (96, 16 * (steps + 2) - 96)]
    copies = [
        pltpu.make_async_copy(amp.at[:, pl.ds(base + r, n)], local.at[:, pl.ds(r, n)], sems.at[i])
        for i, (r, n) in enumerate(bounds)
    ]
    for c in copies:
        c.start()
    if not edge:
        amp, base = local, 0
    if edge:
        more = []
        for side in range(2):
            for i, (source, to) in enumerate(((v_in, v), (m_in, m), (d_in, d))):
                span = pl.ds(side * (RD - 8), 8)
                more.append(pltpu.make_async_copy(source.at[span], to.at[side], end_sems.at[3 * side + i]))
        for c in more:
            c.start()
    lane = lax.broadcasted_iota(jnp.int32, (16, 128), 1)
    band = row_band(16, 48, 16)

    def step(t, carry):
        at = pl.multiple_of(16 * t, 16)
        window = pl.ds(pl.multiple_of(base + 16 * t, 16), 48)
        for part in range(2):
            lanes = slice(0, 640) if part == 0 else slice(384, CD)
            off = 0 if part == 0 else 128
            sums = gradient_sums(lambda s: amp[s, window, lanes], band, slice(16, 32), off, 512)
            for o, value in zip((sii_o, sic_o, scc_o), sums):
                o[pl.ds(at, 16), 512 * part : 512 * part + 512] = value
        return carry

    def edges(t, carry):
        at = pl.ds(pl.multiple_of(16 * t, 16), 16)
        source = pl.ds(pl.multiple_of(16 * t + skip, 16), 16)
        for s in range(K):
            low = moved(amp[s, source, 0:128].astype(F32), 0, 35)
            high = moved(amp[s, source, CD - 128 : CD].astype(F32), 125, 64)
            tile = jnp.where((lane >= 35) & (lane < 38), low, jnp.where((lane >= 64) & (lane < 67), high, 0.0))
            edge_o[s, at, :] = tile.astype(BF16)
        return carry

    done = 0
    for i, (r, n) in enumerate(bounds):
        copies[i].wait()
        until = min(steps, (r + n) // 16 - 2)
        lax.fori_loop(done, until, step, 0, unroll=until - done)
        done = until
    lax.fori_loop(done, steps, step, 0, unroll=max(1, steps - done))
    lax.fori_loop(0, 8, edges, 0, unroll=4)
    if edge:
        for c in more:
            c.wait()
        lines_o[0] = edge_lines(0, amp[:, 0:16, :], v[0], m[0], d[0], rows_t)
        lines_o[1] = edge_lines(1, amp[:, RD - 16 :, :], v[1], m[1], d[1], rows_t)


def inner_stage(first, steps, amplitudes, more=()):
    hbm, vmem = pl.BlockSpec(memory_space=pltpu.HBM), pl.BlockSpec(memory_space=VMEM)
    flat = jax.ShapeDtypeStruct((16 * steps, CD), F32)
    out_shape = [flat, flat, flat, jax.ShapeDtypeStruct((K, 128, 128), BF16)]
    scratch = [] if more else [VMEM((K, 16 * (steps + 2), CD), BF16), pltpu.SemaphoreType.DMA((3,))]
    in_specs = [vmem if more else hbm]
    if more:
        out_shape += [jax.ShapeDtypeStruct((2, MSG, CD), BF16)]
        scratch += [
            VMEM((2, 8, CD), F32), VMEM((2, 8, CD), jnp.int32), VMEM((2, 8, CD), jnp.int32),
            pltpu.SemaphoreType.DMA((6,)),
        ]
        in_specs += [hbm, hbm, hbm, vmem]
    return pl.pallas_call(
        functools.partial(inner_kernel, first, steps, bool(more)),
        in_specs=in_specs, out_specs=[vmem] * len(out_shape), out_shape=out_shape, scratch_shapes=scratch,
        compiler_params=pltpu.CompilerParams(vmem_limit_bytes=14 * 1024 * 1024),
        cost_estimate=pl.CostEstimate(flops=10**8, bytes_accessed=6 * 10**6, transcendentals=0),
        name="inner_stage",
    )(amplitudes if more else in_hbm(amplitudes), *(in_hbm(x) for x in more[:3]), *more[3:])


def block_sums(rows, group):
    return sum(dot(part, group) for part in parts3(rows))


def tensor_kernel(
    n_in, n_cr, cuts, pos, amp, v_in, mask, depth, up, down, left, right, put, group, *rest
):
    inner_refs, rest = rest[: 4 * len(cuts)], rest[4 * len(cuts) :]
    (ta_o, tb_o, tc_o, z_o, r_o, rd_o, blocks_o, sums_o,
     tops, rim, rim_sums, v_ext, w_ext, s_ext, fd, fr, rowsum, sems) = rest
    inner = (slice(16, 16 + RD), slice(128, EC))
    copies = [
        pltpu.make_async_copy(amp.at[:, 0:32], tops.at[0, :, 16:48, 128:EC], sems.at[0]),
        pltpu.make_async_copy(amp.at[:, RD - 32 : RD], tops.at[1, :, 0:32, 128:EC], sems.at[1]),
        pltpu.make_async_copy(v_in, v_ext.at[16 : 16 + RD, 128:EC], sems.at[2]),
    ]
    for c in copies:
        c.start()
    weight = mask[...].astype(F32)
    w_ext[inner] = weight
    s_ext[inner] = weight * (depth[...].astype(F32) - 0.5 * (K - 1))
    lane = lax.broadcasted_iota(jnp.int32, (RD, 128), 1)
    before, after = left[...].astype(F32), right[...].astype(F32)
    here = slice(16, 16 + RD)
    value = jnp.zeros((RD, 128), F32)
    for l in range(2):
        for halo, to in ((before, 126 + l), (after, l)):
            got = sum(moved(halo, 48 + 3 * l + part, to) for part in range(3))
            value = jnp.where(lane == to, got, value)
    v_ext[here, 0:128] = value
    for o, message in ((w_ext, 54), (s_ext, 55)):
        value = jnp.where(lane == 127, moved(before, message, 127), 0.0)
        o[here, 0:128] = jnp.where(lane == 0, moved(after, message, 0), value)
    for s in range(K):
        value = jnp.where(lane < 3, moved(after, 3 * s, 0), 0.0)
        value = jnp.where(lane >= 125, moved(before, 3 * s, 125), value).astype(BF16)
        tops[0, s, 16:48, 0:128] = value[0:32]
        tops[1, s, 0:32, 0:128] = value[RD - 32 : RD]
    for c in range(2):
        span = slice(128 * c, 128 * c + 128)
        turned, turned_after, tile = before[span], after[span], lane[span]
        for s in range(K):
            value = inner_refs[4 * c + 3][s].astype(F32)
            value = jnp.where((tile >= 32) & (tile < 35), moved(turned, 3 * s, 32), value)
            value = jnp.where((tile >= 67) & (tile < 70), moved(turned_after, 3 * s, 67), value)
            rim[s, span, :] = value.astype(BF16)
    for side, halo, row in ((1, up, 0), (0, down, 16 + RD)):
        lines = dot(put[side], halo[...])
        for s in range(K):
            tops[1 - side, s, 32 - 32 * side : 48 - 32 * side, :] = lines[16 * s : 16 * s + 16].astype(BF16)
        v_ext[row : row + 16, :] = lines[256:272]
        w_ext[row : row + 16, :] = lines[272:288]
        s_ext[row : row + 16, :] = lines[288:304]
    for c in copies:
        c.wait()
    at_lane = lax.broadcasted_iota(jnp.int32, (1, EC), 1)
    col = pos[1] * CD + jnp.where(at_lane < 64, at_lane + CD, at_lane - 128)
    valid_right = ((col >= 0) & (col < n_cr * CD - 1)).astype(F32)
    row_iota = lax.broadcasted_iota(jnp.int32, (16, 1), 0)
    tile_lane = lax.broadcasted_iota(jnp.int32, (16, 128), 1)

    def left_of(x):
        return pltpu.roll(x, 1, 1)

    def right_of(x):
        return pltpu.roll(x, EC - 1, 1)

    def finish(at, sums, n=16):
        sii, sic, scc = (0.25 * x for x in sums)
        inv = 1.0 / (sii + scc + 2.0)
        row = pos[0] * RD - 16 + at + row_iota[0:n]
        valid_down = ((row >= 0) & (row < n_in * RD - 1)).astype(F32)
        ta = valid_down * ((scc + 1.0) * inv)
        tb = (valid_down * valid_right) * (-sic * inv)
        tc = valid_right * ((sii + 1.0) * inv)
        value = v_ext[pl.ds(at, n + 8), :]
        here = value[0:n]
        dd = value[1 : n + 1] - here
        dr = right_of(here) - here
        to = pl.ds(at, n)
        ta_o[to, :] = ta
        tb_o[to, :] = tb
        tc_o[to, :] = tc
        fd[to, :] = ta * dd + tb * dr
        fr[to, :] = tb * dd + tc * dr

    for side in range(2):
        for lead, n in ((8, 8), (16, 16)) if side == 0 else ((16, 16), (32, 8)):
            tile = slice(lead // 16 * 16, lead // 16 * 16 + 16)
            keep = slice(lead % 16, lead % 16 + n)
            sums = gradient_sums(
                lambda s, side=side: tops[side, s], row_band(n, 48, lead), tile, 0, EC, keep
            )
            finish(lead + side * (RD - 16), sums, n)

    wide = row_band(32, 64, 16)

    def rim_step(t, carry):
        at = pl.multiple_of(32 * t, 32)
        edge = gradient_sums(lambda s: rim[s, pl.ds(at, 64), :], wide, slice(16, 48), 0, 128)
        for i, e in enumerate(edge):
            rim_sums[i, pl.ds(pl.multiple_of(at + 16, 16), 32), :] = e
        return carry

    lax.fori_loop(0, RD // 32 - 1, rim_step, 0, unroll=7)

    for c, (first, steps) in enumerate(cuts):
        sii, sic, scc = inner_refs[4 * c : 4 * c + 3]

        def step(t, carry, sii=sii, sic=sic, scc=scc, first=first):
            local = pl.ds(pl.multiple_of(16 * (t - first), 16), 16)
            at = pl.ds(pl.multiple_of(16 * t, 16), 16)
            sums = []
            for ref, e in zip((sii, sic, scc), (rim_sums[i, at, :] for i in range(3))):
                low, high = pltpu.roll(e, 93, 1), pltpu.roll(e, 61, 1)
                x = ref[local, :]
                sums.append(
                    jnp.concatenate(
                        [
                            jnp.where(tile_lane < 64, high, low),
                            jnp.where(tile_lane == 0, low, x[:, 0:128]),
                            x[:, 128 : CD - 128],
                            jnp.where(tile_lane == 127, high, x[:, CD - 128 :]),
                        ],
                        axis=1,
                    )
                )
            finish(pl.multiple_of(16 * t + 16, 16), sums)
            return carry

        lax.fori_loop(first, first + steps, step, 0, unroll=7)

    def residuals(at, n):
        before = pl.ds(pl.multiple_of(at - 8, 8), n + 8)
        here = pl.ds(at, n)
        fdw, taw = fd[before, :], ta_o[before, :]
        tc, right_flux, weight = tc_o[here, :], fr[here, :], w_ext[here, :]
        image = fdw[7 : n + 7] - fdw[8 : n + 8] + left_of(right_flux) - right_flux + weight * v_ext[here, :]
        r = s_ext[here, :] - image
        diag = taw[8 : n + 8] + 2.0 * tb_o[here, :] + tc + taw[7 : n + 7] + left_of(tc) + weight
        inv = jnp.where(diag != 0.0, 1.0 / diag, 0.0)
        z = r * inv
        z_o[here, :] = z
        return r, inv, z

    def own(e, total):
        at = pl.multiple_of(16 + 16 * e, 16)
        r, inv, z = (x[:, 128:] for x in residuals(at, 16))
        to = pl.ds(pl.multiple_of(16 * e, 16), 16)
        r_o[to, :] = r
        rd_o[to, :] = inv
        rowsum[pl.ds(2 * e, 1), :] = jnp.sum(r[0:8], axis=0, keepdims=True)
        rowsum[pl.ds(2 * e + 1, 1), :] = jnp.sum(r[8:16], axis=0, keepdims=True)
        rz = r * z
        rz = rz[0:8] + rz[8:16]
        return total + sum(rz[:, k * 128 : k * 128 + 128] for k in range(CD // 128))

    residuals(8, 8)
    residuals(16 + RD, 8)
    sums_o[...] = lax.fori_loop(0, RD // 16, own, jnp.zeros((8, 128), F32), unroll=4)
    sums = block_sums(rowsum[...], group[...])
    for j in range(n_cr):
        blocks_o[j] = sums


def tensor_stage(n_in, n_cr, cuts, pos, amp, v, mask, depth, up, down, left, right, put, group, sums):
    vmem = pl.BlockSpec(memory_space=VMEM)
    hbm = pl.BlockSpec(memory_space=pltpu.HBM)
    ext = jax.ShapeDtypeStruct((ER, EC), F32)
    flat = jax.ShapeDtypeStruct((RD, CD), F32)
    return pl.pallas_call(
        functools.partial(tensor_kernel, n_in, n_cr, cuts),
        in_specs=[pl.BlockSpec(memory_space=pltpu.SMEM), hbm, hbm] + [vmem] * (8 + len(sums)),
        out_specs=[vmem] * 8,
        out_shape=[
            ext, ext, ext, ext, flat, flat,
            jax.ShapeDtypeStruct((n_cr, CR, CC), F32),
            jax.ShapeDtypeStruct((8, 128), F32),
        ],
        scratch_shapes=[
            VMEM((2, K, 48, EC), BF16), VMEM((K, RD, 128), BF16), VMEM((3, RD, 128), F32), VMEM((ER + 8, EC), F32), VMEM((ER, EC), F32),
            VMEM((ER, EC), F32), VMEM((ER, EC), F32), VMEM((ER, EC), F32), VMEM((CR, CD), F32),
            pltpu.SemaphoreType.DMA((3,)),
        ],
        compiler_params=pltpu.CompilerParams(vmem_limit_bytes=28 * 1024 * 1024),
        cost_estimate=pl.CostEstimate(flops=10**8, bytes_accessed=2 * 10**7, transcendentals=0),
        name="tensor_stage",
    )(pos, in_hbm(amp), in_hbm(v), mask, depth, up, down, left, right, put, group, *sums)


def moments_kernel(n_in, n_cr, extra, blocks, fwd_hi, fwd_lo, steps, pay_o, own_o):
    x = jnp.concatenate([blocks[j, :CR] for j in range(n_cr)], axis=1)
    hi, lo = parts2(x)
    span = slice(16, 16 + x.shape[1])
    both = dot(jnp.concatenate([hi, lo], axis=0), fwd_hi[span, :])
    x = both[:CR] + both[CR:] + dot(hi, fwd_lo[span, :])
    width = x.shape[1]
    forth, back = x, x
    for i in range(5):
        d = 1 << i
        zero = jnp.zeros((d, width), F32)
        decay = steps[i : i + 1]
        forth = forth + decay * jnp.concatenate([zero, forth[:-d]], axis=0)
        back = back + decay * jnp.concatenate([back[d:], zero], axis=0)
    decay, scale = steps[0:1], steps[5:6]
    zero = jnp.zeros((1, width), F32)
    inside = forth + decay * jnp.concatenate([back[1:], zero], axis=0)
    inside = scale * inside
    own_o[...] = jnp.concatenate(
        [scale * decay * back[0:1], inside, scale * decay * forth[CR - 1 :], jnp.zeros((6, width), F32)],
        axis=0,
    )
    f = jnp.concatenate([forth[CR - 1 :, 128 * k : 128 * k + 128] for k in range(n_cr)], axis=0)
    b = jnp.concatenate([back[0:1, 128 * k : 128 * k + 128] for k in range(n_cr)], axis=0)
    for i in range(n_in):
        pay_o[i, 0:n_cr] = f
        pay_o[i, n_cr : 2 * n_cr] = b
    if extra:
        sums = sum(blocks[j, CR : CR + 8] for j in range(n_cr))
        energy = jnp.sum(x * inside, axis=0, keepdims=True)
        energy = sum(energy[:, 128 * k : 128 * k + 128] for k in range(n_cr))
        at = lax.broadcasted_iota(jnp.int32, (8, 128), 0)
        sums = jnp.where(at == 3, energy, sums)
        for i in range(n_in):
            pay_o[i, 2 * n_cr : 2 * n_cr + 8] = sums


def moments_stage(n_in, n_cr, extra, blocks, fwd_hi, fwd_lo, steps):
    vmem = pl.BlockSpec(memory_space=VMEM)
    return pl.pallas_call(
        functools.partial(moments_kernel, n_in, n_cr, extra),
        in_specs=[vmem] * 4, out_specs=[vmem] * 2,
        out_shape=[
            jax.ShapeDtypeStruct((n_in, 2 * n_cr + 8 * extra, 128), F32),
            jax.ShapeDtypeStruct((40, CC * n_cr), F32),
        ],
        compiler_params=pltpu.CompilerParams(vmem_limit_bytes=12 * 1024 * 1024),
        cost_estimate=pl.CostEstimate(flops=2 * 10**8, bytes_accessed=5 * 10**6, transcendentals=0),
        name="moments_stage",
    )(blocks, fwd_hi, fwd_lo, steps)


def coarse_values(n_in, n_cr, pos, moments, own, grow, fall, blocks, fwd_hi, fwd_lo, spread):
    mine = pos[0]
    r32, whole, series, link = (blocks[i] for i in range(4))
    f = [moments[i, 0:n_cr] for i in range(n_in)]
    b = [moments[i, n_cr : 2 * n_cr] for i in range(n_in)]
    hf, hb = f[0], b[n_in - 1]
    for i in range(1, n_in):
        hf = r32 * hf + f[i]
        hb = r32 * hb + b[n_in - 1 - i]
    above = (hb + whole * hf) * series
    below = (hf + whole * hb) * series
    mine_above, mine_below = jnp.zeros_like(above), jnp.zeros_like(below)
    energy = jnp.zeros_like(above)
    for i in range(n_in):
        k = n_in - 1 - i
        mine_above = jnp.where(mine == i, above, mine_above)
        mine_below = jnp.where(mine == k, below, mine_below)
        energy += above * b[i] + below * f[k]
        above = r32 * above + f[i]
        below = r32 * below + b[k]
    energy = energy * link
    a_row = jnp.concatenate([mine_above[k : k + 1] for k in range(n_cr)], axis=1)
    b_row = jnp.concatenate([mine_below[k : k + 1] for k in range(n_cr)], axis=1)
    u = own[...] + a_row * grow[...] + b_row * fall[...]
    hi, lo = parts2(u)
    span = pl.ds(pl.multiple_of(pos[1] * CC, CC), 2 * CC)
    turned = (((1,), (1,)), ((), ()))
    both = lax.dot_general(jnp.concatenate([hi, lo], axis=0), fwd_hi[span, :], turned, preferred_element_type=F32)
    values = both[:40] + both[40:] + lax.dot_general(hi, fwd_lo[span, :], turned, preferred_element_type=F32)
    three = dot(jnp.concatenate(parts3(values), axis=0), spread[...])
    return values, three[:40] + three[40:80] + three[80:], energy


def image_kernel(
    n_in, n_cr, pos, moments, own, grow, fall, blocks, fwd_hi, fwd_lo, spread, group,
    ta, tb, tc, z, rd, mask, first_blocks, first_sums,
    p_o, q_o, blocks_o, rowsum, cs,
):
    values, spread_rows, _ = coarse_values(
        n_in, n_cr, pos, moments, own, grow, fall, blocks, fwd_hi, fwd_lo, spread
    )
    cs[...] = spread_rows

    def field(strip):
        at = pl.ds(pl.multiple_of(8 + 8 * strip, 8), 8)
        return z[at, :] + cs[pl.ds(strip, 1), :]

    def fluxes(at, n, value):
        here = value[0:n]
        dd = value[1 : n + 1] - here
        dr = pltpu.roll(here, EC - 1, 1) - here
        at = pl.ds(at, n)
        b = tb[at, :]
        return ta[at, :] * dd + b * dr, b * dd + tc[at, :] * dr

    def images(e, carry):
        pq, qq, strip, above = carry
        following = [field(2 * e + 2), field(2 * e + 3)]
        value = jnp.concatenate([strip] + following, axis=0)
        down, side = fluxes(pl.multiple_of(16 + 16 * e, 16), 16, value)
        flux = jnp.concatenate([above[7:8], down[0:15]], axis=0) - down + pltpu.roll(side, 1, 1) - side
        to = pl.ds(pl.multiple_of(16 * e, 16), 16)
        p = value[0:16, 128:]
        q = flux[:, 128:] + mask[to, :].astype(F32) * p
        p_o[to, :] = p
        q_o[to, :] = q
        rowsum[pl.ds(2 * e, 1), :] = jnp.sum(q[0:8], axis=0, keepdims=True)
        rowsum[pl.ds(2 * e + 1, 1), :] = jnp.sum(q[8:16], axis=0, keepdims=True)
        return pq + folded(p * q), qq + folded(q * q * rd[to, :]), following[1], down[8:16]

    def folded(x):
        x = x[0:8] + x[8:16]
        return sum(x[:, k * 128 : k * 128 + 128] for k in range(CD // 128))

    strip = field(1)
    above, _ = fluxes(8, 8, jnp.concatenate([field(0), strip], axis=0))
    zero = jnp.zeros((8, 128), F32)
    pq, qq, _, _ = lax.fori_loop(0, RD // 16, images, (zero, zero, strip, above), unroll=4)

    def lanes(x):
        return jnp.sum(x, axis=0, keepdims=True)

    rp = jnp.sum(first_sums[...], axis=0, keepdims=True)
    rp += jnp.sum(first_blocks[0] * pltpu.roll(values, 2 * CC - 16, 1)[1 : CR + 1, :CC], axis=0, keepdims=True)
    tail = jnp.concatenate([rp, lanes(pq), lanes(qq), jnp.zeros((5, 128), F32)], axis=0)
    sums = block_sums(rowsum[...], group[...])
    for j in range(n_cr):
        blocks_o[j, 0:CR] = sums
        blocks_o[j, CR : CR + 8] = tail


def final_kernel(
    n_in, n_cr, pos, moments, own, grow, fall, blocks, fwd_hi, fwd_lo, spread,
    p_in, q_in, r_in, rd, v_in, v_o, r_o, d_o, cs,
):
    _, spread_rows, energy = coarse_values(
        n_in, n_cr, pos, moments, own, grow, fall, blocks, fwd_hi, fwd_lo, spread
    )
    cs[...] = spread_rows
    sums = sum(moments[i, 2 * n_cr : 2 * n_cr + 8] for i in range(n_in))
    old = jnp.sum(sums[0:1], axis=1, keepdims=True)
    curvature = jnp.sum(sums[1:2], axis=1, keepdims=True)
    energy = jnp.sum(jnp.sum(energy, axis=0, keepdims=True), axis=1, keepdims=True)
    image = jnp.sum(sums[2:3] + sums[3:4], axis=1, keepdims=True) + energy
    step = old / curvature
    ratio = (step * step * image - old) / old
    more = 1.0 + ratio

    def body(e, carry):
        at = pl.ds(pl.multiple_of(16 * e, 16), 16)
        p, q = p_in[at, :], q_in[at, :]
        coarse = [jnp.broadcast_to(cs[pl.ds(2 * e + k, 1), 128:], (8, CD)) for k in (1, 2)]
        coarse = jnp.concatenate(coarse, axis=0)
        v_o[at, :] = v_in[at, :] + step * p
        r_o[at, :] = r_in[at, :] - step * q
        d_o[at, :] = more * p - step * (q * rd[at, :] + coarse)
        return carry

    lax.fori_loop(0, RD // 16, body, 0, unroll=4)


def coarse_call(kernel, n_in, n_cr, name, out_shape, scratch, pos, moments, own, tables, rest, group=None):
    vmem = pl.BlockSpec(memory_space=VMEM)
    args = [moments, own, tables["grow"], tables["fall"], tables["blocks"], *tables["forward"], tables["spread"]]
    args += ([group] if group is not None else []) + list(rest)
    return pl.pallas_call(
        functools.partial(kernel, n_in, n_cr),
        in_specs=[pl.BlockSpec(memory_space=pltpu.SMEM)] + [vmem] * len(args),
        out_specs=[vmem] * len(out_shape), out_shape=out_shape, scratch_shapes=scratch,
        compiler_params=pltpu.CompilerParams(vmem_limit_bytes=22 * 1024 * 1024),
        cost_estimate=pl.CostEstimate(flops=10**8, bytes_accessed=10**7, transcendentals=0),
        name=name,
    )(pos, *args)


def neighbours(value_low, value_high, axis, count):
    ahead = [(i, i + 1) for i in range(count - 1)]
    behind = [(j, i) for i, j in ahead]
    return lax.ppermute(value_high, axis, ahead), lax.ppermute(value_low, axis, behind)


def per_device(n_in, n_cr, amplitudes, mask, depth, iterate):
    rows, put, mix, lanes = (jnp.asarray(t) for t in line_tables())
    tables = coarse_tables(n_in, n_cr)
    pos = jnp.stack([lax.axis_index("inline"), lax.axis_index("crosslin")]).astype(jnp.int32)
    col_first, col_last, local = pack_columns(amplitudes, iterate, mask, depth)
    left, right = neighbours(col_first, col_last, "crosslin", n_cr)
    cuts = ((1, 7), (8, 7))
    *inner, lines = inner_stage(*cuts[0], local, (iterate, mask, depth, rows))
    (left, right), lines = lax.optimization_barrier(((left, right), lines))
    row_first, row_last = pack_rows(lines, left, right, mix, lanes)
    up, down = neighbours(row_first, row_last, "inline", n_in)
    inner += inner_stage(*cuts[1], amplitudes)
    group = jnp.asarray(tables["group"])
    ta, tb, tc, z, r, rd, blocks, sums = tensor_stage(
        n_in, n_cr, cuts, pos, amplitudes, iterate, mask, depth, up, down, left, right, put, group, inner
    )

    def moments_of(payload, extra):
        gathered = lax.all_to_all(payload, "crosslin", 0, 0, tiled=True)
        pay, own = moments_stage(n_in, n_cr, extra, gathered, *tables["forward"], tables["steps"])
        return lax.all_to_all(pay, "inline", 0, 0, tiled=True), own

    flat = jax.ShapeDtypeStruct((RD, CD), F32)
    cs = VMEM((40, EC), F32)
    moments, own = moments_of(blocks, False)
    p, q, payload = coarse_call(
        image_kernel, n_in, n_cr, "image_stage",
        [flat, flat, jax.ShapeDtypeStruct((n_cr, CR + 8, CC), F32)],
        [VMEM((CR, CD), F32), cs],
        pos, moments, own, tables, [ta, tb, tc, z, rd, mask, blocks, sums], group,
    )
    moments, own = moments_of(payload, True)
    return tuple(
        coarse_call(
            final_kernel, n_in, n_cr, "final_stage", [flat, flat, flat], [cs],
            pos, moments, own, tables, [p, q, r, rd, iterate],
        )
    )


def solution(mesh):
    n_in, n_cr = mesh.shape["inline"], mesh.shape["crosslin"]
    flat = P("inline", "crosslin")
    return jax.shard_map(
        functools.partial(per_device, n_in, n_cr), mesh=mesh,
        in_specs=(P(None, "inline", "crosslin"), flat, flat, flat),
        out_specs=(flat, flat, flat), check_vma=False,
    )
```
